32 devices in a mesh: fsdp: 4 (over y, core), dp: 8 (over z, x).
Axes of the slice: x: 2, y: 2, z: 4, core: 2. Of those that a mesh axis runs over, the one named last changes fastest.
Arguments:
- inputs: bfloat16 [64, 128, 1024], P(('fsdp', 'dp')), may hold values from -12 to 12
- memory: bfloat16 [64, 2048, 1024], P(('fsdp', 'dp')), may hold values from -12 to 12
- lengths: int32 [64], P(('fsdp', 'dp')), may hold values from 64 to 128, as said below
- cotangent: bfloat16 [64, 128, 1024], P(('fsdp', 'dp')), may hold values from -6 to 6
- causal_query: bfloat16 [1024, 1024], P(('fsdp', 'dp')), may hold values from -0.046875 to 0.046875
- causal_key: bfloat16 [1024, 512], P(('fsdp', 'dp')), may hold values from -0.1875 to 0.1875
- causal_value: bfloat16 [1024, 512], P(('fsdp', 'dp')), may hold values from -0.1875 to 0.1875
- causal_out: bfloat16 [1024, 1024], P(('fsdp', 'dp')), may hold values from -0.75 to 0.75
- cross_query: bfloat16 [1024, 1024], P(('fsdp', 'dp')), may hold values from -0.046875 to 0.046875
- cross_key: bfloat16 [1024, 512], P(('fsdp', 'dp')), may hold values from -0.1875 to 0.1875
- cross_value: bfloat16 [1024, 512], P(('fsdp', 'dp')), may hold values from -0.1875 to 0.1875
- cross_out: bfloat16 [1024, 1024], P(('fsdp', 'dp')), may hold values from -1.5 to 1.5
- feed_gate: bfloat16 [1024, 2816], P(('fsdp', 'dp')), may hold values from -0.1875 to 0.1875
- feed_up: bfloat16 [1024, 2816], P(('fsdp', 'dp')), may hold values from -0.1875 to 0.1875
- feed_down: bfloat16 [2816, 1024], P(('fsdp', 'dp')), may hold values from -0.109375 to 0.109375
- gain_causal: bfloat16 [1024], P(('fsdp', 'dp')), may hold values from 0.099609375 to 1.8984375
- gain_cross: bfloat16 [1024], P(('fsdp', 'dp')), may hold values from 0.099609375 to 1.8984375
- gain_feed: bfloat16 [1024], P(('fsdp', 'dp')), may hold values from 0.099609375 to 1.8984375
- bias_table: bfloat16 [512], P(('fsdp', 'dp')), may hold values from -4 to 4
Outputs:
- layer_out: bfloat16 [64, 128, 1024], P(('fsdp', 'dp'))
- input_grad: bfloat16 [64, 128, 1024], P(('fsdp', 'dp'))
- memory_grad: bfloat16 [64, 2048, 1024], P(('fsdp', 'dp'))
- grad_causal_query: float32 [1024, 1024], P(('fsdp', 'dp'))
- grad_causal_key: float32 [1024, 512], P(('fsdp', 'dp'))
- grad_causal_value: float32 [1024, 512], P(('fsdp', 'dp'))
- grad_causal_out: float32 [1024, 1024], P(('fsdp', 'dp'))
- grad_cross_query: float32 [1024, 1024], P(('fsdp', 'dp'))
- grad_cross_key: float32 [1024, 512], P(('fsdp', 'dp'))
- grad_cross_value: float32 [1024, 512], P(('fsdp', 'dp'))
- grad_cross_out: float32 [1024, 1024], P(('fsdp', 'dp'))
- grad_feed_gate: float32 [1024, 2816], P(('fsdp', 'dp'))
- grad_feed_up: float32 [1024, 2816], P(('fsdp', 'dp'))
- grad_feed_down: float32 [2816, 1024], P(('fsdp', 'dp'))
- grad_gain_causal: float32 [1024], P(('fsdp', 'dp'))
- grad_gain_cross: float32 [1024], P(('fsdp', 'dp'))
- grad_gain_feed: float32 [1024], P(('fsdp', 'dp'))
- grad_bias_table: float32 [512], P(('fsdp', 'dp'))
The draws below stay inside these ranges and needn't reach their ends.
Inputs may be any that keep to these rules, and one draw needn't show every extreme that they name: lengths[b] is how many leading target tokens of summary b may serve as keys; some summary has 128 and some 128 // 2.
All inputs are finite; a program needn't handle non-finite values.
Results may differ from the reference program's by a relative error of at most 0.025.
The reference program's roundings to bfloat16 on the way count: a program that leaves them out, or rounds other values in their place, can miss the bound.
Values may be sent and summed in bfloat16 or wider, within the bound.
No kernel may reach another device: no remote copies, remote signals or barrier semaphores. Data moves between devices by JAX's collectives and lax.ppermute only.
A program may use at most 192 MiB of HBM per device.

```python
import jax
import jax.numpy as jnp
import numpy as np
from jax import lax

D = 1024
HEADS = 16
HD = 64
FF = 2816
BUCKETS = 32
KVH = 8
LT = 128
MEM = 2048
SEQS = 64


def draw_lengths(key, part):
    key_values, key_first, key_step = jax.random.split(key, 3)
    drawn = jax.random.randint(key_values, (SEQS,), LT // 2, LT + 1)
    first_pick = jax.random.randint(key_first, (), 0, SEQS)
    offset = jax.random.randint(key_step, (), 1, SEQS)
    second_pick = (first_pick + offset) % SEQS
    drawn = drawn.at[first_pick].set(LT).at[second_pick].set(LT // 2)
    return drawn.astype(jnp.int32)


def spiked(values, key, source, target, shards_of, factor):
    def block_of(dim):
        return (jnp.arange(values.shape[dim]) // (values.shape[dim] // shards_of)).reshape((-1,) + (1,) * (values.ndim - 1 - dim))

    one_side = jax.random.permutation(key, shards_of)[block_of(target)]
    other_side = (block_of(target) + shards_of // 2) % shards_of
    return jnp.where((block_of(source) == one_side) | (block_of(source) == other_side), factor * values, values)


def levels(stream_key, shape, pieces, smallest, high):
    def one(dim, shards_of):
        steps = jax.random.uniform(jax.random.fold_in(jax.random.fold_in(stream_key, 6), dim), (shards_of,), jnp.float32, smallest / len(pieces), high / len(pieces))
        return jnp.repeat(jnp.exp(steps), shape[dim] // shards_of).reshape((-1,) + (1,) * (len(shape) - dim - 1))

    loudness = one(*pieces[0])
    for cut in pieces[1:]:
        loudness = loudness * one(*cut)
    return loudness


def bell_draw(stream_key, dims, width, reach, cuts=(), kind=jnp.bfloat16):
    level = levels(stream_key, dims, cuts, -0.22, 0.18) if cuts else 1.0
    entries = jax.random.normal(stream_key, dims, jnp.float32) * width * level
    return jnp.minimum(jnp.maximum(entries, -reach), reach).astype(kind)


def bell_draw_with(stream_key, shape, scale, most, cuts, heavy, kind=jnp.bfloat16):
    values = scale * jax.random.normal(stream_key, shape, jnp.float32)
    if cuts:
        values = values * levels(stream_key, shape, cuts, -0.22, 0.18)
    return jnp.clip(spiked(values, jax.random.fold_in(stream_key, 3), *heavy), -most, most).astype(kind)


def setup_inputs(seed: int = 0) -> dict:
    seeds = jax.random.split(jax.random.key(seed), 20)
    inputs = bell_draw_with(seeds[0], (SEQS, LT, D), 1.0, 12.0, ((0, 32),), (0, 2, 32, 2.75))
    memory = bell_draw_with(seeds[1], (SEQS, MEM, D), 1.0, 12.0, ((0, 32),), (0, 2, 32, 2.75))
    lengths = draw_lengths(jax.random.fold_in(seeds[19], 71), 0)
    cotangent = bell_draw(seeds[3], (SEQS, LT, D), 1.0, 6.0, ((0, 32),))
    causal_query = bell_draw(seeds[4], (D, HEADS * HD), (16 * D) ** -0.5, 0.046875, ((0, 32),))
    causal_key = bell_draw(seeds[5], (D, KVH * HD), D ** -0.5, 0.1875, ((0, 32),))
    causal_value = bell_draw(seeds[6], (D, KVH * HD), D ** -0.5, 0.1875, ((0, 32),))
    causal_out = bell_draw(seeds[7], (HEADS * HD, D), (HEADS * HD // 16) ** -0.5, 0.75, ((0, 32),))
    cross_query = bell_draw(seeds[8], (D, HEADS * HD), (16 * D) ** -0.5, 0.046875, ((0, 32),))
    cross_key = bell_draw(seeds[9], (D, KVH * HD), D ** -0.5, 0.1875, ((0, 32),))
    cross_value = bell_draw(seeds[10], (D, KVH * HD), D ** -0.5, 0.1875, ((0, 32),))
    cross_out = bell_draw(seeds[11], (HEADS * HD, D), (HEADS * HD // 64) ** -0.5, 1.5, ((0, 32),))
    feed_gate = bell_draw(seeds[12], (D, FF), D ** -0.5, 0.1875, ((0, 32),))
    feed_up = bell_draw(seeds[13], (D, FF), D ** -0.5, 0.1875, ((0, 32),))
    feed_down = bell_draw(seeds[14], (FF, D), FF ** -0.5, 0.109375, ((0, 32),))
    gain_causal = jnp.clip(1.0 + 0.18 * jax.random.normal(seeds[15], (D,), jnp.float32), 0.099609375, 1.8984375).astype(jnp.bfloat16)
    gain_cross = jnp.clip(1.0 + 0.18 * jax.random.normal(seeds[16], (D,), jnp.float32), 0.099609375, 1.8984375).astype(jnp.bfloat16)
    gain_feed = jnp.clip(1.0 + 0.18 * jax.random.normal(seeds[17], (D,), jnp.float32), 0.099609375, 1.8984375).astype(jnp.bfloat16)
    bias_table = bell_draw(seeds[18], (HEADS * BUCKETS,), 1.0, 4.0, ((0, 32),))
    return {"inputs": inputs, "memory": memory, "lengths": lengths, "cotangent": cotangent, "causal_query": causal_query, "causal_key": causal_key, "causal_value": causal_value, "causal_out": causal_out, "cross_query": cross_query, "cross_key": cross_key, "cross_value": cross_value, "cross_out": cross_out, "feed_gate": feed_gate, "feed_up": feed_up, "feed_down": feed_down, "gain_causal": gain_causal, "gain_cross": gain_cross, "gain_feed": gain_feed, "bias_table": bias_table}


@jax.custom_vjp
def low(v):
    return lax.optimization_barrier(v.astype(jnp.bfloat16)).astype(jnp.float32)

@jax.custom_vjp
def low_back(v):
    return v

def low_keep(v):
    return (low(v), None)

def low_pass(kept, grad):
    return (grad,)

def back_keep(v):
    return (v, None)

def back_low(kept, grad):
    return (low(grad),)
low.defvjp(low_keep, low_pass)
low_back.defvjp(back_keep, back_low)
norm_eps = 1e-06
masked_score = -1000000000.0
bucket_reach = 128
highest = lax.Precision.HIGHEST

def bucket_onehot(length):
    query_pos = np.arange(length)[:, None]
    key_pos = np.arange(length)[None, :]
    distance = np.maximum(query_pos - key_pos, 0)
    exact_count = BUCKETS // 2
    spread = np.log(np.maximum(distance, 1) / exact_count) / np.log(bucket_reach / exact_count) * (BUCKETS - exact_count)
    far_bucket = np.minimum(exact_count + np.floor(spread).astype(np.int64), BUCKETS - 1)
    bucket_id = np.where(distance < exact_count, distance, far_bucket)
    return jnp.asarray(bucket_id[None] == np.arange(BUCKETS)[:, None, None]).astype(jnp.float32)

def normalize(stream, gain):
    scale = lax.rsqrt(lax.optimization_barrier(jnp.mean(stream * stream, axis=-1, keepdims=True)) + norm_eps)
    return low(stream * scale * gain)

def attend(normed, source, w_query, w_key, w_value, w_out, added, key_valid):
    group_ratio = HEADS // KVH
    seq_count, row_count, model_width = normed.shape
    key_count = source.shape[1]
    queries = low(low_back(jnp.einsum('bld,dk->blk', normed, w_query, precision=highest)))
    queries = queries.reshape(seq_count, row_count, KVH, group_ratio, HD)
    key_heads = low(low_back(jnp.einsum('bsd,dk->bsk', source, w_key, precision=highest))).reshape(seq_count, key_count, KVH, HD)
    value_heads = low(low_back(jnp.einsum('bsd,dk->bsk', source, w_value, precision=highest))).reshape(seq_count, key_count, KVH, HD)
    scores = jnp.einsum('blgre,bsge->bgrls', queries, key_heads, precision=highest)
    if added is not None:
        scores = scores + added[None]
    scores = low_back(scores)
    if key_valid is not None:
        scores = jnp.where(key_valid[:, None, None], scores, masked_score)
    softmax_out = low(jax.nn.softmax(scores, axis=-1))
    mixed_all = jnp.einsum('bgrls,bsge->blgre', softmax_out, value_heads, precision=highest)
    mixed_all = low(low_back(mixed_all.reshape(seq_count, row_count, HEADS * HD)))
    return low_back(jnp.einsum('blk,kd->bld', mixed_all, w_out, precision=highest))

def decoder_layer(params, stream, source, lengths):
    causal_query, causal_key, causal_value, causal_out, cross_query, cross_key, cross_value, cross_out, feed_gate, feed_up, feed_down, gain_causal, gain_cross, gain_feed, bias_table = params
    seq_count, length, model_width = stream.shape
    onehot = bucket_onehot(length)
    bias_full = jnp.einsum('hc,cij->hij', bias_table.reshape(HEADS, BUCKETS), onehot, precision=highest)
    added = bias_full.reshape(KVH, HEADS // KVH, length, length)
    positions = jnp.arange(length, dtype=jnp.int32)
    key_valid = (positions[None, None, :] <= positions[None, :, None]) & (positions[None, None, :] < lengths[:, None, None])
    normed = normalize(stream, gain_causal)
    after_causal = stream + attend(normed, normed, causal_query, causal_key, causal_value, causal_out, added, key_valid)
    normed = normalize(after_causal, gain_cross)
    after_cross = after_causal + attend(normed, source, cross_query, cross_key, cross_value, cross_out, None, None)
    normed = normalize(after_cross, gain_feed)
    gate_pre = low_back(jnp.einsum('bld,df->blf', normed, feed_gate, precision=highest))
    up_pre = low_back(jnp.einsum('bld,df->blf', normed, feed_up, precision=highest))
    hidden = low(jax.nn.gelu(gate_pre, approximate=True) * up_pre)
    return after_cross + low_back(jnp.einsum('blf,fd->bld', hidden, feed_down, precision=highest))

def reference(inputs, memory, lengths, cotangent, causal_query, causal_key, causal_value, causal_out, cross_query, cross_key, cross_value, cross_out, feed_gate, feed_up, feed_down, gain_causal, gain_cross, gain_feed, bias_table):
    params = tuple((weight.astype(jnp.float32) for weight in (causal_query, causal_key, causal_value, causal_out, cross_query, cross_key, cross_value, cross_out, feed_gate, feed_up, feed_down, gain_causal, gain_cross, gain_feed, bias_table)))
    in_group = 2
    step_count = SEQS // in_group
    stream_groups = inputs.astype(jnp.float32).reshape(step_count, in_group, LT, D)
    source_groups = memory.astype(jnp.float32).reshape(step_count, in_group, MEM, D)
    span_groups = lengths.reshape(step_count, in_group)

    def run_layers(weights, stream_all, source_all):

        def one_group(block_items):
            return decoder_layer(weights, block_items[0], block_items[1], block_items[2])
        return lax.map(jax.checkpoint(one_group), (stream_all, source_all, span_groups))
    result, pullback = jax.vjp(run_layers, params, stream_groups, source_groups)
    gradients, stream_grad, source_grad = pullback(cotangent.astype(jnp.float32).reshape(step_count, in_group, LT, D))
    grad_causal_query, grad_causal_key, grad_causal_value, grad_causal_out, grad_cross_query, grad_cross_key, grad_cross_value, grad_cross_out, grad_feed_gate, grad_feed_up, grad_feed_down, grad_gain_causal, grad_gain_cross, grad_gain_feed, grad_bias_table = gradients
    return (result.reshape(SEQS, LT, D).astype(jnp.bfloat16), stream_grad.reshape(SEQS, LT, D).astype(jnp.bfloat16), source_grad.reshape(SEQS, MEM, D).astype(jnp.bfloat16), grad_causal_query, grad_causal_key, grad_causal_value, grad_causal_out, grad_cross_query, grad_cross_key, grad_cross_value, grad_cross_out, grad_feed_gate, grad_feed_up, grad_feed_down, grad_gain_causal, grad_gain_cross, grad_gain_feed, grad_bias_table)
```

```python
import functools

import jax
import jax.numpy as jnp
import numpy as np
from jax import lax
from jax.experimental import pallas as pl
from jax.experimental.pallas import tpu as pltpu
from jax.sharding import PartitionSpec as P

HEADS = 16
HD = 64
BUCKETS = 32
KVH = 8
PAIR = 2 * HD
AXES = ("fsdp", "dp")
norm_eps = 1e-06
masked_score = -1000000000.0
bucket_reach = 128
f32 = jnp.float32
bf16 = jnp.bfloat16
VMEM_LIMIT = 56 * 1024 * 1024


def reversed_buckets():
    distance = (-np.arange(bucket_reach)) % bucket_reach
    exact_count = BUCKETS // 2
    spread = (
        np.log(np.maximum(distance, 1) / exact_count)
        / np.log(bucket_reach / exact_count)
        * (BUCKETS - exact_count)
    )
    far_bucket = np.minimum(exact_count + np.floor(spread).astype(np.int64), BUCKETS - 1)
    bucket_id = np.where(distance < exact_count, distance, far_bucket)
    return (bucket_id[None] == np.arange(BUCKETS)[:, None]).astype(np.float32)


def dot(a, b, ca=1, cb=0):
    return lax.dot_general(a, b, (((ca,), (cb,)), ((), ())), preferred_element_type=f32)


def call(kernel, ins, in_specs, out_shape, out_specs, name, after=(), grid=(1,), scratch=(), prefetch=None):
    lead = 0 if prefetch is None else 1
    n = lead + len(ins)

    def body(*refs):
        kernel(*refs[:n], *refs[n + len(after) :])

    spec = pltpu.PrefetchScalarGridSpec(
        num_scalar_prefetch=lead,
        grid=grid,
        in_specs=list(in_specs) + [pl.BlockSpec(memory_space=pl.ANY)] * len(after),
        out_specs=out_specs,
        scratch_shapes=list(scratch),
    )
    front = () if prefetch is None else (prefetch,)
    return pl.pallas_call(
        body,
        grid_spec=spec,
        out_shape=out_shape,
        compiler_params=pltpu.CompilerParams(vmem_limit_bytes=VMEM_LIMIT),
        cost_estimate=pl.CostEstimate(flops=1000, bytes_accessed=1000, transcendentals=0),
        name=name,
    )(*front, *ins, *after)


def whole(shape):
    return pl.BlockSpec(shape, lambda *_: (0,) * len(shape))


def struct(shape, dtype):
    return jax.ShapeDtypeStruct(shape, dtype)


def smem():
    return pl.BlockSpec(memory_space=pltpu.SMEM)


class Links:
    names = ("hi", "core", "ring", "lo")

    def __init__(self, mesh):
        nf, nd = mesh.shape["fsdp"], mesh.shape["dp"]
        self.nf, self.nd, self.size = nf, nd, nd // 2
        size = self.size
        self.lengths = {"hi": nf // 2, "core": 2, "ring": size, "lo": 2}
        spots = [(f, d) for f in range(nf) for d in range(nd)]

        def pairs(move):
            out = []
            for f, d in spots:
                g, e = move(f, d)
                out.append((f * nd + d, g * nd + e))
            return out

        self.pairs = {
            "core": pairs(lambda f, d: (f ^ 1, d)),
            "hi": pairs(lambda f, d: (f ^ 2, d)),
            "both": pairs(lambda f, d: (f ^ 3, d)),
            "lo": pairs(lambda f, d: (f, d ^ 1)),
        }
        for s in range(1, size):
            self.pairs[s] = pairs(lambda f, d: (f, ((d // 2 + s) % size) * 2 + d % 2))

    def locate(self):
        f, d = lax.axis_index("fsdp"), lax.axis_index("dp")
        self.hi, self.core, self.ring, self.lo = f // 2, f % 2, d // 2, d % 2
        self.spot = jnp.stack([self.hi, self.core, self.ring, self.lo]).astype(jnp.int32)

    def send(self, a, way):
        return lax.ppermute(a, AXES, self.pairs[way])

    def spread_ring(self, shard, after=()):
        return [shard] + [self.send(tie(shard, *after), s) for s in range(1, self.size)]

    def quarters(self, wide):
        mine = self.hi * 2 + self.core
        out = [lax.dynamic_index_in_dim(wide, mine, 0, keepdims=False)]
        for flip, way in ((1, "core"), (2, "hi"), (3, "both")):
            theirs = lax.dynamic_index_in_dim(wide, mine ^ flip, 0, keepdims=False)
            out.append(self.send(theirs, way))
        return jnp.stack(out)

    def unquarter(self, near):
        mine = self.hi * 2 + self.core
        return jnp.stack(
            [lax.dynamic_index_in_dim(near, mine ^ f, 0, keepdims=False) for f in range(self.nf)]
        )

    def grow(self, stack, order, first=(), second=(), third=()):
        one, two = order
        got = self.send(tie(stack, *first), one)
        pair = jnp.stack([stack, got])
        far = self.send(tie(pair, *second), two)
        near_far = [{}, {one: 1}]
        entries = [(pair, near_far), (far, [{**f, two: 1} for f in near_far])]
        for array, fars in list(entries):
            entries.append(
                (self.send(tie(array, *third), "core"), [{**f, "core": 1} for f in fars])
            )
        return Blocks(self, entries)


class Blocks:
    def __init__(self, links, entries, quads=False):
        self.links = links
        self.arrays = [a for a, _ in entries]
        self.fars = [f for _, f in entries]
        self.quads = quads
        _, _, self.r, self.c = self.arrays[0].shape
        self.count = len(entries)

    def specs(self, width=None, index=0):
        return [
            pl.BlockSpec((*a.shape[:3], width or self.c), lambda *_: (0, 0, 0, index))
            for a in self.arrays
        ]

    def put(self, spot, refs, *outs):
        size = self.links.size
        quads = [(0, 0), (0, 1), (1, 0), (1, 1)] if self.quads else [None]
        r = self.r // len(quads)
        for ref, fars in zip(refs, self.fars):
            for i, far in enumerate(fars):
                at_lo = 1 - spot[3] if far.get("lo") else spot[3]
                for t in range(size):
                    at_ring = lax.rem(spot[2] + (size - t), size)
                    for q, quad in enumerate(quads):
                        far_hi, far_core = quad or (far.get("hi"), far.get("core"))
                        at_hi = 1 - spot[0] if far_hi else spot[0]
                        at_core = 1 - spot[1] if far_core else spot[1]
                        row = (((at_hi * 2 + at_core) * size + at_ring) * 2 + at_lo) * r
                        rows = pl.ds(pl.multiple_of(row, r), r)
                        left = 0
                        for out in outs:
                            width = out.shape[-1]
                            out[rows, :] = ref[i, t, q * r : (q + 1) * r, left : left + width]
                            left += width


def tie(x, *after):
    return lax.optimization_barrier((x, *after))[0] if after else x


def assemble(links, near, far, after=()):
    size = links.size
    _, r, c = near.shape

    def kernel(spot, near_ref, far_ref, out, held, sems_in, sems_out):
        copies = []
        for k, ref in enumerate((near_ref, far_ref)):
            at_lo = 1 - spot[3] if k else spot[3]
            for t in range(size):
                at_ring = lax.rem(spot[2] + (size - t), size)
                copies.append(
                    (
                        pltpu.make_async_copy(ref.at[t], held.at[k, t], sems_in.at[k, t]),
                        pltpu.make_async_copy(held.at[k, t], out.at[at_ring, at_lo], sems_out.at[k, t]),
                    )
                )
        for one, _ in copies:
            one.start()
        for one, two in copies:
            one.wait()
            two.start()
        for _, two in copies:
            two.wait()

    out = call(
        kernel,
        [links.spot, near, far],
        [smem()] + [pl.BlockSpec(memory_space=pl.ANY)] * 2,
        struct((size, 2, r, c), bf16),
        pl.BlockSpec(memory_space=pl.ANY),
        "assemble",
        after=after,
        scratch=[
            pltpu.VMEM((2, size, r, c), bf16),
            pltpu.SemaphoreType.DMA((2, size)),
            pltpu.SemaphoreType.DMA((2, size)),
        ],
    )
    return out.reshape(-1, c)


class Leaf:
    def __init__(self, array, axes, held=(), width=None, index=0):
        self.array, self.axes, self.held = array, axes, dict(held)
        self.width = width or array.shape[-1]
        self.index = index

    def hold(self, way, far):
        held = dict(self.held)
        if way in self.axes:
            held[way] = far
        return Leaf(self.array, self.axes, held, self.width, self.index)

    def free(self):
        return [a for a in self.axes if a not in self.held]

    def spec(self, ring_steps):
        shape, pick = [], []
        for i, a in enumerate(self.axes):
            if a in self.held:
                shape.append(None)
                pick.append(("far" if self.held[a] else "here", Links.names.index(a)))
            elif a == "ring" and ring_steps:
                shape.append(1)
                pick.append(("step", 0))
            else:
                shape.append(self.array.shape[i])
                pick.append(("zero", 0))

        def index(t, spot):
            out = []
            for kind, i in pick:
                if kind == "far":
                    out.append(1 - spot[i])
                elif kind == "here":
                    out.append(spot[i])
                else:
                    out.append(t if kind == "step" else 0)
            return (*out, 0, self.index)

        return pl.BlockSpec((*shape, self.array.shape[-2], self.width), index)


class Scatter:
    def __init__(self, links, jobs):
        self.links = links
        self.jobs = [([*leaves], list(order)) for leaves, order in jobs]
        self.last = None

    def step(self, after=()):
        links = self.links
        size = links.size
        ways = [order.pop(0) for _, order in self.jobs]
        ins, specs, outs, out_specs, plan = [], [], [], [], []
        for (leaves, _), way in zip(self.jobs, ways):
            moving = [leaf.hold(way, True) for leaf in leaves]
            free = moving[0].free()
            ins += [leaf.array for leaf in moving]
            specs += [leaf.spec(True) for leaf in moving]
            shape = tuple(links.lengths[a] for a in free) + (moving[0].array.shape[-2], moving[0].width)
            outs.append(struct(shape, bf16))
            block = tuple(1 if a == "ring" else links.lengths[a] for a in free) + shape[-2:]
            at = free.index("ring")
            out_specs.append(
                pl.BlockSpec(
                    block,
                    functools.partial(
                        lambda at, rank, t, spot: tuple(t if i == at else 0 for i in range(rank)),
                        at,
                        len(block),
                    ),
                )
            )
            plan.append((len(moving), free))

        def kernel(spot, *refs):
            n = 0
            for (count, _), out in zip(plan, refs[len(ins) :]):
                total = refs[n][...].astype(f32)
                for ref in refs[n + 1 : n + count]:
                    total = total + ref[...].astype(f32)
                out[...] = total.astype(bf16)
                n += count

        sent = call(
            kernel, ins, specs, outs, out_specs, "combine", after=after, grid=(size,), prefetch=links.spot
        )
        jobs = []
        for (leaves, order), way, away, (_, free) in zip(self.jobs, ways, sent, plan):
            kept = [leaf.hold(way, False) for leaf in leaves]
            jobs.append((kept + [Leaf(links.send(away, way), free)], order))
        self.jobs = jobs
        return sent[:1]

    def spread(self, after=()):
        links = self.links
        size = links.size
        ins, specs, groups, where = [], [], {}, []
        for leaves, _ in self.jobs:
            ins += [leaf.array for leaf in leaves]
            specs += [leaf.spec(False) for leaf in leaves]
            free = [a for a in leaves[0].free() if a != "ring"]
            key = tuple(links.lengths[a] for a in free) + (leaves[0].array.shape[-2],)
            left = groups.get(key, 0)
            groups[key] = left + leaves[0].width
            where.append((key, left, leaves[0].width, len(leaves), leaves[0].free().index("ring")))
        keys = list(groups)
        outs = []
        for key in keys:
            shape = key + (groups[key],)
            outs += [struct(shape, f32)] + [struct(shape, bf16)] * (size - 1)

        def kernel(spot, *refs):
            n, m = 0, len(ins)
            for key, left, width, count, at in where:
                base = m + keys.index(key) * size
                for s in range(size):
                    ring = lax.rem(spot[2] + s, size)
                    total = None
                    for ref in refs[n : n + count]:
                        term = (ref[ring] if at == 0 else ref[:, :, ring]).astype(f32)
                        total = term if total is None else total + term
                    out = refs[base + s]
                    out[..., left : left + width] = total.astype(out.dtype)
                n += count

        sent = call(
            kernel, ins, specs, outs, [whole(o.shape) for o in outs], "spread", after=after, prefetch=links.spot
        )
        totals = {}
        for i, key in enumerate(keys):
            group = sent[i * size : (i + 1) * size]
            total = group[0]
            for s in range(1, size):
                total = total + links.send(group[s], s).astype(f32)
            totals[key] = total
        self.results = [totals[key][..., left : left + width] for key, left, width, _, _ in where]
        return sent[:1]


def norm_scale(rows):
    return lax.rsqrt(jnp.mean(rows * rows, axis=-1, keepdims=True) + norm_eps)


def norm_back(grad_normed, rows, gain):
    scale = norm_scale(rows)
    scaled = grad_normed * gain
    inner_mean = jnp.mean(scaled * rows, axis=-1, keepdims=True)
    grad_rows = scale * scaled - rows * (scale * scale * scale) * inner_mean
    return grad_rows, jnp.sum(grad_normed * rows * scale, axis=0, keepdims=True)


def swap_halves(block):
    return pltpu.roll(block.astype(f32), HD, 1).astype(bf16)


def low_lanes(shape):
    return lax.broadcasted_iota(jnp.int32, shape, 1) < HD


def heads_low(block):
    keep = low_lanes(block.shape)
    zero = jnp.zeros_like(block)
    return jnp.concatenate(
        [jnp.where(keep, block, zero), jnp.where(keep, swap_halves(block), zero)], axis=0
    )


def heads_high(block):
    keep = low_lanes(block.shape)
    zero = jnp.zeros_like(block)
    return jnp.concatenate(
        [jnp.where(keep, zero, swap_halves(block)), jnp.where(keep, zero, block)], axis=0
    )


def merge_low(both):
    half = both.shape[0] // 2
    even, odd = both[:half], both[half:]
    return jnp.where(low_lanes(even.shape), even, pltpu.roll(odd, HD, 1))


def merge_high(both):
    half = both.shape[0] // 2
    even, odd = both[:half], both[half:]
    return jnp.where(low_lanes(even.shape), pltpu.roll(even, HD, 1), odd)


def toeplitz(row, length):
    return pltpu.roll(jnp.broadcast_to(row, (length, length)), 0, 1, stride=1, stride_axis=0)


def diagonal_sums(flipped):
    turned = pltpu.roll(flipped, 1, 1, stride=1, stride_axis=0)
    return jnp.sum(turned, axis=0, keepdims=True)


def causal_probs(low, keyval, table, g, length, valid_len):
    s = dot(low, keyval, 1, 1)
    bias = jnp.concatenate(
        [toeplitz(table[2 * g : 2 * g + 1], length), toeplitz(table[2 * g + 1 : 2 * g + 2], length)],
        axis=0,
    )
    i = lax.broadcasted_iota(jnp.int32, (length, length), 0)
    j = lax.broadcasted_iota(jnp.int32, (length, length), 1)
    valid = (j <= i) & (j < valid_len)
    valid = jnp.concatenate([valid, valid], axis=0)
    s = jnp.where(valid, s + bias, masked_score)
    e = jnp.exp(s - jnp.max(s, axis=-1, keepdims=True))
    return e / jnp.sum(e, axis=-1, keepdims=True)


def split_rows(lhs_t, rhs, core, keep, away):
    half = keep.shape[1]
    for hi in range(keep.shape[0]):
        for out, at in ((keep, core), (away, 1 - core)):
            row = pl.multiple_of((hi * 2 + at) * half, half)
            out[hi] = dot(lhs_t[pl.ds(row, half), :], rhs).astype(bf16)


def project_memory(links, memory, blocks):
    seqs, count, width = memory.shape
    cols = KVH * PAIR
    tile = 512
    n = blocks.count

    def kernel(spot, mem_ref, *refs):
        held = refs[:n]
        out_ref, small_ref, w_ref, wt_ref = refs[n:]

        @pl.when((pl.program_id(0) == 0) & (pl.program_id(1) == 0))
        def _():
            blocks.put(spot, held, w_ref)
            wt_ref[...] = w_ref[:, :cols].T
            small_ref[...] = w_ref[:, cols:].astype(f32).T[:8]

        out_ref[0] = dot(wt_ref[...], mem_ref[0], 1, 1).astype(bf16)

    return call(
        kernel,
        [links.spot, memory] + blocks.arrays,
        [smem(), pl.BlockSpec((1, tile, width), lambda b, t: (b, t, 0))] + blocks.specs(),
        (struct((seqs, cols, count), bf16), struct((8, width), f32)),
        [pl.BlockSpec((1, cols, tile), lambda b, t: (b, 0, t)), whole((8, width))],
        "project_memory",
        grid=(seqs, count // tile),
        scratch=[pltpu.VMEM((width, blocks.c), bf16), pltpu.VMEM((cols, width), bf16)],
    )


def causal_forward(links, x, blocks, gain, table, lengths, after):
    seqs, length, width = x.shape
    rows = seqs * length
    cols = 2 * width
    n = blocks.count

    def kernel(spot, len_ref, x_ref, gain_ref, tab_ref, *refs):
        x1_ref, n1_ref, qkv_ref, o1_ref, w_ref, wo_ref = refs[n:]
        blocks.put(spot, refs[:n], w_ref, wo_ref)
        xf = x_ref[...].astype(f32)
        n1 = (xf * norm_scale(xf) * gain_ref[...]).astype(bf16)
        n1_ref[...] = n1
        qkv_ref[...] = dot(n1, w_ref[...]).astype(bf16)
        tab = tab_ref[...]
        for g in range(KVH):
            lanes = slice(g * PAIR, (g + 1) * PAIR)
            kv_lanes = slice(width + g * PAIR, width + (g + 1) * PAIR)
            for b in range(seqs):
                part = slice(b * length, (b + 1) * length)
                keyval = qkv_ref[part, kv_lanes]
                p = causal_probs(
                    heads_low(qkv_ref[part, lanes]), keyval, tab, g, length, len_ref[b]
                )
                o1_ref[part, lanes] = merge_high(dot(p.astype(bf16), keyval)).astype(bf16)
        x1_ref[...] = xf + dot(o1_ref[...], wo_ref[...])

    return call(
        kernel,
        [links.spot, lengths, x.reshape(rows, width), gain, table] + blocks.arrays,
        [smem(), smem(), whole((rows, width)), whole((1, width)), whole(table.shape)]
        + blocks.specs(),
        (
            struct((rows, width), f32),
            struct((rows, width), bf16),
            struct((rows, cols), bf16),
            struct((rows, width), bf16),
        ),
        [whole((rows, width)), whole((rows, width)), whole((rows, cols)), whole((rows, width))],
        "causal_forward",
        after=after,
        scratch=[pltpu.VMEM((width, cols), bf16), pltpu.VMEM((width, width), bf16)],
    )


def cross_forward(links, x1, keyval, blocks, gain_cross, gain_feed):
    rows, width = x1.shape
    seqs, _, count = keyval.shape
    length = rows // seqs
    n = blocks.count

    def kernel(spot, x1_ref, kv_ref, g2_ref, g3_ref, *refs):
        n2_ref, q2_ref, o2_ref, x2_ref, n3_ref, p_ref, wq_ref, wo_ref = refs[n:]
        b, g = pl.program_id(0), pl.program_id(1)

        @pl.when((b == 0) & (g == 0))
        def _():
            blocks.put(spot, refs[:n], wq_ref, wo_ref)
            x1v = x1_ref[...]
            n2 = (x1v * norm_scale(x1v) * g2_ref[...]).astype(bf16)
            n2_ref[...] = n2
            q2_ref[...] = dot(n2, wq_ref[...]).astype(bf16)

        part = pl.ds(pl.multiple_of(b * length, length), length)
        lanes = pl.ds(pl.multiple_of(g * PAIR, PAIR), PAIR)
        kv = kv_ref[0]
        s = dot(heads_low(q2_ref[part, lanes]), kv)
        e = jnp.exp(s - jnp.max(s, axis=-1, keepdims=True))
        p = (e * (1.0 / jnp.sum(e, axis=-1, keepdims=True))).astype(bf16)
        p_ref[0] = p
        o2_ref[part, lanes] = merge_high(dot(p, kv, 1, 1)).astype(bf16)

        @pl.when((b == seqs - 1) & (g == KVH - 1))
        def _():
            x2 = x1_ref[...] + dot(o2_ref[...], wo_ref[...])
            x2_ref[...] = x2
            n3_ref[...] = (x2 * norm_scale(x2) * g3_ref[...]).astype(bf16)

    return call(
        kernel,
        [links.spot, x1, keyval, gain_cross, gain_feed] + blocks.arrays,
        [
            smem(),
            whole((rows, width)),
            pl.BlockSpec((1, PAIR, count), lambda b, g: (b, g, 0)),
            whole((1, width)),
            whole((1, width)),
        ]
        + blocks.specs(),
        (
            struct((rows, width), bf16),
            struct((rows, width), bf16),
            struct((rows, width), bf16),
            struct((rows, width), f32),
            struct((rows, width), bf16),
            struct((seqs * KVH, 2 * length, count), bf16),
        ),
        [whole((rows, width))] * 5
        + [pl.BlockSpec((1, 2 * length, count), lambda b, g: (b * KVH + g, 0, 0))],
        "cross_forward",
        grid=(seqs, KVH),
        scratch=[pltpu.VMEM((width, width), bf16)] * 2,
    )


def stack_rows(refs, out):
    rows = refs[0].shape[0]
    for i, ref in enumerate(refs):
        out[i * rows : (i + 1) * rows] = ref[...]


def feed_through(links, n3s, cots, blocks, w_down, after):
    rows, width = n3s[0].shape
    units = w_down.shape[0]
    n = blocks.count
    c0 = np.float32(np.sqrt(2.0 / np.pi))
    c1 = np.float32(0.044715)
    cuts = [slice(i, min(i + 256, units)) for i in range(0, units, 256)]

    def kernel(spot, *refs):
        wd_ref = refs[8]
        held = refs[9 : 9 + n]
        hid_ref, dgate_ref, dup_ref, dn_ref, dn_hi_ref, dn_away_ref = refs[9 + n : 15 + n]
        wg_ref, wu_ref, n3_all, cot_all = refs[15 + n :]
        blocks.put(spot, held, wg_ref, wu_ref)
        stack_rows(refs[:4], n3_all)
        stack_rows(refs[4:8], cot_all)
        for cut in cuts:
            gate = dot(n3_all[...], wg_ref[:, cut])
            up = dot(n3_all[...], wu_ref[:, cut])
            dh = dot(cot_all[...], wd_ref[cut, :], 1, 1)
            square = gate * gate
            t = jnp.tanh(c0 * (gate + c1 * (square * gate)))
            cdf = 0.5 * (1.0 + t)
            value = gate * cdf
            slope = cdf + 0.5 * gate * (1.0 - t * t) * (c0 * (1.0 + 3.0 * c1 * square))
            hid_ref[:, cut] = (value * up).astype(bf16)
            dgate_ref[:, cut] = (dh * up * slope).astype(bf16)
            dup_ref[:, cut] = (dh * value).astype(bf16)
        for i in range(0, width, 256):
            at = slice(i, i + 256)
            dn = dot(dgate_ref[...], wg_ref[at, :], 1, 1) + dot(dup_ref[...], wu_ref[at, :], 1, 1)
            dn_ref[:, at] = dn[:rows]
            dn_away_ref[:rows, at] = dn[rows : 2 * rows].astype(bf16)
            dn_hi_ref[:, at] = dn[2 * rows : 3 * rows]
            dn_away_ref[rows:, at] = dn[3 * rows :].astype(bf16)

    return call(
        kernel,
        [links.spot, *n3s, *cots, w_down] + blocks.arrays,
        [smem()] + [whole((rows, width))] * 8 + [whole(w_down.shape)] + blocks.specs(),
        (
            struct((4 * rows, units), bf16),
            struct((4 * rows, units), bf16),
            struct((4 * rows, units), bf16),
            struct((rows, width), f32),
            struct((rows, width), f32),
            struct((2 * rows, width), bf16),
        ),
        [whole((4 * rows, units))] * 3 + [whole((rows, width))] * 2 + [whole((2 * rows, width))],
        "feed_through",
        after=after,
        scratch=[
            pltpu.VMEM((width, units), bf16),
            pltpu.VMEM((width, units), bf16),
            pltpu.VMEM((4 * rows, width), bf16),
            pltpu.VMEM((4 * rows, width), bf16),
        ],
    )


def feed_weight_grads(n3s, cots, hidden, dgate, dup, w_down, after):
    rows, width = n3s[0].shape
    units = hidden.shape[1]

    def kernel(*refs):
        hid_ref, dgate_ref, dup_ref, wd_ref = refs[8:12]
        y_ref, y_hi_ref, y_away_ref, gu_ref, gd_ref, n3t_ref, cot_all, hid_t = refs[12:]
        for i in range(4):
            n3t_ref[:, i * rows : (i + 1) * rows] = refs[i][...].T
        stack_rows(refs[4:8], cot_all)
        hid_t[...] = hid_ref[...].T
        for i in range(0, width, 256):
            gu_ref[i : i + 256, :units] = dot(n3t_ref[i : i + 256], dgate_ref[...]).astype(bf16)
            gu_ref[i : i + 256, units:] = dot(n3t_ref[i : i + 256], dup_ref[...]).astype(bf16)
        for i in range(0, units, 352):
            gd_ref[i : i + 352] = dot(hid_t[i : i + 352], cot_all[...]).astype(bf16)
        for i in range(0, width, 256):
            at = slice(i, i + 256)
            y = dot(hid_ref[...], wd_ref[:, at])
            y_ref[:, at] = y[:rows]
            y_away_ref[:rows, at] = y[rows : 2 * rows].astype(bf16)
            y_hi_ref[:, at] = y[2 * rows : 3 * rows]
            y_away_ref[rows:, at] = y[3 * rows :].astype(bf16)

    return call(
        kernel,
        [*n3s, *cots, hidden, dgate, dup, w_down],
        [whole((rows, width))] * 8 + [whole((4 * rows, units))] * 3 + [whole(w_down.shape)],
        (
            struct((rows, width), f32),
            struct((rows, width), f32),
            struct((2 * rows, width), bf16),
            struct((width, 2 * units), bf16),
            struct((units, width), bf16),
        ),
        [whole((rows, width))] * 2
        + [whole((2 * rows, width)), whole((width, 2 * units)), whole((units, width))],
        "feed_weight_grads",
        after=after,
        scratch=[
            pltpu.VMEM((width, 4 * rows), bf16),
            pltpu.VMEM((4 * rows, width), bf16),
            pltpu.VMEM((units, 4 * rows), bf16),
        ],
    )


def cross_enter(links, x2, gain_feed, dn3, dn3_core, dn3_hi, cotangent, o2, out_blocks, after):
    rows, width = x2.shape
    n = out_blocks.count
    split = (2, width // 4, width)

    def kernel(spot, x2_ref, g_ref, dn_ref, dn_core_ref, dn_hi_ref, cot_ref, o2_ref, *refs):
        dx_ref, do_ref, keep_ref, away_ref, gg_ref, w_ref, o2t_ref = refs[n:]
        out_blocks.put(spot, refs[:n], w_ref)
        dn = dn_ref[...] + dn_core_ref[...].astype(f32) + dn_hi_ref[...].astype(f32)
        grad_rows, grad_gain = norm_back(dn, x2_ref[...], g_ref[...])
        gg_ref[...] = grad_gain
        dx2 = cot_ref[...].astype(f32) + grad_rows
        dx_ref[...] = dx2
        da = dx2.astype(bf16)
        do_ref[...] = dot(da, w_ref[...], 1, 1).astype(bf16)
        o2t_ref[...] = o2_ref[...].T
        split_rows(o2t_ref, da, spot[1], keep_ref, away_ref)

    return call(
        kernel,
        [links.spot, x2, gain_feed, dn3, dn3_core, dn3_hi, cotangent, o2] + out_blocks.arrays,
        [smem(), whole((rows, width)), whole((1, width))]
        + [whole((rows, width))] * 5
        + out_blocks.specs(width, 1),
        (
            struct((rows, width), f32),
            struct((rows, width), bf16),
            struct(split, bf16),
            struct(split, bf16),
            struct((1, width), f32),
        ),
        [whole((rows, width))] * 2 + [whole(split)] * 2 + [whole((1, width))],
        "cross_enter",
        after=after,
        scratch=[pltpu.VMEM((width, width), bf16), pltpu.VMEM((width, rows), bf16)],
    )


def cross_backward(q2, do2, o2, keyval, probs, after):
    rows, width = q2.shape
    seqs, cols, count = keyval.shape
    length = rows // seqs
    chunk = 512

    def kernel(q_ref, do_ref, o_ref, kv_ref, p_ref, dq_ref, dkv_ref):
        q, do = q_ref[...], do_ref[...]
        low, high = heads_low(q), heads_high(do)
        low_t, high_t = low.T, high.T
        product = do.astype(f32) * o_ref[...].astype(f32)
        keep = low_lanes(product.shape)
        inner = jnp.concatenate(
            [
                jnp.sum(jnp.where(keep, product, 0.0), axis=-1, keepdims=True),
                jnp.sum(jnp.where(keep, 0.0, product), axis=-1, keepdims=True),
            ],
            axis=0,
        )
        dq = jnp.zeros((2 * length, PAIR), f32)
        for c in range(count // chunk):
            cut = slice(c * chunk, (c + 1) * chunk)
            kv = kv_ref[0, :, cut]
            p = p_ref[0, :, cut]
            dp = dot(high, kv)
            ds = (p.astype(f32) * (dp - inner)).astype(bf16)
            dq += dot(ds, kv, 1, 1)
            dkv_ref[0, :, cut] = (dot(low_t, ds) + dot(high_t, p)).astype(bf16)
        dq_ref[...] = merge_low(dq).astype(bf16)

    heads_block = pl.BlockSpec((length, PAIR), lambda b, g: (b, g))
    kv_block = pl.BlockSpec((1, PAIR, count), lambda b, g: (b, g, 0))
    return call(
        kernel,
        [q2, do2, o2, keyval, probs],
        [
            heads_block,
            heads_block,
            heads_block,
            kv_block,
            pl.BlockSpec((1, 2 * length, count), lambda b, g: (b * KVH + g, 0, 0)),
        ],
        (struct((rows, width), bf16), struct((seqs, cols, count), bf16)),
        [heads_block, kv_block],
        "cross_backward",
        after=after,
        grid=(seqs, KVH),
    )


def keyval_weight_grad(links, memory, grad_keyval, small, after):
    seqs, count, width = memory.shape
    cols = grad_keyval.shape[1]
    tile = 512
    steps = count // tile
    wide = cols + EXTRA
    split = (2, width // 4, wide)

    def kernel(spot, mem_ref, dkv_ref, small_ref, keep_ref, away_ref, acc_ref):
        b, t = pl.program_id(0), pl.program_id(1)

        @pl.when((b == 0) & (t == 0))
        def _():
            acc_ref[...] = jnp.zeros_like(acc_ref)
            acc_ref[cols : cols + 8] = small_ref[...]

        acc_ref[:cols] += dot(dkv_ref[0], mem_ref[0])

        @pl.when((b == seqs - 1) & (t == steps - 1))
        def _():
            half = split[1]
            for hi in range(2):
                for out, at in ((keep_ref, spot[1]), (away_ref, 1 - spot[1])):
                    lanes = pl.ds(pl.multiple_of((hi * 2 + at) * half, half), half)
                    out[hi] = acc_ref[:, lanes].T.astype(bf16)

    return call(
        kernel,
        [links.spot, memory, grad_keyval, small],
        [
            smem(),
            pl.BlockSpec((1, tile, width), lambda b, t: (b, t, 0)),
            pl.BlockSpec((1, cols, tile), lambda b, t: (b, 0, t)),
            whole((8, width)),
        ],
        (struct(split, bf16), struct(split, bf16)),
        [whole(split)] * 2,
        "keyval_weight_grad",
        after=after,
        grid=(seqs, steps),
        scratch=[pltpu.VMEM((wide, width), f32)],
    )


def memory_gradient(links, grad_keyval, blocks, after):
    seqs, cols, count = grad_keyval.shape
    width = cols
    tile = 512
    n = blocks.count

    def kernel(spot, dkv_ref, *refs):
        out_ref, w_ref = refs[n:]

        @pl.when((pl.program_id(0) == 0) & (pl.program_id(1) == 0))
        def _():
            blocks.put(spot, refs[:n], w_ref)

        out_ref[0] = dot(dkv_ref[0].T, w_ref[...], 1, 1).astype(bf16)

    return call(
        kernel,
        [links.spot, grad_keyval] + blocks.arrays,
        [smem(), pl.BlockSpec((1, cols, tile), lambda b, t: (b, 0, t))] + blocks.specs(cols, 0),
        struct((seqs, count, width), bf16),
        pl.BlockSpec((1, tile, width), lambda b, t: (b, t, 0)),
        "memory_gradient",
        after=after,
        grid=(seqs, count // tile),
        scratch=[pltpu.VMEM((width, cols), bf16)],
    )


def causal_enter(links, dx2, x1, gain_cross, n2, dq2, o1, out_blocks, query_blocks, after):
    rows, width = x1.shape
    n, m = out_blocks.count, out_blocks.count + query_blocks.count
    split = (2, width // 4, 2 * width)

    def kernel(spot, dx2_ref, x1_ref, g_ref, n2_ref, dq2_ref, o1_ref, *refs):
        dx_ref, do_ref, keep_ref, away_ref, gg_ref, wo_ref, wq_ref, o1t_ref, n2t_ref = refs[m:]
        out_blocks.put(spot, refs[:n], wo_ref)
        query_blocks.put(spot, refs[n:m], wq_ref)
        dq2 = dq2_ref[...]
        grad_rows, grad_gain = norm_back(dot(dq2, wq_ref[...], 1, 1), x1_ref[...], g_ref[...])
        gg_ref[...] = grad_gain
        dx1 = dx2_ref[...] + grad_rows
        dx_ref[...] = dx1
        da = dx1.astype(bf16)
        do_ref[...] = dot(da, wo_ref[...], 1, 1).astype(bf16)
        o1t_ref[...] = o1_ref[...].T
        split_rows(o1t_ref, da, spot[1], keep_ref.at[:, :, :width], away_ref.at[:, :, :width])
        n2t_ref[...] = n2_ref[...].T
        split_rows(n2t_ref, dq2, spot[1], keep_ref.at[:, :, width:], away_ref.at[:, :, width:])

    return call(
        kernel,
        [links.spot, dx2, x1, gain_cross, n2, dq2, o1] + out_blocks.arrays + query_blocks.arrays,
        [smem(), whole((rows, width)), whole((rows, width)), whole((1, width))]
        + [whole((rows, width))] * 3
        + out_blocks.specs(width, 2)
        + query_blocks.specs(width, 0),
        (
            struct((rows, width), f32),
            struct((rows, width), bf16),
            struct(split, bf16),
            struct(split, bf16),
            struct((1, width), f32),
        ),
        [whole((rows, width))] * 2 + [whole(split)] * 2 + [whole((1, width))],
        "causal_enter",
        after=after,
        scratch=[
            pltpu.VMEM((width, width), bf16),
            pltpu.VMEM((width, width), bf16),
            pltpu.VMEM((width, rows), bf16),
            pltpu.VMEM((width, rows), bf16),
        ],
    )


def causal_backward(links, lengths, dx1, do1, qkv1, n1, x, gain_causal, table, blocks, after):
    rows, width = n1.shape
    cols = qkv1.shape[1]
    seqs = lengths.shape[0]
    length = rows // seqs
    n = blocks.count
    split = (2, width // 4, cols)

    def kernel(spot, len_ref, dx1_ref, do_ref, qkv_ref, n1_ref, x_ref, g1_ref, tab_ref, *refs):
        keep_ref, away_ref, gg1_ref, bias_ref, dx_ref, w_ref, dqkv_ref, n1t_ref = refs[n:]
        blocks.put(spot, refs[:n], w_ref)
        tab = tab_ref[...]
        i = lax.broadcasted_iota(jnp.int32, (length, length), 0)
        j = lax.broadcasted_iota(jnp.int32, (length, length), 1)
        flip = jnp.where(i + j == length - 1, 1.0, 0.0).astype(bf16)
        for g in range(KVH):
            lanes = slice(g * PAIR, (g + 1) * PAIR)
            kv_lanes = slice(width + g * PAIR, width + (g + 1) * PAIR)
            even_sum = jnp.zeros((length, length), f32)
            odd_sum = jnp.zeros((length, length), f32)
            for b in range(seqs):
                part = slice(b * length, (b + 1) * length)
                keyval = qkv_ref[part, kv_lanes]
                low = heads_low(qkv_ref[part, lanes])
                high = heads_high(do_ref[part, lanes])
                p = causal_probs(low, keyval, tab, g, length, len_ref[b])
                dp = dot(high, keyval, 1, 1)
                ds = (p * (dp - jnp.sum(p * dp, axis=-1, keepdims=True))).astype(bf16)
                even_sum += dot(flip, ds[:length])
                odd_sum += dot(flip, ds[length:])
                dqkv_ref[part, lanes] = merge_low(dot(ds, keyval)).astype(bf16)
                dqkv_ref[part, kv_lanes] = (
                    dot(ds.T, low) + dot(p.astype(bf16).T, high)
                ).astype(bf16)
            bias_ref[2 * g : 2 * g + 1] = diagonal_sums(even_sum)
            bias_ref[2 * g + 1 : 2 * g + 2] = diagonal_sums(odd_sum)
        dqkv = dqkv_ref[...]
        n1t_ref[...] = n1_ref[...].T
        split_rows(n1t_ref, dqkv, spot[1], keep_ref, away_ref)
        grad_rows, grad_gain = norm_back(
            dot(dqkv, w_ref[...], 1, 1), x_ref[...].astype(f32), g1_ref[...]
        )
        gg1_ref[...] = grad_gain
        dx_ref[...] = (dx1_ref[...] + grad_rows).astype(bf16)

    return call(
        kernel,
        [links.spot, lengths, dx1, do1, qkv1, n1, x, gain_causal, table] + blocks.arrays,
        [smem(), smem(), whole((rows, width)), whole((rows, width)), whole((rows, cols))]
        + [whole((rows, width))] * 2
        + [whole((1, width)), whole(table.shape)]
        + blocks.specs(cols, 0),
        (
            struct(split, bf16),
            struct(split, bf16),
            struct((1, width), f32),
            struct((HEADS, bucket_reach), f32),
            struct((rows, width), bf16),
        ),
        [whole(split)] * 2 + [whole((1, width)), whole((HEADS, bucket_reach)), whole((rows, width))],
        "causal_backward",
        after=after,
        scratch=[
            pltpu.VMEM((width, cols), bf16),
            pltpu.VMEM((rows, cols), bf16),
            pltpu.VMEM((width, rows), bf16),
        ],
    )


def interleave(w_key, w_value):
    r = w_key.shape[0]
    return jnp.concatenate(
        [w_key.reshape(r, KVH, HD), w_value.reshape(r, KVH, HD)], axis=2
    ).reshape(r, KVH * PAIR)


def part_keyval(pair):
    r = pair.shape[0]
    both = pair.reshape(r, KVH, 2, HD)
    return both[:, :, 0].reshape(r, KVH * HD), both[:, :, 1].reshape(r, KVH * HD)


XY = ("lo", "hi")
YX = ("hi", "lo")
EXTRA = 128


def local(
    links,
    inputs,
    memory,
    lengths,
    cotangent,
    causal_query,
    causal_key,
    causal_value,
    causal_out,
    cross_query,
    cross_key,
    cross_value,
    cross_out,
    feed_gate,
    feed_up,
    feed_down,
    gain_causal,
    gain_cross,
    gain_feed,
    bias_table,
):
    links.locate()
    seqs, length, width = inputs.shape
    rows = seqs * length
    r = causal_query.shape[0]
    devices = links.nf * links.nd
    table_part = bias_table.shape[0]
    x = inputs.reshape(rows, width)
    cot = cotangent.reshape(rows, width)

    small = jnp.concatenate(
        [
            gain_causal[:, None],
            gain_cross[:, None],
            gain_feed[:, None],
            jnp.pad(bias_table[:, None], ((0, r - table_part), (0, 0))),
            jnp.zeros((r, EXTRA - 4), bf16),
        ],
        axis=1,
    )
    first_shard = jnp.concatenate([interleave(cross_key, cross_value), small], axis=1)
    causal_shard = jnp.concatenate(
        [causal_query, interleave(causal_key, causal_value), causal_out], axis=1
    )
    second_shard = jnp.concatenate([causal_shard, cross_query, cross_out], axis=1)
    units = feed_gate.shape[1] // links.nf
    feed_wide = jnp.stack(
        [
            jnp.concatenate([w[:, f * units : (f + 1) * units] for w in (feed_gate, feed_up)], axis=1)
            for f in range(links.nf)
        ]
    )

    first_pieces = links.spread_ring(first_shard)
    feed_near = links.quarters(tie(feed_wide, first_pieces[-1])).reshape(4 * r, 2 * units)
    second_pieces = links.spread_ring(second_shard, first_pieces[1:])
    first_blocks = links.grow(jnp.stack(first_pieces), XY)
    cot_core = links.send(tie(cot, first_blocks.arrays[-1]), "core")
    keyval, small_all = project_memory(links, memory, first_blocks)
    feed_pieces = links.spread_ring(feed_near, second_pieces[1:])

    cut = causal_shard.shape[1]
    causal_stack = jnp.stack([p[:, :cut] for p in second_pieces])
    cross_stack = jnp.stack([p[:, cut:] for p in second_pieces])
    causal_blocks = links.grow(causal_stack, XY)
    cross_blocks = links.grow(cross_stack, YX)
    down_pieces = links.spread_ring(feed_down, feed_pieces[1:])
    feed_stack = jnp.stack(feed_pieces)
    feed_far = links.send(tie(feed_stack, cross_blocks.arrays[1]), "lo")
    feed_blocks = Blocks(
        links, [(feed_stack[None], [{}]), (feed_far[None], [{"lo": 1}])], quads=True
    )
    cot_hi = links.send(tie(cot, causal_blocks.arrays[1]), "hi")
    cot_both = links.send(cot_hi, "core")
    cots = (cot, cot_core, cot_hi, cot_both)

    gain_one, gain_two, gain_three = (small_all[i : i + 1] for i in range(3))
    bias_all = small_all[3].reshape(devices, r)[:, :table_part].reshape(HEADS, BUCKETS)
    onehot = jnp.asarray(reversed_buckets())
    table = jnp.dot(bias_all.astype(bf16), onehot.astype(bf16), preferred_element_type=f32)

    x1, n1, qkv1, o1 = causal_forward(
        links, inputs, causal_blocks, gain_one, table, lengths, (keyval,)
    )
    down_stack = jnp.stack(down_pieces)
    down_far = links.send(tie(down_stack, feed_far), "lo")
    n2, q2, o2, x2, n3, probs = cross_forward(links, x1, keyval, cross_blocks, gain_two, gain_three)
    n3_hi = links.send(n3, "hi")
    n3_core = links.send(n3, "core")
    n3_both = links.send(n3_hi, "core")
    n3s = (n3, n3_core, n3_hi, n3_both)
    w_down = assemble(links, down_stack, down_far, (x2,))
    hidden, dgate, dup, dn3, dn3_hi, dn3_away = feed_through(
        links, n3s, cots, feed_blocks, w_down, ()
    )

    def over_four(own, hi, away, after=()):
        got = links.send(tie(away, *after), "core")
        passed = (hi + got[rows:].astype(f32)).astype(bf16)
        return own, got[:rows], links.send(passed, "hi")

    dn3_terms = over_four(dn3, dn3_hi, dn3_away)
    y, y_hi, y_away, grad_gu, grad_down = feed_weight_grads(
        n3s, cots, hidden, dgate, dup, w_down, ()
    )

    def split(a, way_axes):
        return a.reshape(tuple(links.lengths[w] for w in way_axes) + (-1, a.shape[-1]))

    every = ("hi", "core", "ring", "lo")
    apart = ("hi", "ring", "lo")
    feed_sums = Scatter(
        links,
        [
            ([Leaf(split(grad_gu, every), every)], ("lo",)),
            ([Leaf(split(grad_down, ("ring", "lo")), ("ring", "lo"))], ("lo",)),
        ],
    )

    def halves(keep, away, *windows):
        keep, away = split(keep, apart), split(away, apart)
        got = links.send(away, "core")
        return [
            ([Leaf(keep, apart, (), w, i), Leaf(got, apart, (), w, i)], order)
            for w, i, order in windows
        ]

    done = feed_sums.step((y,))
    dx2, do2, keep, away, grad_gain_three = cross_enter(
        links, x2, gain_three, *dn3_terms, cot, o2, cross_blocks, done
    )
    jobs_o2 = halves(keep, away, (width, 0, YX))
    y_terms = over_four(y, y_hi, y_away, (dx2,))
    dq2, grad_keyval = cross_backward(q2, do2, o2, keyval, probs, (dx2,))
    dx1, do1, keep, away, grad_gain_two = causal_enter(
        links, dx2, x1, gain_two, n2, dq2, o1, causal_blocks, cross_blocks, ()
    )
    jobs_o1q2 = halves(keep, away, (width, 0, XY), (width, 1, YX))
    done = feed_sums.spread((dx1,))
    early_sums = Scatter(links, jobs_o2 + jobs_o1q2)
    done = early_sums.step(done)
    keep, away, grad_gain_one, grad_bias, input_grad = causal_backward(
        links, lengths, dx1, do1, qkv1, n1, x, gain_one, table, causal_blocks, done
    )
    jobs_qkv1 = halves(keep, away, (width, 0, XY), (width, 1, YX))
    done = early_sums.step((input_grad,))

    grad_table = lax.dot_general(
        grad_bias, onehot, (((1,), (1,)), ((), ())), precision=lax.Precision.HIGHEST
    )
    table_rows = jnp.pad(
        grad_table.reshape(devices, table_part), ((0, 0), (0, r - table_part))
    ).reshape(1, width)
    small_rows = jnp.concatenate(
        [grad_gain_one, grad_gain_two, grad_gain_three, table_rows, jnp.zeros((4, width), f32)],
        axis=0,
    )
    middle_sums = Scatter(links, jobs_qkv1)
    done = middle_sums.step(done)
    keep, away = keyval_weight_grad(links, memory, grad_keyval, small_rows, done)
    jobs_kv2 = halves(keep, away, (KVH * PAIR + EXTRA, 0, YX))
    late_sums = Scatter(links, jobs_kv2)
    done = early_sums.spread((keep,))
    done = middle_sums.step(done)
    done = late_sums.step(done)
    memory_grad = memory_gradient(links, grad_keyval, first_blocks, done)
    done = middle_sums.spread((memory_grad,))
    done = late_sums.step(done)
    late_sums.spread(done)

    layer_out = (x2 + sum(t.astype(f32) for t in y_terms)).astype(bf16)
    sum_gu, sum_down = feed_sums.results
    sum_o2, sum_o1, sum_q2 = early_sums.results
    sum_q1, sum_kv1 = middle_sums.results
    sum_kv2, sum_small = late_sums.results[0][:, :width], late_sums.results[0][:, width:]
    sum_k1, sum_v1 = part_keyval(sum_kv1)
    sum_k2, sum_v2 = part_keyval(sum_kv2)

    wide = sum_gu.reshape(links.nf, r, 2 * units)
    mine = links.hi * 2 + links.core
    near = [lax.dynamic_index_in_dim(wide, mine, 0, keepdims=False)]
    for flip, way in ((1, "core"), (2, "hi"), (3, "both")):
        theirs = lax.dynamic_index_in_dim(wide, mine ^ flip, 0, keepdims=False).astype(bf16)
        near.append(links.send(theirs, way).astype(f32))
    wide = links.unquarter(jnp.stack(near))
    sum_gate, sum_up = (
        wide[:, :, i * units : (i + 1) * units].transpose(1, 0, 2).reshape(r, links.nf * units)
        for i in range(2)
    )
    return (
        layer_out.reshape(seqs, length, width),
        input_grad.reshape(seqs, length, width),
        memory_grad,
        sum_q1,
        sum_k1,
        sum_v1,
        sum_o1,
        sum_q2,
        sum_k2,
        sum_v2,
        sum_o2,
        sum_gate,
        sum_up,
        sum_down,
        sum_small[:, 0],
        sum_small[:, 1],
        sum_small[:, 2],
        sum_small[:table_part, 3],
    )


def solution(mesh):
    three = P(AXES, None, None)
    two = P(AXES, None)
    one = P(AXES)
    in_specs = (three, three, one, three) + (two,) * 11 + (one,) * 4
    out_specs = (three,) * 3 + (two,) * 11 + (one,) * 4
    body = functools.partial(local, Links(mesh))
    return jax.shard_map(body, mesh=mesh, in_specs=in_specs, out_specs=out_specs, check_vma=False)
```

```python
import functools

import jax
import jax.numpy as jnp
import numpy as np
from jax import lax
from jax.experimental import pallas as pl
from jax.experimental.pallas import tpu as pltpu
from jax.sharding import PartitionSpec as P

HEADS = 16
HD = 64
BUCKETS = 32
KVH = 8
PAIR = 2 * HD
AXES = ("fsdp", "dp")
norm_eps = 1e-06
masked_score = -1000000000.0
bucket_reach = 128
f32 = jnp.float32
bf16 = jnp.bfloat16
VMEM_LIMIT = 56 * 1024 * 1024
PLAN = 2e9


def reversed_buckets():
    distance = (-np.arange(bucket_reach)) % bucket_reach
    exact_count = BUCKETS // 2
    spread = (
        np.log(np.maximum(distance, 1) / exact_count)
        / np.log(bucket_reach / exact_count)
        * (BUCKETS - exact_count)
    )
    far_bucket = np.minimum(exact_count + np.floor(spread).astype(np.int64), BUCKETS - 1)
    bucket_id = np.where(distance < exact_count, distance, far_bucket)
    return (bucket_id[None] == np.arange(BUCKETS)[:, None]).astype(np.float32)


def dot(a, b, ca=1, cb=0):
    return lax.dot_general(a, b, (((ca,), (cb,)), ((), ())), preferred_element_type=f32)


def call(kernel, ins, in_specs, out_shape, out_specs, name, after=(), grid=(1,), scratch=(), prefetch=None, micros=1):
    lead = 0 if prefetch is None else 1
    n = lead + len(ins)

    def body(*refs):
        kernel(*refs[:n], *refs[n + len(after) :])

    spec = pltpu.PrefetchScalarGridSpec(
        num_scalar_prefetch=lead,
        grid=grid,
        in_specs=list(in_specs) + [pl.BlockSpec(memory_space=pl.ANY)] * len(after),
        out_specs=out_specs,
        scratch_shapes=list(scratch),
    )
    front = () if prefetch is None else (prefetch,)
    return pl.pallas_call(
        body,
        grid_spec=spec,
        out_shape=out_shape,
        compiler_params=pltpu.CompilerParams(vmem_limit_bytes=VMEM_LIMIT),
        cost_estimate=pl.CostEstimate(
            flops=int(micros * PLAN), bytes_accessed=1000, transcendentals=0
        ),
        name=name,
    )(*front, *ins, *after)


def whole(shape):
    return pl.BlockSpec(shape, lambda *_: (0,) * len(shape))


def struct(shape, dtype):
    return jax.ShapeDtypeStruct(shape, dtype)


def smem():
    return pl.BlockSpec(memory_space=pltpu.SMEM)


class Links:
    def __init__(self, mesh):
        nf, nd = mesh.shape["fsdp"], mesh.shape["dp"]
        self.nf, self.nd, self.size = nf, nd, nd // 2
        self.bits = tuple(f"z{b}" for b in reversed(range(self.size.bit_length() - 1)))
        self.names = ("hi", "core", "ring", "lo") + self.bits
        spots = [(f, d) for f in range(nf) for d in range(nd)]

        def pairs(flip_f, flip_d):
            return [(f * nd + d, (f ^ flip_f) * nd + (d ^ flip_d)) for f, d in spots]

        self.pairs = {"core": pairs(1, 0), "hi": pairs(2, 0), "both": pairs(3, 0), "lo": pairs(0, 1)}
        self.masks = {}
        for name in self.bits:
            self.masks[name] = 1 << int(name[1:])
            self.pairs[name] = pairs(0, 2 << int(name[1:]))

    def locate(self):
        f, d = lax.axis_index("fsdp"), lax.axis_index("dp")
        self.hi, self.core, self.ring, self.lo = f // 2, f % 2, d // 2, d % 2
        zs = [(self.ring // self.masks[name]) % 2 for name in self.bits]
        self.spot = jnp.stack([self.hi, self.core, self.ring, self.lo, *zs]).astype(jnp.int32)

    def send(self, a, way, *after):
        return lax.ppermute(tie(a, *after), AXES, self.pairs[way])

    def grow(self, held, ways, *after, then=()):
        array, fars = held
        for way in ways:
            got = self.send(array, way, *after)
            after = ()
            array = jnp.concatenate([tie(array, *then), got], axis=0)
            fars = fars + [f | {way} for f in fars]
        return array, fars

    def quarters(self, wide, *after):
        mine = self.hi * 2 + self.core
        out = [lax.dynamic_index_in_dim(wide, mine, 0, keepdims=False)]
        for flip, way in ((1, "core"), (2, "hi"), (3, "both")):
            theirs = lax.dynamic_index_in_dim(wide, mine ^ flip, 0, keepdims=False)
            out.append(self.send(theirs, way, *after))
        return jnp.concatenate(out, axis=0)

    def unquarter(self, wide, after):
        _, _, r, c = wide.shape
        wide = wide.reshape(self.nf, r, c)
        mine = self.hi * 2 + self.core
        near = [tie(lax.dynamic_index_in_dim(wide, mine, 0, keepdims=False), *after)]
        for flip, way in ((1, "core"), (2, "hi"), (3, "both")):
            theirs = lax.dynamic_index_in_dim(wide, mine ^ flip, 0, keepdims=False).astype(bf16)
            near.append(tie(self.send(theirs, way), *after).astype(f32))
        near = jnp.stack(near)
        return [lax.dynamic_index_in_dim(near, mine ^ f, 0, keepdims=False) for f in range(self.nf)]


class Blocks:
    def __init__(self, links, *helds, quads=False):
        self.links = links
        self.arrays = [a for a, _ in helds]
        self.fars = [f for _, f in helds]
        self.quads = quads
        _, self.r, self.c = self.arrays[0].shape
        self.count = len(helds)

    def specs(self, width=None, index=0):
        return [
            pl.BlockSpec((*a.shape[:2], width or self.c), lambda *_: (0, 0, index))
            for a in self.arrays
        ]

    def put(self, spot, refs, *outs):
        quads = [(0, 0), (0, 1), (1, 0), (1, 1)] if self.quads else [None]
        r = self.r // len(quads)
        for ref, fars in zip(refs, self.fars):
            for i, far in enumerate(fars):
                for q, quad in enumerate(quads):
                    far_hi, far_core = quad or ("hi" in far, "core" in far)
                    at_hi = 1 - spot[0] if far_hi else spot[0]
                    at_core = 1 - spot[1] if far_core else spot[1]
                    row = ((at_hi * 2 + at_core) * self.links.nd + place_of(self.links, spot, far)) * r
                    rows = pl.ds(pl.multiple_of(row, r), r)
                    left = 0
                    for out in outs:
                        width = out.shape[-1]
                        out[rows, :] = ref[i, q * r : (q + 1) * r, left : left + width]
                        left += width


def place_of(links, spot, far):
    mask = sum(links.masks[name] for name in links.bits if name in far)
    at_ring = jnp.bitwise_xor(spot[2], mask) if mask else spot[2]
    at_lo = 1 - spot[3] if "lo" in far else spot[3]
    return at_ring * 2 + at_lo


def tie(x, *after):
    return lax.optimization_barrier((x, *after))[0] if after else x


def assemble(links, helds, after=()):
    _, r, c = helds[0][0].shape
    n = len(helds)
    most = max(len(f) for _, f in helds)

    def kernel(spot, *refs):
        out, held, sems_in, sems_out = refs[n:]
        copies = []
        for k, (ref, (_, fars)) in enumerate(zip(refs, helds)):
            for i, far in enumerate(fars):
                copies.append(
                    (
                        pltpu.make_async_copy(ref.at[i], held.at[k, i], sems_in.at[k, i]),
                        pltpu.make_async_copy(
                            held.at[k, i], out.at[place_of(links, spot, far)], sems_out.at[k, i]
                        ),
                    )
                )
        for one, _ in copies:
            one.start()
        for one, two in copies:
            one.wait()
            two.start()
        for _, two in copies:
            two.wait()

    out = call(
        kernel,
        [links.spot] + [a for a, _ in helds],
        [smem()] + [pl.BlockSpec(memory_space=pl.ANY)] * n,
        struct((links.nd, r, c), bf16),
        pl.BlockSpec(memory_space=pl.ANY),
        "assemble",
        micros=3,
        after=after,
        scratch=[
            pltpu.VMEM((n, most, r, c), bf16),
            pltpu.SemaphoreType.DMA((n, most)),
            pltpu.SemaphoreType.DMA((n, most)),
        ],
    )
    return out.reshape(-1, c)


class Leaf:
    def __init__(self, array, axes, left=0, width=None, held=()):
        self.array, self.axes, self.left, self.held = array, axes, left, dict(held)
        self.width = width or array.shape[-1]

    def hold(self, way, far):
        held = dict(self.held)
        if way in self.axes:
            held[way] = far
        return Leaf(self.array, self.axes, self.left, self.width, held)

    def free(self):
        return tuple(a for a in self.axes if a not in self.held)

    def spec(self, links):
        shape = tuple(None if a in self.held else 2 for a in self.axes) + self.array.shape[-2:]
        picks = [(self.held.get(a), links.names.index(a)) for a in self.axes]

        def index(_, spot):
            return (
                *(0 if far is None else 1 - spot[i] if far else spot[i] for far, i in picks),
                0,
                0,
            )

        return pl.BlockSpec(shape, index)


class Sum:
    def __init__(self, leaves, ways):
        self.leaves, self.ways = leaves, list(ways)


def gather_terms(links, leaves_of):
    ins = [leaf.array for leaves in leaves_of for leaf in leaves]
    specs = [leaf.spec(links) for leaves in leaves_of for leaf in leaves]

    def totals(refs):
        n = 0
        for leaves in leaves_of:
            total = None
            for leaf in leaves:
                term = refs[n][..., leaf.left : leaf.left + leaf.width].astype(f32)
                total = term if total is None else total + term
                n += 1
            yield total

    return ins, specs, totals


def advance(links, sums, after=()):
    moves = []
    for one in sums:
        way = one.ways.pop(0)
        moves.append((way, [leaf.hold(way, True) for leaf in one.leaves]))
        one.leaves = [leaf.hold(way, False) for leaf in one.leaves]
    groups, where = {}, []
    for way, leaves in moves:
        free = leaves[0].free()
        key = (way, free, leaves[0].array.shape[-2])
        left = groups.get(key, 0)
        groups[key] = left + leaves[0].width
        where.append((key, left, leaves[0].width))
    keys = list(groups)
    outs = [struct((2,) * len(free) + (r, groups[way, free, r]), bf16) for way, free, r in keys]
    ins, specs, totals = gather_terms(links, [leaves for _, leaves in moves])

    def kernel(spot, *refs):
        for total, (key, left, width) in zip(totals(refs), where):
            refs[len(ins) + keys.index(key)][..., left : left + width] = total.astype(bf16)

    sent = call(
        kernel, ins, specs, outs, [whole(o.shape) for o in outs], "combine", micros=3, after=after, prefetch=links.spot
    )
    got = {key: links.send(a, key[0]) for key, a in zip(keys, sent)}
    for one, (key, left, width) in zip(sums, where):
        one.leaves.append(Leaf(got[key], key[1], left, width))
    return (sent[0],)


def finish(links, sums, cuts, after=()):
    ins, specs, totals = gather_terms(links, [one.leaves for one in sums])
    outs = [
        struct((2,) * len(one.leaves[0].free()) + (one.leaves[0].array.shape[-2], width), f32)
        for one, widths in zip(sums, cuts)
        for width in widths
    ]

    def kernel(spot, *refs):
        n = len(ins)
        for total, widths in zip(totals(refs), cuts):
            left = 0
            for width in widths:
                refs[n][...] = total[..., left : left + width]
                left += width
                n += 1

    return call(
        kernel, ins, specs, outs, [whole(o.shape) for o in outs], "finish", micros=3, after=after, prefetch=links.spot
    )


def norm_scale(rows):
    return lax.rsqrt(jnp.mean(rows * rows, axis=-1, keepdims=True) + norm_eps)


def norm_back(grad_normed, rows, gain):
    scale = norm_scale(rows)
    scaled = grad_normed * gain
    inner_mean = jnp.mean(scaled * rows, axis=-1, keepdims=True)
    grad_rows = scale * scaled - rows * (scale * scale * scale) * inner_mean
    return grad_rows, jnp.sum(grad_normed * rows * scale, axis=0, keepdims=True)


def swap_halves(block):
    return pltpu.roll(block.astype(f32), HD, 1).astype(bf16)


def low_lanes(shape):
    return lax.broadcasted_iota(jnp.int32, shape, 1) < HD


def heads_low(block):
    keep = low_lanes(block.shape)
    zero = jnp.zeros_like(block)
    return jnp.concatenate(
        [jnp.where(keep, block, zero), jnp.where(keep, swap_halves(block), zero)], axis=0
    )


def heads_high(block):
    keep = low_lanes(block.shape)
    zero = jnp.zeros_like(block)
    return jnp.concatenate(
        [jnp.where(keep, zero, swap_halves(block)), jnp.where(keep, zero, block)], axis=0
    )


def merge_low(both):
    half = both.shape[0] // 2
    even, odd = both[:half], both[half:]
    return jnp.where(low_lanes(even.shape), even, pltpu.roll(odd, HD, 1))


def merge_high(both):
    half = both.shape[0] // 2
    even, odd = both[:half], both[half:]
    return jnp.where(low_lanes(even.shape), pltpu.roll(even, HD, 1), odd)


def toeplitz(row, length):
    return pltpu.roll(jnp.broadcast_to(row, (length, length)), 0, 1, stride=1, stride_axis=0)


def diagonal_sums(flipped):
    turned = pltpu.roll(flipped, 1, 1, stride=1, stride_axis=0)
    return jnp.sum(turned, axis=0, keepdims=True)


def causal_probs(low, keyval, table, g, length, valid_len):
    s = dot(low, keyval, 1, 1)
    bias = jnp.concatenate(
        [toeplitz(table[2 * g : 2 * g + 1], length), toeplitz(table[2 * g + 1 : 2 * g + 2], length)],
        axis=0,
    )
    i = lax.broadcasted_iota(jnp.int32, (length, length), 0)
    j = lax.broadcasted_iota(jnp.int32, (length, length), 1)
    valid = (j <= i) & (j < valid_len)
    valid = jnp.concatenate([valid, valid], axis=0)
    s = jnp.where(valid, s + bias, masked_score)
    e = jnp.exp(s - jnp.max(s, axis=-1, keepdims=True))
    return e / jnp.sum(e, axis=-1, keepdims=True)


def split_rows(lhs_t, rhs, core, keep, away):
    half = keep.shape[1]
    for hi in range(keep.shape[0]):
        for out, at in ((keep, core), (away, 1 - core)):
            row = pl.multiple_of((hi * 2 + at) * half, half)
            out[hi] = dot(lhs_t[pl.ds(row, half), :], rhs).astype(bf16)


def project_memory(links, memory, blocks):
    seqs, count, width = memory.shape
    cols = KVH * PAIR
    tile = 512
    n = blocks.count

    def kernel(spot, mem_ref, *refs):
        held = refs[:n]
        out_ref, small_ref, w_ref, wt_ref = refs[n:]

        @pl.when((pl.program_id(0) == 0) & (pl.program_id(1) == 0))
        def _():
            blocks.put(spot, held, w_ref)
            wt_ref[...] = w_ref[:, :cols].T
            small_ref[...] = w_ref[:, cols:].astype(f32).T[:8]

        out_ref[0] = dot(wt_ref[...], mem_ref[0], 1, 1).astype(bf16)

    return call(
        kernel,
        [links.spot, memory] + blocks.arrays,
        [smem(), pl.BlockSpec((1, tile, width), lambda b, t: (b, t, 0))] + blocks.specs(),
        (struct((seqs, cols, count), bf16), struct((8, width), f32)),
        [pl.BlockSpec((1, cols, tile), lambda b, t: (b, 0, t)), whole((8, width))],
        "project_memory",
        micros=15,
        grid=(seqs, count // tile),
        scratch=[pltpu.VMEM((width, blocks.c), bf16), pltpu.VMEM((cols, width), bf16)],
    )


def causal_forward(links, x, blocks, gain, table, lengths, after):
    seqs, length, width = x.shape
    rows = seqs * length
    cols = 2 * width
    n = blocks.count

    def kernel(spot, len_ref, x_ref, gain_ref, tab_ref, *refs):
        x1_ref, n1_ref, qkv_ref, o1_ref, w_ref, wo_ref = refs[n:]
        blocks.put(spot, refs[:n], w_ref, wo_ref)
        xf = x_ref[...].astype(f32)
        n1 = (xf * norm_scale(xf) * gain_ref[...]).astype(bf16)
        n1_ref[...] = n1
        qkv_ref[...] = dot(n1, w_ref[...]).astype(bf16)
        tab = tab_ref[...]
        for g in range(KVH):
            lanes = slice(g * PAIR, (g + 1) * PAIR)
            kv_lanes = slice(width + g * PAIR, width + (g + 1) * PAIR)
            for b in range(seqs):
                part = slice(b * length, (b + 1) * length)
                keyval = qkv_ref[part, kv_lanes]
                p = causal_probs(
                    heads_low(qkv_ref[part, lanes]), keyval, tab, g, length, len_ref[b]
                )
                o1_ref[part, lanes] = merge_high(dot(p.astype(bf16), keyval)).astype(bf16)
        x1_ref[...] = xf + dot(o1_ref[...], wo_ref[...])

    return call(
        kernel,
        [links.spot, lengths, x.reshape(rows, width), gain, table] + blocks.arrays,
        [smem(), smem(), whole((rows, width)), whole((1, width)), whole(table.shape)]
        + blocks.specs(cols + width, 0),
        (
            struct((rows, width), f32),
            struct((rows, width), bf16),
            struct((rows, cols), bf16),
            struct((rows, width), bf16),
        ),
        [whole((rows, width)), whole((rows, width)), whole((rows, cols)), whole((rows, width))],
        "causal_forward",
        micros=9,
        after=after,
        scratch=[pltpu.VMEM((width, cols), bf16), pltpu.VMEM((width, width), bf16)],
    )


def cross_forward(links, x1, keyval, blocks, gain_cross, gain_feed, after):
    rows, width = x1.shape
    seqs, _, count = keyval.shape
    length = rows // seqs
    n = blocks.count * 2

    def kernel(spot, x1_ref, kv_ref, g2_ref, g3_ref, *refs):
        n2_ref, q2_ref, o2_ref, x2_ref, n3_ref, p_ref, wq_ref, wo_ref = refs[n:]
        b, g = pl.program_id(0), pl.program_id(1)

        @pl.when((b == 0) & (g == 0))
        def _():
            blocks.put(spot, refs[: n // 2], wq_ref)
            blocks.put(spot, refs[n // 2 : n], wo_ref)
            x1v = x1_ref[...]
            n2 = (x1v * norm_scale(x1v) * g2_ref[...]).astype(bf16)
            n2_ref[...] = n2
            q2_ref[...] = dot(n2, wq_ref[...]).astype(bf16)

        part = pl.ds(pl.multiple_of(b * length, length), length)
        lanes = pl.ds(pl.multiple_of(g * PAIR, PAIR), PAIR)
        kv = kv_ref[0]
        s = dot(heads_low(q2_ref[part, lanes]), kv)
        e = jnp.exp(s - jnp.max(s, axis=-1, keepdims=True))
        p = (e * (1.0 / jnp.sum(e, axis=-1, keepdims=True))).astype(bf16)
        p_ref[0] = p
        o2_ref[part, lanes] = merge_high(dot(p, kv, 1, 1)).astype(bf16)

        @pl.when((b == seqs - 1) & (g == KVH - 1))
        def _():
            x2 = x1_ref[...] + dot(o2_ref[...], wo_ref[...])
            x2_ref[...] = x2
            n3_ref[...] = (x2 * norm_scale(x2) * g3_ref[...]).astype(bf16)

    return call(
        kernel,
        [links.spot, x1, keyval, gain_cross, gain_feed] + blocks.arrays * 2,
        [
            smem(),
            whole((rows, width)),
            pl.BlockSpec((1, PAIR, count), lambda b, g: (b, g, 0)),
            whole((1, width)),
            whole((1, width)),
        ]
        + blocks.specs(width, 3)
        + blocks.specs(width, 4),
        (
            struct((rows, width), bf16),
            struct((rows, width), bf16),
            struct((rows, width), bf16),
            struct((rows, width), f32),
            struct((rows, width), bf16),
            struct((seqs * KVH, 2 * length, count), bf16),
        ),
        [whole((rows, width))] * 5
        + [pl.BlockSpec((1, 2 * length, count), lambda b, g: (b * KVH + g, 0, 0))],
        "cross_forward",
        micros=34,
        after=after,
        grid=(seqs, KVH),
        scratch=[pltpu.VMEM((width, width), bf16)] * 2,
    )


def stack_rows(refs, out):
    rows = refs[0].shape[0]
    for i, ref in enumerate(refs):
        out[i * rows : (i + 1) * rows] = ref[...]


def feed_through(links, n3s, cots, blocks, w_down, after):
    rows, width = n3s[0].shape
    units = w_down.shape[0]
    n = blocks.count
    c0 = np.float32(np.sqrt(2.0 / np.pi))
    c1 = np.float32(0.044715)
    cuts = [slice(i, min(i + 256, units)) for i in range(0, units, 256)]

    def kernel(spot, *refs):
        wd_ref = refs[8]
        held = refs[9 : 9 + n]
        hid_ref, dgate_ref, dup_ref, dn_ref, dn_hi_ref, dn_away_ref = refs[9 + n : 15 + n]
        wg_ref, wu_ref, n3_all, cot_all = refs[15 + n :]
        blocks.put(spot, held, wg_ref, wu_ref)
        stack_rows(refs[:4], n3_all)
        stack_rows(refs[4:8], cot_all)
        for cut in cuts:
            gate = dot(n3_all[...], wg_ref[:, cut])
            up = dot(n3_all[...], wu_ref[:, cut])
            dh = dot(cot_all[...], wd_ref[cut, :], 1, 1)
            square = gate * gate
            t = jnp.tanh(c0 * (gate + c1 * (square * gate)))
            cdf = 0.5 * (1.0 + t)
            value = gate * cdf
            slope = cdf + 0.5 * gate * (1.0 - t * t) * (c0 * (1.0 + 3.0 * c1 * square))
            hid_ref[:, cut] = (value * up).astype(bf16)
            dgate_ref[:, cut] = (dh * up * slope).astype(bf16)
            dup_ref[:, cut] = (dh * value).astype(bf16)
        for i in range(0, width, 256):
            at = slice(i, i + 256)
            dn = dot(dgate_ref[...], wg_ref[at, :], 1, 1) + dot(dup_ref[...], wu_ref[at, :], 1, 1)
            dn_ref[:, at] = dn[:rows]
            dn_away_ref[:rows, at] = dn[rows : 2 * rows].astype(bf16)
            dn_hi_ref[:, at] = dn[2 * rows : 3 * rows]
            dn_away_ref[rows:, at] = dn[3 * rows :].astype(bf16)

    return call(
        kernel,
        [links.spot, *n3s, *cots, w_down] + blocks.arrays,
        [smem()] + [whole((rows, width))] * 8 + [whole(w_down.shape)] + blocks.specs(),
        (
            struct((4 * rows, units), bf16),
            struct((4 * rows, units), bf16),
            struct((4 * rows, units), bf16),
            struct((rows, width), f32),
            struct((rows, width), f32),
            struct((2 * rows, width), bf16),
        ),
        [whole((4 * rows, units))] * 3 + [whole((rows, width))] * 2 + [whole((2 * rows, width))],
        "feed_through",
        micros=14,
        after=after,
        scratch=[
            pltpu.VMEM((width, units), bf16),
            pltpu.VMEM((width, units), bf16),
            pltpu.VMEM((4 * rows, width), bf16),
            pltpu.VMEM((4 * rows, width), bf16),
        ],
    )


def feed_weight_grads(n3s, cots, hidden, dgate, dup, w_down, after):
    rows, width = n3s[0].shape
    units = hidden.shape[1]

    def kernel(*refs):
        hid_ref, dgate_ref, dup_ref, wd_ref = refs[8:12]
        y_ref, y_hi_ref, y_away_ref, gu_ref, gd_ref, n3t_ref, cot_all, hid_t = refs[12:]
        for i in range(4):
            n3t_ref[:, i * rows : (i + 1) * rows] = refs[i][...].T
        stack_rows(refs[4:8], cot_all)
        hid_t[...] = hid_ref[...].T
        for i in range(0, width, 256):
            gu_ref[i : i + 256, :units] = dot(n3t_ref[i : i + 256], dgate_ref[...]).astype(bf16)
            gu_ref[i : i + 256, units:] = dot(n3t_ref[i : i + 256], dup_ref[...]).astype(bf16)
        for i in range(0, units, 352):
            gd_ref[i : i + 352] = dot(hid_t[i : i + 352], cot_all[...]).astype(bf16)
        for i in range(0, width, 256):
            at = slice(i, i + 256)
            y = dot(hid_ref[...], wd_ref[:, at])
            y_ref[:, at] = y[:rows]
            y_away_ref[:rows, at] = y[rows : 2 * rows].astype(bf16)
            y_hi_ref[:, at] = y[2 * rows : 3 * rows]
            y_away_ref[rows:, at] = y[3 * rows :].astype(bf16)

    return call(
        kernel,
        [*n3s, *cots, hidden, dgate, dup, w_down],
        [whole((rows, width))] * 8 + [whole((4 * rows, units))] * 3 + [whole(w_down.shape)],
        (
            struct((rows, width), f32),
            struct((rows, width), f32),
            struct((2 * rows, width), bf16),
            struct((width, 2 * units), bf16),
            struct((units, width), bf16),
        ),
        [whole((rows, width))] * 2
        + [whole((2 * rows, width)), whole((width, 2 * units)), whole((units, width))],
        "feed_weight_grads",
        micros=12,
        after=after,
        scratch=[
            pltpu.VMEM((width, 4 * rows), bf16),
            pltpu.VMEM((4 * rows, width), bf16),
            pltpu.VMEM((units, 4 * rows), bf16),
        ],
    )


def cross_enter(links, x2, gain_feed, dn3, dn3_core, dn3_hi, cotangent, o2, out_blocks, after):
    rows, width = x2.shape
    n = out_blocks.count
    split = (2, width // 4, width)

    def kernel(spot, x2_ref, g_ref, dn_ref, dn_core_ref, dn_hi_ref, cot_ref, o2_ref, *refs):
        dx_ref, do_ref, keep_ref, away_ref, gg_ref, w_ref, o2t_ref = refs[n:]
        out_blocks.put(spot, refs[:n], w_ref)
        dn = dn_ref[...] + dn_core_ref[...].astype(f32) + dn_hi_ref[...].astype(f32)
        grad_rows, grad_gain = norm_back(dn, x2_ref[...], g_ref[...])
        gg_ref[...] = grad_gain
        dx2 = cot_ref[...].astype(f32) + grad_rows
        dx_ref[...] = dx2
        da = dx2.astype(bf16)
        do_ref[...] = dot(da, w_ref[...], 1, 1).astype(bf16)
        o2t_ref[...] = o2_ref[...].T
        split_rows(o2t_ref, da, spot[1], keep_ref, away_ref)

    return call(
        kernel,
        [links.spot, x2, gain_feed, dn3, dn3_core, dn3_hi, cotangent, o2] + out_blocks.arrays,
        [smem(), whole((rows, width)), whole((1, width))]
        + [whole((rows, width))] * 5
        + out_blocks.specs(width, 4),
        (
            struct((rows, width), f32),
            struct((rows, width), bf16),
            struct(split, bf16),
            struct(split, bf16),
            struct((1, width), f32),
        ),
        [whole((rows, width))] * 2 + [whole(split)] * 2 + [whole((1, width))],
        "cross_enter",
        micros=6,
        after=after,
        scratch=[pltpu.VMEM((width, width), bf16), pltpu.VMEM((width, rows), bf16)],
    )


def cross_backward(q2, do2, o2, keyval, probs, after):
    rows, width = q2.shape
    seqs, cols, count = keyval.shape
    length = rows // seqs
    chunk = 512

    def kernel(q_ref, do_ref, o_ref, kv_ref, p_ref, dq_ref, dkv_ref):
        q, do = q_ref[...], do_ref[...]
        low, high = heads_low(q), heads_high(do)
        low_t, high_t = low.T, high.T
        product = do.astype(f32) * o_ref[...].astype(f32)
        keep = low_lanes(product.shape)
        inner = jnp.concatenate(
            [
                jnp.sum(jnp.where(keep, product, 0.0), axis=-1, keepdims=True),
                jnp.sum(jnp.where(keep, 0.0, product), axis=-1, keepdims=True),
            ],
            axis=0,
        )
        dq = jnp.zeros((2 * length, PAIR), f32)
        for c in range(count // chunk):
            cut = slice(c * chunk, (c + 1) * chunk)
            kv = kv_ref[0, :, cut]
            p = p_ref[0, :, cut]
            dp = dot(high, kv)
            ds = (p.astype(f32) * (dp - inner)).astype(bf16)
            dq += dot(ds, kv, 1, 1)
            dkv_ref[0, :, cut] = (dot(low_t, ds) + dot(high_t, p)).astype(bf16)
        dq_ref[...] = merge_low(dq).astype(bf16)

    heads_block = pl.BlockSpec((length, PAIR), lambda b, g: (b, g))
    kv_block = pl.BlockSpec((1, PAIR, count), lambda b, g: (b, g, 0))
    return call(
        kernel,
        [q2, do2, o2, keyval, probs],
        [
            heads_block,
            heads_block,
            heads_block,
            kv_block,
            pl.BlockSpec((1, 2 * length, count), lambda b, g: (b * KVH + g, 0, 0)),
        ],
        (struct((rows, width), bf16), struct((seqs, cols, count), bf16)),
        [heads_block, kv_block],
        "cross_backward",
        micros=25,
        after=after,
        grid=(seqs, KVH),
    )


def keyval_weight_grad(links, memory, grad_keyval, small, after):
    seqs, count, width = memory.shape
    cols = grad_keyval.shape[1]
    tile = 512
    steps = count // tile
    wide = cols + EXTRA
    split = (2, width // 4, wide)

    def kernel(spot, mem_ref, dkv_ref, small_ref, keep_ref, away_ref, acc_ref):
        b, t = pl.program_id(0), pl.program_id(1)

        @pl.when((b == 0) & (t == 0))
        def _():
            acc_ref[...] = jnp.zeros_like(acc_ref)
            acc_ref[cols : cols + 8] = small_ref[...]

        acc_ref[:cols] += dot(dkv_ref[0], mem_ref[0])

        @pl.when((b == seqs - 1) & (t == steps - 1))
        def _():
            half = split[1]
            for hi in range(2):
                for out, at in ((keep_ref, spot[1]), (away_ref, 1 - spot[1])):
                    lanes = pl.ds(pl.multiple_of((hi * 2 + at) * half, half), half)
                    for side in range(2):
                        for g in range(0, KVH, 2):
                            pair = [
                                acc_ref[(g + i) * PAIR + side * HD : (g + i) * PAIR + (side + 1) * HD, lanes]
                                for i in range(2)
                            ]
                            left = side * cols // 2 + g * HD
                            out[hi, :, left : left + PAIR] = jnp.concatenate(pair, axis=0).T.astype(bf16)
                    out[hi, :, cols:] = acc_ref[cols:, lanes].T.astype(bf16)

    return call(
        kernel,
        [links.spot, memory, grad_keyval, small],
        [
            smem(),
            pl.BlockSpec((1, tile, width), lambda b, t: (b, t, 0)),
            pl.BlockSpec((1, cols, tile), lambda b, t: (b, 0, t)),
            whole((8, width)),
        ],
        (struct(split, bf16), struct(split, bf16)),
        [whole(split)] * 2,
        "keyval_weight_grad",
        micros=15,
        after=after,
        grid=(seqs, steps),
        scratch=[pltpu.VMEM((wide, width), f32)],
    )


def memory_gradient(links, grad_keyval, blocks, after):
    seqs, cols, count = grad_keyval.shape
    width = cols
    tile = 512
    n = blocks.count

    def kernel(spot, dkv_ref, *refs):
        out_ref, w_ref = refs[n:]

        @pl.when((pl.program_id(0) == 0) & (pl.program_id(1) == 0))
        def _():
            blocks.put(spot, refs[:n], w_ref)

        out_ref[0] = dot(dkv_ref[0].T, w_ref[...], 1, 1).astype(bf16)

    return call(
        kernel,
        [links.spot, grad_keyval] + blocks.arrays,
        [smem(), pl.BlockSpec((1, cols, tile), lambda b, t: (b, 0, t))] + blocks.specs(cols, 0),
        struct((seqs, count, width), bf16),
        pl.BlockSpec((1, tile, width), lambda b, t: (b, t, 0)),
        "memory_gradient",
        micros=15,
        after=after,
        grid=(seqs, count // tile),
        scratch=[pltpu.VMEM((width, cols), bf16)],
    )


def causal_enter(links, dx2, x1, gain_cross, n2, dq2, o1, blocks, after):
    rows, width = x1.shape
    n, m = blocks.count, 2 * blocks.count
    split = (2, width // 4, 2 * width)

    def kernel(spot, dx2_ref, x1_ref, g_ref, n2_ref, dq2_ref, o1_ref, *refs):
        dx_ref, do_ref, keep_ref, away_ref, gg_ref, wo_ref, wq_ref, o1t_ref, n2t_ref = refs[m:]
        blocks.put(spot, refs[:n], wo_ref)
        blocks.put(spot, refs[n:m], wq_ref)
        dq2 = dq2_ref[...]
        grad_rows, grad_gain = norm_back(dot(dq2, wq_ref[...], 1, 1), x1_ref[...], g_ref[...])
        gg_ref[...] = grad_gain
        dx1 = dx2_ref[...] + grad_rows
        dx_ref[...] = dx1
        da = dx1.astype(bf16)
        do_ref[...] = dot(da, wo_ref[...], 1, 1).astype(bf16)
        o1t_ref[...] = o1_ref[...].T
        split_rows(o1t_ref, da, spot[1], keep_ref.at[:, :, :width], away_ref.at[:, :, :width])
        n2t_ref[...] = n2_ref[...].T
        split_rows(n2t_ref, dq2, spot[1], keep_ref.at[:, :, width:], away_ref.at[:, :, width:])

    return call(
        kernel,
        [links.spot, dx2, x1, gain_cross, n2, dq2, o1] + blocks.arrays * 2,
        [smem(), whole((rows, width)), whole((rows, width)), whole((1, width))]
        + [whole((rows, width))] * 3
        + blocks.specs(width, 2)
        + blocks.specs(width, 3),
        (
            struct((rows, width), f32),
            struct((rows, width), bf16),
            struct(split, bf16),
            struct(split, bf16),
            struct((1, width), f32),
        ),
        [whole((rows, width))] * 2 + [whole(split)] * 2 + [whole((1, width))],
        "causal_enter",
        micros=8,
        after=after,
        scratch=[
            pltpu.VMEM((width, width), bf16),
            pltpu.VMEM((width, width), bf16),
            pltpu.VMEM((width, rows), bf16),
            pltpu.VMEM((width, rows), bf16),
        ],
    )


def causal_backward(links, lengths, dx1, do1, qkv1, n1, x, gain_causal, table, blocks, after):
    rows, width = n1.shape
    cols = qkv1.shape[1]
    seqs = lengths.shape[0]
    length = rows // seqs
    n = blocks.count
    split = (2, width // 4, cols)

    def kernel(spot, len_ref, dx1_ref, do_ref, qkv_ref, n1_ref, x_ref, g1_ref, tab_ref, *refs):
        keep_ref, away_ref, gg1_ref, bias_ref, dx_ref, w_ref, dqkv_ref, n1t_ref = refs[n:]
        blocks.put(spot, refs[:n], w_ref)
        tab = tab_ref[...]
        i = lax.broadcasted_iota(jnp.int32, (length, length), 0)
        j = lax.broadcasted_iota(jnp.int32, (length, length), 1)
        flip = jnp.where(i + j == length - 1, 1.0, 0.0).astype(bf16)
        for g in range(KVH):
            lanes = slice(g * PAIR, (g + 1) * PAIR)
            kv_lanes = slice(width + g * PAIR, width + (g + 1) * PAIR)
            even_sum = jnp.zeros((length, length), f32)
            odd_sum = jnp.zeros((length, length), f32)
            for b in range(seqs):
                part = slice(b * length, (b + 1) * length)
                keyval = qkv_ref[part, kv_lanes]
                low = heads_low(qkv_ref[part, lanes])
                high = heads_high(do_ref[part, lanes])
                p = causal_probs(low, keyval, tab, g, length, len_ref[b])
                dp = dot(high, keyval, 1, 1)
                ds = (p * (dp - jnp.sum(p * dp, axis=-1, keepdims=True))).astype(bf16)
                even_sum += dot(flip, ds[:length])
                odd_sum += dot(flip, ds[length:])
                dqkv_ref[part, lanes] = merge_low(dot(ds, keyval)).astype(bf16)
                dqkv_ref[part, kv_lanes] = (
                    dot(ds.T, low) + dot(p.astype(bf16).T, high)
                ).astype(bf16)
            bias_ref[2 * g : 2 * g + 1] = diagonal_sums(even_sum)
            bias_ref[2 * g + 1 : 2 * g + 2] = diagonal_sums(odd_sum)
        dqkv = dqkv_ref[...]
        n1t_ref[...] = n1_ref[...].T
        grad_rows, grad_gain = norm_back(
            dot(dqkv, w_ref[...], 1, 1), x_ref[...].astype(f32), g1_ref[...]
        )
        split_rows(n1t_ref, dqkv[:, :width], spot[1], keep_ref.at[:, :, :width], away_ref.at[:, :, :width])
        keep_low = low_lanes((rows, PAIR))
        apart = [[], []]
        for g in range(0, KVH, 2):
            one, two = (dqkv[:, width + i * PAIR : width + (i + 1) * PAIR] for i in (g, g + 1))
            apart[0].append(jnp.where(keep_low, one, swap_halves(two)))
            apart[1].append(jnp.where(keep_low, swap_halves(one), two))
        dkv = jnp.concatenate(apart[0] + apart[1], axis=1)
        split_rows(n1t_ref, dkv, spot[1], keep_ref.at[:, :, width:], away_ref.at[:, :, width:])
        gg1_ref[...] = grad_gain
        dx_ref[...] = (dx1_ref[...] + grad_rows).astype(bf16)

    return call(
        kernel,
        [links.spot, lengths, dx1, do1, qkv1, n1, x, gain_causal, table] + blocks.arrays,
        [smem(), smem(), whole((rows, width)), whole((rows, width)), whole((rows, cols))]
        + [whole((rows, width))] * 2
        + [whole((1, width)), whole(table.shape)]
        + blocks.specs(cols, 0),
        (
            struct(split, bf16),
            struct(split, bf16),
            struct((1, width), f32),
            struct((HEADS, bucket_reach), f32),
            struct((rows, width), bf16),
        ),
        [whole(split)] * 2 + [whole((1, width)), whole((HEADS, bucket_reach)), whole((rows, width))],
        "causal_backward",
        micros=15,
        after=after,
        scratch=[
            pltpu.VMEM((width, cols), bf16),
            pltpu.VMEM((rows, cols), bf16),
            pltpu.VMEM((width, rows), bf16),
        ],
    )


def interleave(w_key, w_value):
    r = w_key.shape[0]
    return jnp.concatenate(
        [w_key.reshape(r, KVH, HD), w_value.reshape(r, KVH, HD)], axis=2
    ).reshape(r, KVH * PAIR)


EXTRA = 128


def local(
    links,
    inputs,
    memory,
    lengths,
    cotangent,
    causal_query,
    causal_key,
    causal_value,
    causal_out,
    cross_query,
    cross_key,
    cross_value,
    cross_out,
    feed_gate,
    feed_up,
    feed_down,
    gain_causal,
    gain_cross,
    gain_feed,
    bias_table,
):
    links.locate()
    seqs, length, width = inputs.shape
    rows = seqs * length
    r = causal_query.shape[0]
    devices = links.nf * links.nd
    table_part = bias_table.shape[0]
    x = inputs.reshape(rows, width)
    cot = cotangent.reshape(rows, width)

    small = jnp.concatenate(
        [
            gain_causal[:, None],
            gain_cross[:, None],
            gain_feed[:, None],
            jnp.pad(bias_table[:, None], ((0, r - table_part), (0, 0))),
            jnp.zeros((r, EXTRA - 4), bf16),
        ],
        axis=1,
    )
    first_shard = jnp.concatenate([interleave(cross_key, cross_value), small], axis=1)
    causal_shard = jnp.concatenate(
        [causal_query, interleave(causal_key, causal_value), causal_out], axis=1
    )
    second_shard = jnp.concatenate([causal_shard, cross_query, cross_out], axis=1)
    units = feed_gate.shape[1] // links.nf
    feed_wide = jnp.stack(
        [
            jnp.concatenate([w[:, f * units : (f + 1) * units] for w in (feed_gate, feed_up)], axis=1)
            for f in range(links.nf)
        ]
    )

    bits = links.bits
    near = [frozenset()]
    lo_hi, hi_lo = ("lo", "hi"), ("hi", "lo")

    first_ring = links.grow((first_shard[None], near), bits)
    first_lo = links.grow(first_ring, ("lo",))
    second_one = links.grow((second_shard[None], near), bits[:1], first_ring[0])
    first_near = links.grow(first_lo, ("hi",))
    cot_core = links.send(cot, "core", first_lo[0])
    cot_hi = links.send(cot, "hi", first_lo[0])
    first_far = links.send(first_near[0], "core"), [f | {"core"} for f in first_near[1]]
    first_blocks = Blocks(links, first_near, first_far)
    second_ring = links.grow(second_one, bits[1:], first_near[0])
    feed_near = links.quarters(feed_wide, first_near[0], cot_core, cot_hi)

    stack, fars = second_ring
    half = stack.shape[2] // 2
    left_one = links.grow((stack[..., :half], fars), ("lo",))
    right_one = links.grow((stack[..., half:], fars), ("hi",))
    keyval, small_all = project_memory(
        links, tie(memory, stack, first_far[0], feed_near), first_blocks
    )
    down_one = links.grow((feed_down[None], near), bits[:1], stack, feed_near, then=(keyval,))
    feed_one = links.grow((feed_near[None], near), bits[:1], stack, then=(keyval,))
    left_two = links.send(left_one[0], "hi", keyval, down_one[0], feed_one[0])
    right_two = links.send(right_one[0], "lo", keyval, down_one[0], feed_one[0])
    down_ring = links.grow(down_one, bits[1:], keyval)
    feed_ring = links.grow(feed_one, bits[1:], keyval)
    n = len(fars)
    second_near = jnp.concatenate(
        [
            jnp.concatenate([left_one[0], left_two], axis=0),
            jnp.concatenate(
                [right_one[0][:n], right_two[:n], right_one[0][n:], right_two[n:]], axis=0
            ),
        ],
        axis=2,
    )
    second_near = tie(second_near, down_ring[0], feed_ring[0])
    cot_both = links.send(cot_hi, "core", second_near)
    second_fars = left_one[1] + [f | {"hi"} for f in left_one[1]]
    second_far = links.send(second_near, "core"), [f | {"core"} for f in second_fars]
    second_blocks = Blocks(links, (second_near, second_fars), second_far)
    down_far = links.send(down_ring[0], "lo", right_two), [f | {"lo"} for f in down_ring[1]]
    cots = (cot, cot_core, cot_hi, cot_both)

    gain_one, gain_two, gain_three = (small_all[i : i + 1] for i in range(3))
    bias_all = small_all[3].reshape(devices, r)[:, :table_part].reshape(HEADS, BUCKETS)
    onehot = jnp.asarray(reversed_buckets())
    table = jnp.dot(bias_all.astype(bf16), onehot.astype(bf16), preferred_element_type=f32)

    x1, n1, qkv1, o1 = causal_forward(
        links, inputs, second_blocks, gain_one, table, lengths, (keyval, feed_ring[0], down_ring[0])
    )
    w_down = assemble(links, (down_ring, down_far), (x1,))
    feed_far = links.send(feed_ring[0], "lo", x1), [f | {"lo"} for f in feed_ring[1]]
    feed_blocks = Blocks(links, feed_ring, feed_far, quads=True)
    n2, q2, o2, x2, n3, probs = cross_forward(
        links, x1, keyval, second_blocks, gain_two, gain_three, (w_down,)
    )
    n3_hi = links.send(n3, "hi")
    n3_core = links.send(n3, "core")
    n3_both = links.send(n3_hi, "core")
    n3s = (n3, n3_core, n3_hi, n3_both)
    hidden, dgate, dup, dn3, dn3_hi, dn3_away = feed_through(
        links, n3s, cots, feed_blocks, w_down, ()
    )

    dn3_got = links.send(dn3_away, "core")
    dn3_passed = (dn3_hi + dn3_got[rows:].astype(f32)).astype(bf16)
    dn3_terms = (dn3, dn3_got[:rows], links.send(dn3_passed, "hi"))
    y, y_hi, y_away, grad_gu, grad_down = feed_weight_grads(
        n3s, cots, hidden, dgate, dup, w_down, (dn3_passed,)
    )

    def split(a, axes):
        return a.reshape((2,) * len(axes) + (-1, a.shape[-1]))

    dp_axes = bits + ("lo",)
    apart = ("hi",) + dp_axes
    back = tuple(reversed(bits))

    def halves(keep, away, ways, *windows):
        got = split(links.send(away, "core"), apart)
        keep = split(keep, apart)
        return [
            Sum([Leaf(keep, apart, left, width), Leaf(got, apart, left, width)], ways + back)
            for left, width in windows
        ]

    gu_axes = ("hi", "core") + dp_axes
    feed_sums = [
        Sum([Leaf(split(grad_gu, gu_axes), gu_axes)], ("lo",) + back),
        Sum([Leaf(split(grad_down, dp_axes), dp_axes)], ("lo",) + back),
    ]
    done = advance(links, feed_sums, (y,))
    dx2, do2, keep, away, grad_gain_three = cross_enter(
        links, x2, gain_three, *dn3_terms, cot, o2, second_blocks, done
    )
    early_sums = halves(keep, away, hi_lo, (0, width))
    y_got = links.send(y_away, "core", dx2)
    dq2, grad_keyval = cross_backward(q2, do2, o2, keyval, probs, (dx2,))
    dx1, do1, keep, away, grad_gain_two = causal_enter(
        links, dx2, x1, gain_two, n2, dq2, o1, second_blocks, ()
    )
    early_sums += halves(keep, away, lo_hi, (0, 2 * width))
    y_passed = (tie(y_hi, dx1) + y_got[rows:].astype(f32)).astype(bf16)
    y_terms = (y, y_got[:rows], links.send(y_passed, "hi"))
    keep, away, grad_gain_one, grad_bias, input_grad = causal_backward(
        links, lengths, dx1, do1, qkv1, n1, x, gain_one, table, second_blocks, ()
    )
    middle_sums = halves(keep, away, lo_hi, (0, width))
    middle_sums += [
        Sum([Leaf(leaf.array, leaf.axes, width, width) for leaf in middle_sums[0].leaves], hi_lo + back)
    ]
    done = advance(links, feed_sums, (input_grad,))
    done = advance(links, early_sums, done)

    grad_table = lax.dot_general(
        grad_bias, onehot, (((1,), (1,)), ((), ())), precision=lax.Precision.HIGHEST
    )
    table_rows = jnp.pad(
        grad_table.reshape(devices, table_part), ((0, 0), (0, r - table_part))
    ).reshape(1, width)
    small_rows = jnp.concatenate(
        [grad_gain_one, grad_gain_two, grad_gain_three, table_rows, jnp.zeros((4, width), f32)],
        axis=0,
    )
    keep, away = keyval_weight_grad(links, memory, grad_keyval, small_rows, done)
    late_sums = halves(keep, away, hi_lo, (0, KVH * PAIR + EXTRA))
    done = advance(links, early_sums + middle_sums, (keep,))
    memory_grad = memory_gradient(links, grad_keyval, first_blocks, done)
    done = advance(links, early_sums + middle_sums + late_sums, (memory_grad,))
    done = advance(links, feed_sums + early_sums + middle_sums + late_sums, done)
    done = advance(links, middle_sums + late_sums, done)
    half = width // 2
    while feed_sums[0].ways:
        done = advance(links, feed_sums, done)
    sum_gu, sum_down = finish(links, feed_sums, [(2 * units,), (width,)], done)
    done = (sum_down,)
    while late_sums[0].ways:
        done = advance(links, [one for one in early_sums + middle_sums + late_sums if one.ways], done)
    wide = links.unquarter(sum_gu, done)
    sum_o2, sum_o1, sum_q2, sum_q1, sum_k1, sum_v1 = finish(
        links, early_sums + middle_sums, [(width,), (width, width), (width,), (half, half)], done
    )
    sum_k2, sum_v2, sum_small = finish(links, late_sums, [(half, half, EXTRA)], (sum_o2,))

    layer_out = (x2 + sum(t.astype(f32) for t in y_terms)).astype(bf16)
    sum_gate, sum_up = (
        jnp.concatenate([part[:, i * units : (i + 1) * units] for part in wide], axis=1)
        for i in range(2)
    )
    return (
        layer_out.reshape(seqs, length, width),
        input_grad.reshape(seqs, length, width),
        memory_grad,
        sum_q1,
        sum_k1,
        sum_v1,
        sum_o1,
        sum_q2,
        sum_k2,
        sum_v2,
        sum_o2,
        sum_gate,
        sum_up,
        sum_down,
        sum_small[:, 0],
        sum_small[:, 1],
        sum_small[:, 2],
        sum_small[:table_part, 3],
    )


def solution(mesh):
    three = P(AXES, None, None)
    two = P(AXES, None)
    one = P(AXES)
    in_specs = (three, three, one, three) + (two,) * 11 + (one,) * 4
    out_specs = (three,) * 3 + (two,) * 11 + (one,) * 4
    body = functools.partial(local, Links(mesh))
    return jax.shard_map(body, mesh=mesh, in_specs=in_specs, out_specs=out_specs, check_vma=False)
```

```python
import functools

import jax
import jax.numpy as jnp
import numpy as np
from jax import lax
from jax.experimental import pallas as pl
from jax.experimental.pallas import tpu as pltpu
from jax.sharding import PartitionSpec as P

HEADS = 16
HD = 64
BUCKETS = 32
KVH = 8
PAIR = 2 * HD
AXES = ("fsdp", "dp")
norm_eps = 1e-06
masked_score = -1000000000.0
bucket_reach = 128
f32 = jnp.float32
bf16 = jnp.bfloat16
VMEM_LIMIT = 56 * 1024 * 1024
PLAN = 2e9
GROUPS = 4


def reversed_buckets():
    distance = (-np.arange(bucket_reach)) % bucket_reach
    exact_count = BUCKETS // 2
    spread = (
        np.log(np.maximum(distance, 1) / exact_count)
        / np.log(bucket_reach / exact_count)
        * (BUCKETS - exact_count)
    )
    far_bucket = np.minimum(exact_count + np.floor(spread).astype(np.int64), BUCKETS - 1)
    bucket_id = np.where(distance < exact_count, distance, far_bucket)
    return (bucket_id[None] == np.arange(BUCKETS)[:, None]).astype(np.float32)


def dot(a, b, ca=1, cb=0):
    return lax.dot_general(a, b, (((ca,), (cb,)), ((), ())), preferred_element_type=f32)


def call(kernel, ins, in_specs, out_shape, out_specs, name, after=(), grid=(1,), scratch=(), prefetch=None, micros=1, aliases=None):
    lead = 0 if prefetch is None else 1
    n = lead + len(ins)

    def body(*refs):
        kernel(*refs[:n], *refs[n + len(after) :])

    spec = pltpu.PrefetchScalarGridSpec(
        num_scalar_prefetch=lead,
        grid=grid,
        in_specs=list(in_specs) + [pl.BlockSpec(memory_space=pl.ANY)] * len(after),
        out_specs=out_specs,
        scratch_shapes=list(scratch),
    )
    front = () if prefetch is None else (prefetch,)
    return pl.pallas_call(
        body,
        grid_spec=spec,
        out_shape=out_shape,
        input_output_aliases=aliases or {},
        compiler_params=pltpu.CompilerParams(vmem_limit_bytes=VMEM_LIMIT),
        cost_estimate=pl.CostEstimate(
            flops=int(micros * PLAN), bytes_accessed=1000, transcendentals=0
        ),
        name=name,
    )(*front, *ins, *after)


def whole(shape):
    return pl.BlockSpec(shape, lambda *_: (0,) * len(shape))


def struct(shape, dtype):
    return jax.ShapeDtypeStruct(shape, dtype)


def smem():
    return pl.BlockSpec(memory_space=pltpu.SMEM)


class Links:
    def __init__(self, mesh):
        nf, nd = mesh.shape["fsdp"], mesh.shape["dp"]
        self.nf, self.nd, self.size = nf, nd, nd // 2
        self.bits = tuple(f"z{b}" for b in reversed(range(self.size.bit_length() - 1)))
        self.names = ("hi", "core", "ring", "lo") + self.bits
        spots = [(f, d) for f in range(nf) for d in range(nd)]

        def pairs(flip_f, flip_d):
            return [(f * nd + d, (f ^ flip_f) * nd + (d ^ flip_d)) for f, d in spots]

        self.pairs = {"core": pairs(1, 0), "hi": pairs(2, 0), "both": pairs(3, 0), "lo": pairs(0, 1)}
        self.masks = {}
        for name in self.bits:
            self.masks[name] = 1 << int(name[1:])
            self.pairs[name] = pairs(0, 2 << int(name[1:]))

    def locate(self):
        f, d = lax.axis_index("fsdp"), lax.axis_index("dp")
        self.hi, self.core, self.ring, self.lo = f // 2, f % 2, d // 2, d % 2
        zs = [(self.ring // self.masks[name]) % 2 for name in self.bits]
        self.spot = jnp.stack([self.hi, self.core, self.ring, self.lo, *zs]).astype(jnp.int32)

    def send(self, a, way, *after):
        return lax.ppermute(tie(a, *after), AXES, self.pairs[way])

    def grow(self, held, ways, *after, then=()):
        array, fars = held
        for way in ways:
            got = self.send(array, way, *after)
            after = ()
            array = jnp.concatenate([tie(array, *then), got], axis=0)
            fars = fars + [f | {way} for f in fars]
        return array, fars

    def quarters(self, wide, *after):
        mine = self.hi * 2 + self.core
        out = [lax.dynamic_index_in_dim(wide, mine, 0, keepdims=False)]
        for flip, way in ((1, "core"), (2, "hi"), (3, "both")):
            theirs = lax.dynamic_index_in_dim(wide, mine ^ flip, 0, keepdims=False)
            out.append(self.send(theirs, way, *after))
        return jnp.concatenate(out, axis=0)

    def unquarter(self, wide, after):
        _, _, r, c = wide.shape
        wide = wide.reshape(self.nf, r, c)
        mine = self.hi * 2 + self.core
        near = [tie(lax.dynamic_index_in_dim(wide, mine, 0, keepdims=False), *after)]
        for flip, way in ((1, "core"), (2, "hi"), (3, "both")):
            theirs = lax.dynamic_index_in_dim(wide, mine ^ flip, 0, keepdims=False).astype(bf16)
            near.append(tie(self.send(theirs, way), *after).astype(f32))
        near = jnp.stack(near)
        return [lax.dynamic_index_in_dim(near, mine ^ f, 0, keepdims=False) for f in range(self.nf)]


class Blocks:
    def __init__(self, links, *helds, quads=False):
        self.links = links
        self.arrays = [a for a, _ in helds]
        self.fars = [f for _, f in helds]
        self.quads = quads
        _, self.r, self.c = self.arrays[0].shape
        self.count = len(helds)

    def specs(self, width=None, index=0):
        return [
            pl.BlockSpec((*a.shape[:2], width or self.c), lambda *_: (0, 0, index))
            for a in self.arrays
        ]

    def put(self, spot, refs, *outs):
        quads = [(0, 0), (0, 1), (1, 0), (1, 1)] if self.quads else [None]
        r = self.r // len(quads)
        for ref, fars in zip(refs, self.fars):
            for i, far in enumerate(fars):
                for q, quad in enumerate(quads):
                    far_hi, far_core = quad or ("hi" in far, "core" in far)
                    at_hi = 1 - spot[0] if far_hi else spot[0]
                    at_core = 1 - spot[1] if far_core else spot[1]
                    row = ((at_hi * 2 + at_core) * self.links.nd + place_of(self.links, spot, far)) * r
                    rows = pl.ds(pl.multiple_of(row, r), r)
                    left = 0
                    for out in outs:
                        width = out.shape[-1]
                        out[rows, :] = ref[i, q * r : (q + 1) * r, left : left + width]
                        left += width


def place_of(links, spot, far):
    mask = sum(links.masks[name] for name in links.bits if name in far)
    at_ring = jnp.bitwise_xor(spot[2], mask) if mask else spot[2]
    at_lo = 1 - spot[3] if "lo" in far else spot[3]
    return at_ring * 2 + at_lo


def tie(x, *after):
    return lax.optimization_barrier((x, *after))[0] if after else x


def assemble(links, helds, after=()):
    _, r, c = helds[0][0].shape
    n = len(helds)
    most = max(len(f) for _, f in helds)

    def kernel(spot, *refs):
        out, held, sems_in, sems_out = refs[n:]
        copies = []
        for k, (ref, (_, fars)) in enumerate(zip(refs, helds)):
            for i, far in enumerate(fars):
                copies.append(
                    (
                        pltpu.make_async_copy(ref.at[i], held.at[k, i], sems_in.at[k, i]),
                        pltpu.make_async_copy(
                            held.at[k, i], out.at[place_of(links, spot, far)], sems_out.at[k, i]
                        ),
                    )
                )
        for one, _ in copies:
            one.start()
        for one, two in copies:
            one.wait()
            two.start()
        for _, two in copies:
            two.wait()

    out = call(
        kernel,
        [links.spot] + [a for a, _ in helds],
        [smem()] + [pl.BlockSpec(memory_space=pl.ANY)] * n,
        struct((links.nd, r, c), bf16),
        pl.BlockSpec(memory_space=pl.ANY),
        "assemble",
        micros=3,
        after=after,
        scratch=[
            pltpu.VMEM((n, most, r, c), bf16),
            pltpu.SemaphoreType.DMA((n, most)),
            pltpu.SemaphoreType.DMA((n, most)),
        ],
    )
    return out.reshape(-1, c)


class Leaf:
    def __init__(self, array, axes, left=0, width=None, held=()):
        self.array, self.axes, self.left, self.held = array, axes, left, dict(held)
        self.width = width or array.shape[-1]

    def hold(self, way, far):
        held = dict(self.held)
        if way in self.axes:
            held[way] = far
        return Leaf(self.array, self.axes, self.left, self.width, held)

    def free(self):
        return tuple(a for a in self.axes if a not in self.held)

    def spec(self, links):
        shape = tuple(None if a in self.held else 2 for a in self.axes) + self.array.shape[-2:]
        picks = [(self.held.get(a), links.names.index(a)) for a in self.axes]

        def index(_, spot):
            return (
                *(0 if far is None else 1 - spot[i] if far else spot[i] for far, i in picks),
                0,
                0,
            )

        return pl.BlockSpec(shape, index)


class Sum:
    def __init__(self, leaves, ways):
        self.leaves, self.ways = leaves, list(ways)


def gather_terms(links, leaves_of):
    ins = [leaf.array for leaves in leaves_of for leaf in leaves]
    specs = [leaf.spec(links) for leaves in leaves_of for leaf in leaves]

    def totals(refs):
        n = 0
        for leaves in leaves_of:
            total = None
            for leaf in leaves:
                term = refs[n][..., leaf.left : leaf.left + leaf.width].astype(f32)
                total = term if total is None else total + term
                n += 1
            yield total

    return ins, specs, totals


def advance(links, sums, after=()):
    moves = []
    for one in sums:
        way = one.ways.pop(0)
        moves.append((way, [leaf.hold(way, True) for leaf in one.leaves]))
        one.leaves = [leaf.hold(way, False) for leaf in one.leaves]
    groups, where = {}, []
    for way, leaves in moves:
        free = leaves[0].free()
        key = (way, free, leaves[0].array.shape[-2])
        left = groups.get(key, 0)
        groups[key] = left + leaves[0].width
        where.append((key, left, leaves[0].width))
    keys = list(groups)
    outs = [struct((2,) * len(free) + (r, groups[way, free, r]), bf16) for way, free, r in keys]
    ins, specs, totals = gather_terms(links, [leaves for _, leaves in moves])

    def kernel(spot, *refs):
        for total, (key, left, width) in zip(totals(refs), where):
            refs[len(ins) + keys.index(key)][..., left : left + width] = total.astype(bf16)

    sent = call(
        kernel, ins, specs, outs, [whole(o.shape) for o in outs], "combine", micros=3, after=after, prefetch=links.spot
    )
    got = {key: links.send(a, key[0]) for key, a in zip(keys, sent)}
    for one, (key, left, width) in zip(sums, where):
        one.leaves.append(Leaf(got[key], key[1], left, width))
    return (sent[0],)


def finish(links, sums, cuts, after=()):
    ins, specs, totals = gather_terms(links, [one.leaves for one in sums])
    outs = [
        struct((2,) * len(one.leaves[0].free()) + (one.leaves[0].array.shape[-2], width), f32)
        for one, widths in zip(sums, cuts)
        for width in widths
    ]

    def kernel(spot, *refs):
        n = len(ins)
        for total, widths in zip(totals(refs), cuts):
            left = 0
            for width in widths:
                refs[n][...] = total[..., left : left + width]
                left += width
                n += 1

    return call(
        kernel, ins, specs, outs, [whole(o.shape) for o in outs], "finish", micros=3, after=after, prefetch=links.spot
    )


def norm_scale(rows):
    return lax.rsqrt(jnp.mean(rows * rows, axis=-1, keepdims=True) + norm_eps)


def norm_back(grad_normed, rows, gain):
    scale = norm_scale(rows)
    scaled = grad_normed * gain
    inner_mean = jnp.mean(scaled * rows, axis=-1, keepdims=True)
    grad_rows = scale * scaled - rows * (scale * scale * scale) * inner_mean
    return grad_rows, jnp.sum(grad_normed * rows * scale, axis=0, keepdims=True)


def swap_halves(block):
    return pltpu.roll(block.astype(f32), HD, 1).astype(bf16)


def low_lanes(shape):
    return lax.broadcasted_iota(jnp.int32, shape, 1) < HD


def heads_low(block):
    keep = low_lanes(block.shape)
    zero = jnp.zeros_like(block)
    return jnp.concatenate(
        [jnp.where(keep, block, zero), jnp.where(keep, swap_halves(block), zero)], axis=0
    )


def heads_high(block):
    keep = low_lanes(block.shape)
    zero = jnp.zeros_like(block)
    return jnp.concatenate(
        [jnp.where(keep, zero, swap_halves(block)), jnp.where(keep, zero, block)], axis=0
    )


def merge_low(both):
    half = both.shape[0] // 2
    even, odd = both[:half], both[half:]
    return jnp.where(low_lanes(even.shape), even, pltpu.roll(odd, HD, 1))


def merge_high(both):
    half = both.shape[0] // 2
    even, odd = both[:half], both[half:]
    return jnp.where(low_lanes(even.shape), pltpu.roll(even, HD, 1), odd)


def toeplitz(row, length):
    return pltpu.roll(jnp.broadcast_to(row, (length, length)), 0, 1, stride=1, stride_axis=0)


def diagonal_sums(flipped):
    turned = pltpu.roll(flipped, 1, 1, stride=1, stride_axis=0)
    return jnp.sum(turned, axis=0, keepdims=True)


def batches(seqs):
    return [[(b, g) for g in range(k, k + 4) for b in range(seqs)] for k in range(0, KVH, 4)]


def rows_of(b, length):
    return slice(b * length, (b + 1) * length)


def lanes_of(g, left=0):
    return slice(left + g * PAIR, left + (g + 1) * PAIR)


def causal_probs(s, table, g, length, valid_len):
    bias = jnp.concatenate(
        [toeplitz(table[2 * g : 2 * g + 1], length), toeplitz(table[2 * g + 1 : 2 * g + 2], length)],
        axis=0,
    )
    i = lax.broadcasted_iota(jnp.int32, (length, length), 0)
    j = lax.broadcasted_iota(jnp.int32, (length, length), 1)
    valid = (j <= i) & (j < valid_len)
    valid = jnp.concatenate([valid, valid], axis=0)
    s = jnp.where(valid, s + bias, masked_score)
    e = jnp.exp(s - jnp.max(s, axis=-1, keepdims=True))
    return e / jnp.sum(e, axis=-1, keepdims=True)


def split_rows(lhs_t, rhs, core, keep, away):
    half = keep.shape[1]
    for hi in range(keep.shape[0]):
        for out, at in ((keep, core), (away, 1 - core)):
            row = pl.multiple_of((hi * 2 + at) * half, half)
            out[hi] = dot(lhs_t[pl.ds(row, half), :], rhs).astype(bf16)


def project_memory(links, memory, blocks):
    seqs, count, width = memory.shape
    cols = KVH * PAIR
    tile = 1024
    n = blocks.count

    def kernel(spot, mem_ref, *refs):
        held = refs[:n]
        out_ref, small_ref, w_ref, wt_ref = refs[n:]

        @pl.when((pl.program_id(0) == 0) & (pl.program_id(1) == 0))
        def _():
            blocks.put(spot, held, w_ref)
            wt_ref[...] = w_ref[:, :cols].T
            small_ref[...] = w_ref[:, cols:].astype(f32).T[:8]

        out_ref[0] = dot(wt_ref[...], mem_ref[0], 1, 1).astype(bf16)

    return call(
        kernel,
        [links.spot, memory] + blocks.arrays,
        [smem(), pl.BlockSpec((1, tile, width), lambda b, t: (b, t, 0))] + blocks.specs(),
        (struct((seqs, cols, count), bf16), struct((8, width), f32)),
        [pl.BlockSpec((1, cols, tile), lambda b, t: (b, 0, t)), whole((8, width))],
        "project_memory",
        micros=15,
        grid=(seqs, count // tile),
        scratch=[pltpu.VMEM((width, blocks.c), bf16), pltpu.VMEM((cols, width), bf16)],
    )


def causal_forward(links, x, blocks, gain, table, lengths, after):
    seqs, length, width = x.shape
    rows = seqs * length
    cols = 2 * width
    n = blocks.count

    def kernel(spot, len_ref, x_ref, gain_ref, tab_ref, *refs):
        x1_ref, n1_ref, qkv_ref, o1_ref, w_ref, wo_ref = refs[n:]
        blocks.put(spot, refs[:n], w_ref, wo_ref)
        xf = x_ref[...].astype(f32)
        n1 = (xf * norm_scale(xf) * gain_ref[...]).astype(bf16)
        n1_ref[...] = n1
        qkv_ref[...] = dot(n1, w_ref[...]).astype(bf16)
        tab = tab_ref[...]
        for spots in batches(seqs):
            held = [
                (qkv_ref[rows_of(b, length), lanes_of(g)], qkv_ref[rows_of(b, length), lanes_of(g, width)])
                for b, g in spots
            ]
            scores = [dot(heads_low(q), keyval, 1, 1) for q, keyval in held]
            probs = [
                causal_probs(s, tab, g, length, len_ref[b]).astype(bf16)
                for s, (b, g) in zip(scores, spots)
            ]
            for p, (_, keyval), (b, g) in zip(probs, held, spots):
                o1_ref[rows_of(b, length), lanes_of(g)] = merge_high(dot(p, keyval)).astype(bf16)
        x1_ref[...] = xf + dot(o1_ref[...], wo_ref[...])

    return call(
        kernel,
        [links.spot, lengths, x.reshape(rows, width), gain, table] + blocks.arrays,
        [smem(), smem(), whole((rows, width)), whole((1, width)), whole(table.shape)]
        + blocks.specs(cols + width, 0),
        (
            struct((rows, width), f32),
            struct((rows, width), bf16),
            struct((rows, cols), bf16),
            struct((rows, width), bf16),
        ),
        [whole((rows, width)), whole((rows, width)), whole((rows, cols)), whole((rows, width))],
        "causal_forward",
        micros=9,
        after=after,
        scratch=[pltpu.VMEM((width, cols), bf16), pltpu.VMEM((width, width), bf16)],
    )


def cross_forward(links, x1, keyval, blocks, gain_cross, gain_feed, after):
    rows, width = x1.shape
    seqs, _, count = keyval.shape
    length = rows // seqs
    n = blocks.count * 2
    steps = KVH // GROUPS

    def kernel(spot, x1_ref, kv_ref, g2_ref, g3_ref, *refs):
        n2_ref, q2_ref, o2_ref, x2_ref, n3_ref, p_ref, wq_ref, wo_ref = refs[n:]
        b, g = pl.program_id(0), pl.program_id(1)

        @pl.when((b == 0) & (g == 0))
        def _():
            blocks.put(spot, refs[: n // 2], wq_ref)
            blocks.put(spot, refs[n // 2 : n], wo_ref)
            x1v = x1_ref[...]
            n2 = (x1v * norm_scale(x1v) * g2_ref[...]).astype(bf16)
            n2_ref[...] = n2
            q2_ref[...] = dot(n2, wq_ref[...]).astype(bf16)

        part = pl.ds(pl.multiple_of(b * length, length), length)
        lanes = [pl.ds(pl.multiple_of((g * GROUPS + i) * PAIR, PAIR), PAIR) for i in range(GROUPS)]
        scores = [
            dot(heads_low(q2_ref[part, lanes[i]]), kv_ref[0, i * PAIR : (i + 1) * PAIR])
            for i in range(GROUPS)
        ]
        for i, s in enumerate(scores):
            e = jnp.exp(s - jnp.max(s, axis=-1, keepdims=True))
            p_ref[i] = (e * (1.0 / jnp.sum(e, axis=-1, keepdims=True))).astype(bf16)
        for i in range(GROUPS):
            mixed = dot(p_ref[i], kv_ref[0, i * PAIR : (i + 1) * PAIR], 1, 1)
            o2_ref[part, lanes[i]] = merge_high(mixed).astype(bf16)

        @pl.when((b == seqs - 1) & (g == steps - 1))
        def _():
            x2 = x1_ref[...] + dot(o2_ref[...], wo_ref[...])
            x2_ref[...] = x2
            n3_ref[...] = (x2 * norm_scale(x2) * g3_ref[...]).astype(bf16)

    return call(
        kernel,
        [links.spot, x1, keyval, gain_cross, gain_feed] + blocks.arrays * 2,
        [
            smem(),
            whole((rows, width)),
            pl.BlockSpec((1, GROUPS * PAIR, count), lambda b, g: (b, g, 0)),
            whole((1, width)),
            whole((1, width)),
        ]
        + blocks.specs(width, 3)
        + blocks.specs(width, 4),
        (
            struct((rows, width), bf16),
            struct((rows, width), bf16),
            struct((rows, width), bf16),
            struct((rows, width), f32),
            struct((rows, width), bf16),
            struct((seqs * KVH, 2 * length, count), bf16),
        ),
        [whole((rows, width))] * 5
        + [pl.BlockSpec((GROUPS, 2 * length, count), lambda b, g: (b * steps + g, 0, 0))],
        "cross_forward",
        micros=34,
        after=after,
        grid=(seqs, steps),
        scratch=[pltpu.VMEM((width, width), bf16)] * 2,
    )


def stack_rows(refs, out):
    rows = refs[0].shape[0]
    for i, ref in enumerate(refs):
        out[i * rows : (i + 1) * rows] = ref[...]


def feed_prepare(links, cots, blocks, w_down, after):
    rows, width = cots[0].shape
    units = w_down.shape[0]
    n = blocks.count

    def kernel(spot, *refs):
        wd_ref = refs[4]
        wg_ref, wu_ref, dh_ref, cot_all = refs[5 + n :]
        blocks.put(spot, refs[5 : 5 + n], wg_ref, wu_ref)
        stack_rows(refs[:4], cot_all)
        dh_ref[...] = dot(cot_all[...], wd_ref[...], 1, 1)

    return call(
        kernel,
        [links.spot, *cots, w_down] + blocks.arrays,
        [smem()] + [whole((rows, width))] * 4 + [whole(w_down.shape)] + blocks.specs(),
        (
            struct((width, units), bf16),
            struct((width, units), bf16),
            struct((4 * rows, units), f32),
        ),
        [whole((width, units))] * 2 + [whole((4 * rows, units))],
        "feed_prepare",
        micros=6,
        after=after,
        scratch=[pltpu.VMEM((4 * rows, width), bf16)],
    )


def feed_through(n3s, w_gate, w_up, dh, after):
    rows, width = n3s[0].shape
    units = w_gate.shape[1]
    c0 = np.float32(np.sqrt(2.0 / np.pi))
    c1 = np.float32(0.044715)
    cuts = [slice(i, min(i + 256, units)) for i in range(0, units, 256)]

    def kernel(*refs):
        wg_ref, wu_ref, dh_ref = refs[4:7]
        hid_ref, dgate_ref, dup_ref, dn_ref, dn_hi_ref, dn_away_ref, n3_all = refs[7:]
        stack_rows(refs[:4], n3_all)
        for cut in cuts:
            gate = dot(n3_all[...], wg_ref[:, cut])
            up = dot(n3_all[...], wu_ref[:, cut])
            dh = dh_ref[:, cut]
            square = gate * gate
            t = jnp.tanh(c0 * (gate + c1 * (square * gate)))
            cdf = 0.5 * (1.0 + t)
            value = gate * cdf
            slope = cdf + 0.5 * gate * (1.0 - t * t) * (c0 * (1.0 + 3.0 * c1 * square))
            hid_ref[:, cut] = (value * up).astype(bf16)
            dgate_ref[:, cut] = (dh * up * slope).astype(bf16)
            dup_ref[:, cut] = (dh * value).astype(bf16)
        for i in range(0, width, 256):
            at = slice(i, i + 256)
            dn = dot(dgate_ref[...], wg_ref[at, :], 1, 1) + dot(dup_ref[...], wu_ref[at, :], 1, 1)
            dn_ref[:, at] = dn[:rows]
            dn_away_ref[:rows, at] = dn[rows : 2 * rows].astype(bf16)
            dn_hi_ref[:, at] = dn[2 * rows : 3 * rows]
            dn_away_ref[rows:, at] = dn[3 * rows :].astype(bf16)

    return call(
        kernel,
        [*n3s, w_gate, w_up, dh],
        [whole((rows, width))] * 4 + [whole((width, units))] * 2 + [whole((4 * rows, units))],
        (
            struct((4 * rows, units), bf16),
            struct((4 * rows, units), bf16),
            struct((4 * rows, units), bf16),
            struct((rows, width), f32),
            struct((rows, width), f32),
            struct((2 * rows, width), bf16),
        ),
        [whole((4 * rows, units))] * 3 + [whole((rows, width))] * 2 + [whole((2 * rows, width))],
        "feed_through",
        micros=14,
        after=after,
        scratch=[pltpu.VMEM((4 * rows, width), bf16)],
    )


def feed_weight_grads(n3s, cots, hidden, dgate, dup, w_down, after):
    rows, width = n3s[0].shape
    units = hidden.shape[1]
    tile = 256

    def kernel(*refs):
        hid_ref, dgate_ref, dup_ref, wd_ref = refs[8:12]
        y_ref, y_hi_ref, y_away_ref, gu_ref, gd_ref, n3t_ref, cot_all, hid_t = refs[12:]

        @pl.when(pl.program_id(0) == 0)
        def _():
            hid_t[...] = hid_ref[...].T

        for i in range(4):
            n3t_ref[:, i * rows : (i + 1) * rows] = refs[i][...].T
        stack_rows(refs[4:8], cot_all)
        gu_ref[:, :units] = dot(n3t_ref[...], dgate_ref[...]).astype(bf16)
        gu_ref[:, units:] = dot(n3t_ref[...], dup_ref[...]).astype(bf16)
        gd_ref[...] = dot(hid_t[...], cot_all[...]).astype(bf16)
        y = dot(hid_ref[...], wd_ref[...])
        y_ref[...] = y[:rows]
        y_away_ref[:rows] = y[rows : 2 * rows].astype(bf16)
        y_hi_ref[...] = y[2 * rows : 3 * rows]
        y_away_ref[rows:] = y[3 * rows :].astype(bf16)

    def columns(count):
        return pl.BlockSpec((count, tile), lambda t: (0, t))

    return call(
        kernel,
        [*n3s, *cots, hidden, dgate, dup, w_down],
        [columns(rows)] * 8 + [whole((4 * rows, units))] * 3 + [columns(units)],
        (
            struct((rows, width), f32),
            struct((rows, width), f32),
            struct((2 * rows, width), bf16),
            struct((width, 2 * units), bf16),
            struct((units, width), bf16),
        ),
        [columns(rows)] * 2
        + [columns(2 * rows), pl.BlockSpec((tile, 2 * units), lambda t: (t, 0)), columns(units)],
        "feed_weight_grads",
        micros=12,
        after=after,
        grid=(width // tile,),
        scratch=[
            pltpu.VMEM((tile, 4 * rows), bf16),
            pltpu.VMEM((4 * rows, tile), bf16),
            pltpu.VMEM((units, 4 * rows), bf16),
        ],
    )


def cross_enter(links, x2, gain_feed, dn3, dn3_core, dn3_hi, cotangent, o2, out_blocks, after):
    rows, width = x2.shape
    n = out_blocks.count
    split = (2, width // 4, width)

    def kernel(spot, x2_ref, g_ref, dn_ref, dn_core_ref, dn_hi_ref, cot_ref, o2_ref, *refs):
        dx_ref, do_ref, keep_ref, away_ref, gg_ref, w_ref, o2t_ref = refs[n:]
        out_blocks.put(spot, refs[:n], w_ref)
        dn = dn_ref[...] + dn_core_ref[...].astype(f32) + dn_hi_ref[...].astype(f32)
        grad_rows, grad_gain = norm_back(dn, x2_ref[...], g_ref[...])
        gg_ref[...] = grad_gain
        dx2 = cot_ref[...].astype(f32) + grad_rows
        dx_ref[...] = dx2
        da = dx2.astype(bf16)
        do_ref[...] = dot(da, w_ref[...], 1, 1).astype(bf16)
        o2t_ref[...] = o2_ref[...].T
        split_rows(o2t_ref, da, spot[1], keep_ref, away_ref)

    return call(
        kernel,
        [links.spot, x2, gain_feed, dn3, dn3_core, dn3_hi, cotangent, o2] + out_blocks.arrays,
        [smem(), whole((rows, width)), whole((1, width))]
        + [whole((rows, width))] * 5
        + out_blocks.specs(width, 4),
        (
            struct((rows, width), f32),
            struct((rows, width), bf16),
            struct(split, bf16),
            struct(split, bf16),
            struct((1, width), f32),
        ),
        [whole((rows, width))] * 2 + [whole(split)] * 2 + [whole((1, width))],
        "cross_enter",
        micros=6,
        after=after,
        scratch=[pltpu.VMEM((width, width), bf16), pltpu.VMEM((width, rows), bf16)],
    )


def cross_backward(q2, do2, o2, keyval, probs, after):
    rows, width = q2.shape
    seqs, cols, count = keyval.shape
    length = rows // seqs
    steps = KVH // GROUPS

    def kernel(q_ref, do_ref, o_ref, kv_ref, p_ref, dq_ref, dkv_ref):
        for i in range(GROUPS):
            lanes = slice(i * PAIR, (i + 1) * PAIR)
            q, do = q_ref[:, lanes], do_ref[:, lanes]
            low, high = heads_low(q), heads_high(do)
            product = do.astype(f32) * o_ref[:, lanes].astype(f32)
            keep = low_lanes(product.shape)
            inner = jnp.concatenate(
                [
                    jnp.sum(jnp.where(keep, product, 0.0), axis=-1, keepdims=True),
                    jnp.sum(jnp.where(keep, 0.0, product), axis=-1, keepdims=True),
                ],
                axis=0,
            )
            kv = kv_ref[0, lanes]
            p = p_ref[i]
            ds = (p.astype(f32) * (dot(high, kv) - inner)).astype(bf16)
            dq_ref[:, lanes] = merge_low(dot(ds, kv, 1, 1)).astype(bf16)
            dkv_ref[0, lanes] = (dot(low.T, ds) + dot(high.T, p)).astype(bf16)

    heads_block = pl.BlockSpec((length, GROUPS * PAIR), lambda b, g: (b, g))
    kv_block = pl.BlockSpec((1, GROUPS * PAIR, count), lambda b, g: (b, g, 0))
    return call(
        kernel,
        [q2, do2, o2, keyval, probs],
        [
            heads_block,
            heads_block,
            heads_block,
            kv_block,
            pl.BlockSpec((GROUPS, 2 * length, count), lambda b, g: (b * steps + g, 0, 0)),
        ],
        (struct((rows, width), bf16), struct((seqs, cols, count), bf16)),
        [heads_block, kv_block],
        "cross_backward",
        micros=25,
        after=after,
        grid=(seqs, steps),
    )


def keyval_weight_grad(links, memory, grad_keyval, small, after):
    seqs, count, width = memory.shape
    cols = grad_keyval.shape[1]
    tile = 1024
    steps = count // tile
    wide = cols + EXTRA
    split = (2, width // 4, wide)

    def kernel(spot, mem_ref, dkv_ref, small_ref, keep_ref, away_ref, acc_ref):
        b, t = pl.program_id(0), pl.program_id(1)

        @pl.when((b == 0) & (t == 0))
        def _():
            acc_ref[...] = jnp.zeros_like(acc_ref)
            acc_ref[cols : cols + 8] = small_ref[...]

        acc_ref[:cols] += dot(dkv_ref[0], mem_ref[0])

        @pl.when((b == seqs - 1) & (t == steps - 1))
        def _():
            half = split[1]
            for hi in range(2):
                for out, at in ((keep_ref, spot[1]), (away_ref, 1 - spot[1])):
                    lanes = pl.ds(pl.multiple_of((hi * 2 + at) * half, half), half)
                    for side in range(2):
                        for g in range(0, KVH, 2):
                            pair = [
                                acc_ref[(g + i) * PAIR + side * HD : (g + i) * PAIR + (side + 1) * HD, lanes]
                                for i in range(2)
                            ]
                            left = side * cols // 2 + g * HD
                            out[hi, :, left : left + PAIR] = jnp.concatenate(pair, axis=0).T.astype(bf16)
                    out[hi, :, cols:] = acc_ref[cols:, lanes].T.astype(bf16)

    return call(
        kernel,
        [links.spot, memory, grad_keyval, small],
        [
            smem(),
            pl.BlockSpec((1, tile, width), lambda b, t: (b, t, 0)),
            pl.BlockSpec((1, cols, tile), lambda b, t: (b, 0, t)),
            whole((8, width)),
        ],
        (struct(split, bf16), struct(split, bf16)),
        [whole(split)] * 2,
        "keyval_weight_grad",
        micros=15,
        after=after,
        grid=(seqs, steps),
        scratch=[pltpu.VMEM((wide, width), f32)],
    )


def memory_gradient(links, grad_keyval, blocks, b, before, after):
    seqs, cols, count = grad_keyval.shape
    width = cols
    tile = 1024
    n = blocks.count
    given = () if before is None else (before,)

    def kernel(spot, dkv_ref, *refs):
        out_ref, w_ref = refs[n + len(given) :]

        @pl.when(pl.program_id(0) == 0)
        def _():
            blocks.put(spot, refs[:n], w_ref)

        out_ref[0] = dot(dkv_ref[0].T, w_ref[...], 1, 1).astype(bf16)

    return call(
        kernel,
        [links.spot, grad_keyval] + blocks.arrays + list(given),
        [smem(), pl.BlockSpec((1, cols, tile), lambda t: (b, 0, t))]
        + blocks.specs(cols, 0)
        + [pl.BlockSpec(memory_space=pl.ANY)] * len(given),
        struct((seqs, count, width), bf16),
        pl.BlockSpec((1, tile, width), lambda t: (b, t, 0)),
        "memory_gradient",
        micros=8,
        after=after,
        grid=(count // tile,),
        scratch=[pltpu.VMEM((width, cols), bf16)],
        aliases={2 + n: 0} if given else {},
    )


def causal_enter(links, dx2, x1, gain_cross, n2, dq2, o1, blocks, after):
    rows, width = x1.shape
    n, m = blocks.count, 2 * blocks.count
    split = (2, width // 4, 2 * width)

    def kernel(spot, dx2_ref, x1_ref, g_ref, n2_ref, dq2_ref, o1_ref, *refs):
        dx_ref, do_ref, keep_ref, away_ref, gg_ref, wo_ref, wq_ref, o1t_ref, n2t_ref = refs[m:]
        blocks.put(spot, refs[:n], wo_ref)
        blocks.put(spot, refs[n:m], wq_ref)
        dq2 = dq2_ref[...]
        grad_rows, grad_gain = norm_back(dot(dq2, wq_ref[...], 1, 1), x1_ref[...], g_ref[...])
        gg_ref[...] = grad_gain
        dx1 = dx2_ref[...] + grad_rows
        dx_ref[...] = dx1
        da = dx1.astype(bf16)
        do_ref[...] = dot(da, wo_ref[...], 1, 1).astype(bf16)
        o1t_ref[...] = o1_ref[...].T
        split_rows(o1t_ref, da, spot[1], keep_ref.at[:, :, :width], away_ref.at[:, :, :width])
        n2t_ref[...] = n2_ref[...].T
        split_rows(n2t_ref, dq2, spot[1], keep_ref.at[:, :, width:], away_ref.at[:, :, width:])

    return call(
        kernel,
        [links.spot, dx2, x1, gain_cross, n2, dq2, o1] + blocks.arrays * 2,
        [smem(), whole((rows, width)), whole((rows, width)), whole((1, width))]
        + [whole((rows, width))] * 3
        + blocks.specs(width, 2)
        + blocks.specs(width, 3),
        (
            struct((rows, width), f32),
            struct((rows, width), bf16),
            struct(split, bf16),
            struct(split, bf16),
            struct((1, width), f32),
        ),
        [whole((rows, width))] * 2 + [whole(split)] * 2 + [whole((1, width))],
        "causal_enter",
        micros=8,
        after=after,
        scratch=[
            pltpu.VMEM((width, width), bf16),
            pltpu.VMEM((width, width), bf16),
            pltpu.VMEM((width, rows), bf16),
            pltpu.VMEM((width, rows), bf16),
        ],
    )


def causal_backward(links, lengths, dx1, do1, qkv1, n1, x, gain_causal, table, blocks, after):
    rows, width = n1.shape
    cols = qkv1.shape[1]
    seqs = lengths.shape[0]
    length = rows // seqs
    n = blocks.count
    split = (2, width // 4, cols)

    def kernel(spot, len_ref, dx1_ref, do_ref, qkv_ref, n1_ref, x_ref, g1_ref, tab_ref, *refs):
        keep_ref, away_ref, gg1_ref, bias_ref, dx_ref, w_ref, dqkv_ref, n1t_ref = refs[n:]
        blocks.put(spot, refs[:n], w_ref)
        tab = tab_ref[...]
        i = lax.broadcasted_iota(jnp.int32, (length, length), 0)
        j = lax.broadcasted_iota(jnp.int32, (length, length), 1)
        flip = jnp.where(i + j == length - 1, 1.0, 0.0).astype(bf16)
        for spots in batches(seqs):
            held = [
                (
                    heads_low(qkv_ref[rows_of(b, length), lanes_of(g)]),
                    heads_high(do_ref[rows_of(b, length), lanes_of(g)]),
                    qkv_ref[rows_of(b, length), lanes_of(g, width)],
                )
                for b, g in spots
            ]
            scores = [dot(low, keyval, 1, 1) for low, _, keyval in held]
            dps = [dot(high, keyval, 1, 1) for _, high, keyval in held]
            probs = [causal_probs(s, tab, g, length, len_ref[b]) for s, (b, g) in zip(scores, spots)]
            dss = [
                (p * (dp - jnp.sum(p * dp, axis=-1, keepdims=True))).astype(bf16)
                for p, dp in zip(probs, dps)
            ]
            for ds, p, (low, high, keyval), (b, g) in zip(dss, probs, held, spots):
                part = rows_of(b, length)
                dqkv_ref[part, lanes_of(g)] = merge_low(dot(ds, keyval)).astype(bf16)
                dqkv_ref[part, lanes_of(g, width)] = (
                    dot(ds.T, low) + dot(p.astype(bf16).T, high)
                ).astype(bf16)
            for i in range(0, len(spots), seqs):
                g = spots[i][1]
                for side in range(2):
                    total = None
                    for ds in dss[i : i + seqs]:
                        term = dot(flip, ds[side * length : (side + 1) * length])
                        total = term if total is None else total + term
                    bias_ref[2 * g + side : 2 * g + side + 1] = diagonal_sums(total)
        dqkv = dqkv_ref[...]
        n1t_ref[...] = n1_ref[...].T
        grad_rows, grad_gain = norm_back(
            dot(dqkv, w_ref[...], 1, 1), x_ref[...].astype(f32), g1_ref[...]
        )
        split_rows(n1t_ref, dqkv[:, :width], spot[1], keep_ref.at[:, :, :width], away_ref.at[:, :, :width])
        keep_low = low_lanes((rows, PAIR))
        apart = [[], []]
        for g in range(0, KVH, 2):
            one, two = (dqkv[:, width + i * PAIR : width + (i + 1) * PAIR] for i in (g, g + 1))
            apart[0].append(jnp.where(keep_low, one, swap_halves(two)))
            apart[1].append(jnp.where(keep_low, swap_halves(one), two))
        dkv = jnp.concatenate(apart[0] + apart[1], axis=1)
        split_rows(n1t_ref, dkv, spot[1], keep_ref.at[:, :, width:], away_ref.at[:, :, width:])
        gg1_ref[...] = grad_gain
        dx_ref[...] = (dx1_ref[...] + grad_rows).astype(bf16)

    return call(
        kernel,
        [links.spot, lengths, dx1, do1, qkv1, n1, x, gain_causal, table] + blocks.arrays,
        [smem(), smem(), whole((rows, width)), whole((rows, width)), whole((rows, cols))]
        + [whole((rows, width))] * 2
        + [whole((1, width)), whole(table.shape)]
        + blocks.specs(cols, 0),
        (
            struct(split, bf16),
            struct(split, bf16),
            struct((1, width), f32),
            struct((HEADS, bucket_reach), f32),
            struct((rows, width), bf16),
        ),
        [whole(split)] * 2 + [whole((1, width)), whole((HEADS, bucket_reach)), whole((rows, width))],
        "causal_backward",
        micros=15,
        after=after,
        scratch=[
            pltpu.VMEM((width, cols), bf16),
            pltpu.VMEM((rows, cols), bf16),
            pltpu.VMEM((width, rows), bf16),
        ],
    )


def interleave(w_key, w_value):
    r = w_key.shape[0]
    return jnp.concatenate(
        [w_key.reshape(r, KVH, HD), w_value.reshape(r, KVH, HD)], axis=2
    ).reshape(r, KVH * PAIR)


EXTRA = 128


def local(
    links,
    inputs,
    memory,
    lengths,
    cotangent,
    causal_query,
    causal_key,
    causal_value,
    causal_out,
    cross_query,
    cross_key,
    cross_value,
    cross_out,
    feed_gate,
    feed_up,
    feed_down,
    gain_causal,
    gain_cross,
    gain_feed,
    bias_table,
):
    links.locate()
    seqs, length, width = inputs.shape
    rows = seqs * length
    r = causal_query.shape[0]
    devices = links.nf * links.nd
    table_part = bias_table.shape[0]
    x = inputs.reshape(rows, width)
    cot = cotangent.reshape(rows, width)

    small = jnp.concatenate(
        [
            gain_causal[:, None],
            gain_cross[:, None],
            gain_feed[:, None],
            jnp.pad(bias_table[:, None], ((0, r - table_part), (0, 0))),
            jnp.zeros((r, EXTRA - 4), bf16),
        ],
        axis=1,
    )
    first_shard = jnp.concatenate([interleave(cross_key, cross_value), small], axis=1)
    causal_shard = jnp.concatenate(
        [causal_query, interleave(causal_key, causal_value), causal_out], axis=1
    )
    second_shard = jnp.concatenate([causal_shard, cross_query, cross_out], axis=1)
    units = feed_gate.shape[1] // links.nf
    feed_wide = jnp.stack(
        [
            jnp.concatenate([w[:, f * units : (f + 1) * units] for w in (feed_gate, feed_up)], axis=1)
            for f in range(links.nf)
        ]
    )

    bits = links.bits
    near = [frozenset()]
    lo_hi, hi_lo = ("lo", "hi"), ("hi", "lo")

    first_ring = links.grow((first_shard[None], near), bits)
    first_lo = links.grow(first_ring, ("lo",))
    second_one = links.grow((second_shard[None], near), bits[:1], first_ring[0])
    first_near = links.grow(first_lo, ("hi",))
    cot_core = links.send(cot, "core", first_lo[0])
    cot_hi = links.send(cot, "hi", first_lo[0])
    first_far = links.send(first_near[0], "core"), [f | {"core"} for f in first_near[1]]
    first_blocks = Blocks(links, first_near, first_far)
    second_ring = links.grow(second_one, bits[1:], first_near[0])
    feed_near = links.quarters(feed_wide, first_near[0], cot_core, cot_hi)

    stack, fars = second_ring
    half = stack.shape[2] // 2
    left_one = links.grow((stack[..., :half], fars), ("lo",))
    right_one = links.grow((stack[..., half:], fars), ("hi",))
    keyval, small_all = project_memory(
        links, tie(memory, stack, first_far[0], feed_near), first_blocks
    )
    feed_one = links.grow((feed_near[None], near), bits[:1], stack, then=(keyval,))
    left_two = links.send(left_one[0], "hi", keyval, feed_one[0])
    right_two = links.send(right_one[0], "lo", keyval, feed_one[0])
    feed_ring = links.grow(feed_one, bits[1:], keyval, then=(left_two, right_two))
    down_one = links.grow((feed_down[None], near), bits[:1], feed_one[0], left_one[0])
    n = len(fars)
    second_near = jnp.concatenate(
        [
            jnp.concatenate([left_one[0], left_two], axis=0),
            jnp.concatenate(
                [right_one[0][:n], right_two[:n], right_one[0][n:], right_two[n:]], axis=0
            ),
        ],
        axis=2,
    )
    down_ring = links.grow(down_one, bits[1:], then=(left_two, right_two))
    second_near = tie(second_near, feed_ring[0], down_ring[0])
    cot_both = links.send(cot_hi, "core", second_near)
    second_fars = left_one[1] + [f | {"hi"} for f in left_one[1]]
    second_far = links.send(second_near, "core"), [f | {"core"} for f in second_fars]
    second_blocks = Blocks(links, (second_near, second_fars), second_far)
    feed_far = links.send(feed_ring[0], "lo", right_two), [f | {"lo"} for f in feed_ring[1]]
    feed_blocks = Blocks(links, feed_ring, feed_far, quads=True)
    down_far = links.send(down_ring[0], "lo", right_two), [f | {"lo"} for f in down_ring[1]]
    cots = (cot, cot_core, cot_hi, cot_both)

    gain_one, gain_two, gain_three = (small_all[i : i + 1] for i in range(3))
    bias_all = small_all[3].reshape(devices, r)[:, :table_part].reshape(HEADS, BUCKETS)
    onehot = jnp.asarray(reversed_buckets())
    table = jnp.dot(bias_all.astype(bf16), onehot.astype(bf16), preferred_element_type=f32)

    x1, n1, qkv1, o1 = causal_forward(
        links, inputs, second_blocks, gain_one, table, lengths, (keyval,)
    )
    n2, q2, o2, x2, n3, probs = cross_forward(
        links, x1, keyval, second_blocks, gain_two, gain_three, ()
    )
    n3_hi = links.send(n3, "hi")
    n3_core = links.send(n3, "core")
    w_down = assemble(links, (down_ring, down_far), (n3,))
    w_gate, w_up, dh = feed_prepare(links, cots, feed_blocks, w_down, (n3,))
    n3_both = links.send(n3_hi, "core", dh)
    n3s = (n3, n3_core, n3_hi, n3_both)
    hidden, dgate, dup, dn3, dn3_hi, dn3_away = feed_through(n3s, w_gate, w_up, dh, ())

    dn3_got = links.send(dn3_away, "core")
    dn3_passed = (dn3_hi + dn3_got[rows:].astype(f32)).astype(bf16)
    dn3_terms = (dn3, dn3_got[:rows], links.send(dn3_passed, "hi"))
    y, y_hi, y_away, grad_gu, grad_down = feed_weight_grads(
        n3s, cots, hidden, dgate, dup, w_down, (dn3_passed,)
    )

    def split(a, axes):
        return a.reshape((2,) * len(axes) + (-1, a.shape[-1]))

    dp_axes = bits + ("lo",)
    apart = ("hi",) + dp_axes
    back = tuple(reversed(bits))

    def halves(keep, away, ways, *windows):
        got = split(links.send(away, "core"), apart)
        keep = split(keep, apart)
        return [
            Sum([Leaf(keep, apart, left, width), Leaf(got, apart, left, width)], ways + back)
            for left, width in windows
        ]

    gu_axes = ("hi", "core") + dp_axes
    feed_sums = [
        Sum([Leaf(split(grad_gu, gu_axes), gu_axes)], ("lo",) + back),
        Sum([Leaf(split(grad_down, dp_axes), dp_axes)], ("lo",) + back),
    ]
    done = advance(links, feed_sums, (y,))
    dx2, do2, keep, away, grad_gain_three = cross_enter(
        links, x2, gain_three, *dn3_terms, cot, o2, second_blocks, done
    )
    early_sums = halves(keep, away, hi_lo, (0, width))
    y_got = links.send(y_away, "core", dx2)
    dq2, grad_keyval = cross_backward(q2, do2, o2, keyval, probs, (dx2,))
    dx1, do1, keep, away, grad_gain_two = causal_enter(
        links, dx2, x1, gain_two, n2, dq2, o1, second_blocks, ()
    )
    done = advance(links, early_sums, (dx1,))
    o1q2_sums = halves(keep, away, hi_lo, (0, 2 * width))
    y_passed = (tie(y_hi, dx1) + y_got[rows:].astype(f32)).astype(bf16)
    y_terms = (y, y_got[:rows], links.send(y_passed, "hi"))
    keep, away, grad_gain_one, grad_bias, input_grad = causal_backward(
        links, lengths, dx1, do1, qkv1, n1, x, gain_one, table, second_blocks, done
    )
    middle_sums = halves(keep, away, hi_lo, (0, 2 * width))
    done = advance(links, feed_sums, (input_grad,))
    done = advance(links, o1q2_sums, (*done, early_sums[0].leaves[-1].array, y_terms[2]))
    early_sums += o1q2_sums

    grad_table = lax.dot_general(
        grad_bias, onehot, (((1,), (1,)), ((), ())), precision=lax.Precision.HIGHEST
    )
    table_rows = jnp.pad(
        grad_table.reshape(devices, table_part), ((0, 0), (0, r - table_part))
    ).reshape(1, width)
    small_rows = jnp.concatenate(
        [grad_gain_one, grad_gain_two, grad_gain_three, table_rows, jnp.zeros((4, width), f32)],
        axis=0,
    )
    keep, away = keyval_weight_grad(links, memory, grad_keyval, small_rows, done)
    late_sums = halves(keep, away, lo_hi, (0, KVH * PAIR + EXTRA))
    memory_grad = memory_gradient(links, grad_keyval, first_blocks, 0, None, (keep,))
    done = advance(links, feed_sums + early_sums + middle_sums + late_sums, (memory_grad,))
    for b in range(1, seqs):
        memory_grad = memory_gradient(links, grad_keyval, first_blocks, b, memory_grad, done)
    done = (memory_grad,)
    done = advance(links, early_sums + middle_sums + late_sums, done)
    half = width // 2
    while feed_sums[0].ways:
        done = advance(links, feed_sums, done)
    sum_gu, sum_down = finish(links, feed_sums, [(2 * units,), (width,)], done)
    done = (sum_down,)
    while late_sums[0].ways:
        done = advance(links, [one for one in early_sums + middle_sums + late_sums if one.ways], done)
    wide = links.unquarter(sum_gu, done)
    sum_o2, sum_o1, sum_q2, sum_q1, sum_k1, sum_v1, sum_k2, sum_v2, sum_small = finish(
        links,
        early_sums + middle_sums + late_sums,
        [(width,), (width, width), (width, half, half), (half, half, EXTRA)],
        done,
    )

    layer_out = (x2 + sum(tie(t, memory_grad).astype(f32) for t in y_terms)).astype(bf16)
    sum_gate, sum_up = (
        jnp.concatenate([part[:, i * units : (i + 1) * units] for part in wide], axis=1)
        for i in range(2)
    )
    return (
        layer_out.reshape(seqs, length, width),
        input_grad.reshape(seqs, length, width),
        memory_grad,
        sum_q1,
        sum_k1,
        sum_v1,
        sum_o1,
        sum_q2,
        sum_k2,
        sum_v2,
        sum_o2,
        sum_gate,
        sum_up,
        sum_down,
        sum_small[:, 0],
        sum_small[:, 1],
        sum_small[:, 2],
        sum_small[:table_part, 3],
    )


def solution(mesh):
    three = P(AXES, None, None)
    two = P(AXES, None)
    one = P(AXES)
    in_specs = (three, three, one, three) + (two,) * 11 + (one,) * 4
    out_specs = (three,) * 3 + (two,) * 11 + (one,) * 4
    body = functools.partial(local, Links(mesh))
    return jax.shard_map(body, mesh=mesh, in_specs=in_specs, out_specs=out_specs, check_vma=False)
```

```python
import functools

import jax
import jax.numpy as jnp
import numpy as np
from jax import lax
from jax.experimental import pallas as pl
from jax.experimental.pallas import tpu as pltpu
from jax.sharding import PartitionSpec as P

HEADS = 16
HD = 64
BUCKETS = 32
KVH = 8
PAIR = 2 * HD
AXES = ("fsdp", "dp")
norm_eps = 1e-06
masked_score = -1000000000.0
bucket_reach = 128
f32 = jnp.float32
bf16 = jnp.bfloat16
VMEM_LIMIT = 56 * 1024 * 1024
PLAN = 2e9
GROUPS = 4


def reversed_buckets():
    distance = (-np.arange(bucket_reach)) % bucket_reach
    exact_count = BUCKETS // 2
    spread = (
        np.log(np.maximum(distance, 1) / exact_count)
        / np.log(bucket_reach / exact_count)
        * (BUCKETS - exact_count)
    )
    far_bucket = np.minimum(exact_count + np.floor(spread).astype(np.int64), BUCKETS - 1)
    bucket_id = np.where(distance < exact_count, distance, far_bucket)
    return (bucket_id[None] == np.arange(BUCKETS)[:, None]).astype(np.float32)


def dot(a, b, ca=1, cb=0):
    return lax.dot_general(a, b, (((ca,), (cb,)), ((), ())), preferred_element_type=f32)


def call(kernel, ins, in_specs, out_shape, out_specs, name, after=(), grid=(1,), scratch=(), prefetch=None, micros=1, aliases=None):
    lead = 0 if prefetch is None else 1
    n = lead + len(ins)

    def body(*refs):
        kernel(*refs[:n], *refs[n + len(after) :])

    spec = pltpu.PrefetchScalarGridSpec(
        num_scalar_prefetch=lead,
        grid=grid,
        in_specs=list(in_specs) + [pl.BlockSpec(memory_space=pl.ANY)] * len(after),
        out_specs=out_specs,
        scratch_shapes=list(scratch),
    )
    front = () if prefetch is None else (prefetch,)
    return pl.pallas_call(
        body,
        grid_spec=spec,
        out_shape=out_shape,
        input_output_aliases=aliases or {},
        compiler_params=pltpu.CompilerParams(vmem_limit_bytes=VMEM_LIMIT),
        cost_estimate=pl.CostEstimate(
            flops=int(micros * PLAN), bytes_accessed=1000, transcendentals=0
        ),
        name=name,
    )(*front, *ins, *after)


def whole(shape):
    return pl.BlockSpec(shape, lambda *_: (0,) * len(shape))


def struct(shape, dtype):
    return jax.ShapeDtypeStruct(shape, dtype)


def smem():
    return pl.BlockSpec(memory_space=pltpu.SMEM)


class Links:
    def __init__(self, mesh):
        nf, nd = mesh.shape["fsdp"], mesh.shape["dp"]
        self.nf, self.nd, self.size = nf, nd, nd // 2
        self.bits = tuple(f"z{b}" for b in reversed(range(self.size.bit_length() - 1)))
        self.names = ("hi", "core", "ring", "lo") + self.bits
        spots = [(f, d) for f in range(nf) for d in range(nd)]

        def pairs(flip_f, flip_d):
            return [(f * nd + d, (f ^ flip_f) * nd + (d ^ flip_d)) for f, d in spots]

        self.pairs = {"core": pairs(1, 0), "hi": pairs(2, 0), "both": pairs(3, 0), "lo": pairs(0, 1)}
        self.masks = {}
        for name in self.bits:
            self.masks[name] = 1 << int(name[1:])
            self.pairs[name] = pairs(0, 2 << int(name[1:]))

    def locate(self):
        f, d = lax.axis_index("fsdp"), lax.axis_index("dp")
        self.hi, self.core, self.ring, self.lo = f // 2, f % 2, d // 2, d % 2
        zs = [(self.ring // self.masks[name]) % 2 for name in self.bits]
        self.spot = jnp.stack([self.hi, self.core, self.ring, self.lo, *zs]).astype(jnp.int32)

    def send(self, a, way, *after):
        return lax.ppermute(tie(a, *after), AXES, self.pairs[way])

    def grow(self, held, ways, *after, then=()):
        array, fars = held
        for way in ways:
            got = self.send(array, way, *after)
            after = ()
            array = jnp.concatenate([tie(array, *then), got], axis=0)
            fars = fars + [f | {way} for f in fars]
        return array, fars

    def quarters(self, wide, *after):
        mine = self.hi * 2 + self.core
        out = [lax.dynamic_index_in_dim(wide, mine, 0, keepdims=False)]
        for flip, way in ((1, "core"), (2, "hi"), (3, "both")):
            theirs = lax.dynamic_index_in_dim(wide, mine ^ flip, 0, keepdims=False)
            out.append(self.send(theirs, way, *after))
        return jnp.concatenate(out, axis=0)

    def unquarter(self, wide, after):
        _, _, r, c = wide.shape
        wide = wide.reshape(self.nf, r, c)
        mine = self.hi * 2 + self.core
        near = [tie(lax.dynamic_index_in_dim(wide, mine, 0, keepdims=False), *after)]
        for flip, way in ((1, "core"), (2, "hi"), (3, "both")):
            theirs = lax.dynamic_index_in_dim(wide, mine ^ flip, 0, keepdims=False).astype(bf16)
            near.append(tie(self.send(theirs, way), *after).astype(f32))
        near = jnp.stack(near)
        return [lax.dynamic_index_in_dim(near, mine ^ f, 0, keepdims=False) for f in range(self.nf)]


class Blocks:
    def __init__(self, links, *helds, quads=False):
        self.links = links
        self.arrays = [a for a, _ in helds]
        self.fars = [f for _, f in helds]
        self.quads = quads
        _, self.r, self.c = self.arrays[0].shape
        self.count = len(helds)

    def specs(self, width=None, index=0):
        return [
            pl.BlockSpec((*a.shape[:2], width or self.c), lambda *_: (0, 0, index))
            for a in self.arrays
        ]

    def put(self, spot, refs, *outs):
        quads = [(0, 0), (0, 1), (1, 0), (1, 1)] if self.quads else [None]
        r = self.r // len(quads)
        for ref, fars in zip(refs, self.fars):
            for i, far in enumerate(fars):
                for q, quad in enumerate(quads):
                    far_hi, far_core = quad or ("hi" in far, "core" in far)
                    at_hi = 1 - spot[0] if far_hi else spot[0]
                    at_core = 1 - spot[1] if far_core else spot[1]
                    row = ((at_hi * 2 + at_core) * self.links.nd + place_of(self.links, spot, far)) * r
                    rows = pl.ds(pl.multiple_of(row, r), r)
                    left = 0
                    for out in outs:
                        width = out.shape[-1]
                        out[rows, :] = ref[i, q * r : (q + 1) * r, left : left + width]
                        left += width


def place_of(links, spot, far):
    mask = sum(links.masks[name] for name in links.bits if name in far)
    at_ring = jnp.bitwise_xor(spot[2], mask) if mask else spot[2]
    at_lo = 1 - spot[3] if "lo" in far else spot[3]
    return at_ring * 2 + at_lo


def tie(x, *after):
    return lax.optimization_barrier((x, *after))[0] if after else x


def assemble(links, helds, after=()):
    _, r, c = helds[0][0].shape
    n = len(helds)
    most = max(len(f) for _, f in helds)

    def kernel(spot, *refs):
        out, held, sems_in, sems_out = refs[n:]
        copies = []
        for k, (ref, (_, fars)) in enumerate(zip(refs, helds)):
            for i, far in enumerate(fars):
                copies.append(
                    (
                        pltpu.make_async_copy(ref.at[i], held.at[k, i], sems_in.at[k, i]),
                        pltpu.make_async_copy(
                            held.at[k, i], out.at[place_of(links, spot, far)], sems_out.at[k, i]
                        ),
                    )
                )
        for one, _ in copies:
            one.start()
        for one, two in copies:
            one.wait()
            two.start()
        for _, two in copies:
            two.wait()

    out = call(
        kernel,
        [links.spot] + [a for a, _ in helds],
        [smem()] + [pl.BlockSpec(memory_space=pl.ANY)] * n,
        struct((links.nd, r, c), bf16),
        pl.BlockSpec(memory_space=pl.ANY),
        "assemble",
        micros=3,
        after=after,
        scratch=[
            pltpu.VMEM((n, most, r, c), bf16),
            pltpu.SemaphoreType.DMA((n, most)),
            pltpu.SemaphoreType.DMA((n, most)),
        ],
    )
    return out.reshape(-1, c)


class Leaf:
    def __init__(self, array, axes, left=0, width=None, held=()):
        self.array, self.axes, self.left, self.held = array, axes, left, dict(held)
        self.width = width or array.shape[-1]

    def hold(self, way, far):
        held = dict(self.held)
        if way in self.axes:
            held[way] = far
        return Leaf(self.array, self.axes, self.left, self.width, held)

    def free(self):
        return tuple(a for a in self.axes if a not in self.held)

    def spec(self, links):
        shape = tuple(None if a in self.held else 2 for a in self.axes) + self.array.shape[-2:]
        picks = [(self.held.get(a), links.names.index(a)) for a in self.axes]

        def index(_, spot):
            return (
                *(0 if far is None else 1 - spot[i] if far else spot[i] for far, i in picks),
                0,
                0,
            )

        return pl.BlockSpec(shape, index)


class Sum:
    def __init__(self, leaves, ways):
        self.leaves, self.ways = leaves, list(ways)


def gather_terms(links, leaves_of):
    ins = [leaf.array for leaves in leaves_of for leaf in leaves]
    specs = [leaf.spec(links) for leaves in leaves_of for leaf in leaves]

    def totals(refs):
        n = 0
        for leaves in leaves_of:
            total = None
            for leaf in leaves:
                term = refs[n][..., leaf.left : leaf.left + leaf.width].astype(f32)
                total = term if total is None else total + term
                n += 1
            yield total

    return ins, specs, totals


def advance(links, sums, after=()):
    moves = []
    for one in sums:
        way = one.ways.pop(0)
        moves.append((way, [leaf.hold(way, True) for leaf in one.leaves]))
        one.leaves = [leaf.hold(way, False) for leaf in one.leaves]
    groups, where = {}, []
    for way, leaves in moves:
        free = leaves[0].free()
        key = (way, free, leaves[0].array.shape[-2])
        left = groups.get(key, 0)
        groups[key] = left + leaves[0].width
        where.append((key, left, leaves[0].width))
    keys = list(groups)
    outs = [struct((2,) * len(free) + (r, groups[way, free, r]), bf16) for way, free, r in keys]
    ins, specs, totals = gather_terms(links, [leaves for _, leaves in moves])

    def kernel(spot, *refs):
        for total, (key, left, width) in zip(totals(refs), where):
            refs[len(ins) + keys.index(key)][..., left : left + width] = total.astype(bf16)

    sent = call(
        kernel, ins, specs, outs, [whole(o.shape) for o in outs], "combine", micros=3, after=after, prefetch=links.spot
    )
    got = {key: links.send(a, key[0]) for key, a in zip(keys, sent)}
    for one, (key, left, width) in zip(sums, where):
        one.leaves.append(Leaf(got[key], key[1], left, width))
    return (sent[0],)


def finish(links, sums, cuts, after=()):
    ins, specs, totals = gather_terms(links, [one.leaves for one in sums])
    outs = [
        struct((2,) * len(one.leaves[0].free()) + (one.leaves[0].array.shape[-2], width), f32)
        for one, widths in zip(sums, cuts)
        for width in widths
    ]

    def kernel(spot, *refs):
        n = len(ins)
        for total, widths in zip(totals(refs), cuts):
            left = 0
            for width in widths:
                refs[n][...] = total[..., left : left + width]
                left += width
                n += 1

    return call(
        kernel, ins, specs, outs, [whole(o.shape) for o in outs], "finish", micros=3, after=after, prefetch=links.spot
    )


def norm_scale(rows):
    return lax.rsqrt(jnp.mean(rows * rows, axis=-1, keepdims=True) + norm_eps)


def norm_back(grad_normed, rows, gain):
    scale = norm_scale(rows)
    scaled = grad_normed * gain
    inner_mean = jnp.mean(scaled * rows, axis=-1, keepdims=True)
    grad_rows = scale * scaled - rows * (scale * scale * scale) * inner_mean
    return grad_rows, jnp.sum(grad_normed * rows * scale, axis=0, keepdims=True)


def swap_halves(block):
    return pltpu.roll(block.astype(f32), HD, 1).astype(bf16)


def low_lanes(shape):
    return lax.broadcasted_iota(jnp.int32, shape, 1) < HD


def heads_low(block):
    keep = low_lanes(block.shape)
    zero = jnp.zeros_like(block)
    return jnp.concatenate(
        [jnp.where(keep, block, zero), jnp.where(keep, swap_halves(block), zero)], axis=0
    )


def heads_high(block):
    keep = low_lanes(block.shape)
    zero = jnp.zeros_like(block)
    return jnp.concatenate(
        [jnp.where(keep, zero, swap_halves(block)), jnp.where(keep, zero, block)], axis=0
    )


def merge_low(both):
    half = both.shape[0] // 2
    even, odd = both[:half], both[half:]
    return jnp.where(low_lanes(even.shape), even, pltpu.roll(odd, HD, 1))


def merge_high(both):
    half = both.shape[0] // 2
    even, odd = both[:half], both[half:]
    return jnp.where(low_lanes(even.shape), pltpu.roll(even, HD, 1), odd)


def toeplitz(row, length):
    return pltpu.roll(jnp.broadcast_to(row, (length, length)), 0, 1, stride=1, stride_axis=0)


def diagonal_sums(flipped):
    turned = pltpu.roll(flipped, 1, 1, stride=1, stride_axis=0)
    return jnp.sum(turned, axis=0, keepdims=True)


def batches(seqs):
    return [[(b, g) for g in range(k, k + 4) for b in range(seqs)] for k in range(0, KVH, 4)]


def rows_of(b, length):
    return slice(b * length, (b + 1) * length)


def lanes_of(g, left=0):
    return slice(left + g * PAIR, left + (g + 1) * PAIR)


def causal_probs(s, table, g, length, valid_len):
    bias = jnp.concatenate(
        [toeplitz(table[2 * g : 2 * g + 1], length), toeplitz(table[2 * g + 1 : 2 * g + 2], length)],
        axis=0,
    )
    i = lax.broadcasted_iota(jnp.int32, (length, length), 0)
    j = lax.broadcasted_iota(jnp.int32, (length, length), 1)
    valid = (j <= i) & (j < valid_len)
    valid = jnp.concatenate([valid, valid], axis=0)
    s = jnp.where(valid, s + bias, masked_score)
    e = jnp.exp(s - jnp.max(s, axis=-1, keepdims=True))
    return e / jnp.sum(e, axis=-1, keepdims=True)


def split_rows(lhs_t, rhs, core, keep, away):
    half = keep.shape[1]
    for hi in range(keep.shape[0]):
        for out, at in ((keep, core), (away, 1 - core)):
            row = pl.multiple_of((hi * 2 + at) * half, half)
            out[hi] = dot(lhs_t[pl.ds(row, half), :], rhs).astype(bf16)


def project_memory(links, memory, blocks):
    seqs, count, width = memory.shape
    cols = KVH * PAIR
    tile = 1024
    n = blocks.count

    def kernel(spot, mem_ref, *refs):
        held = refs[:n]
        out_ref, small_ref, w_ref, wt_ref = refs[n:]

        @pl.when((pl.program_id(0) == 0) & (pl.program_id(1) == 0))
        def _():
            blocks.put(spot, held, w_ref)
            wt_ref[...] = w_ref[:, :cols].T
            small_ref[...] = w_ref[:, cols:].astype(f32).T[:8]

        out_ref[0] = dot(wt_ref[...], mem_ref[0], 1, 1).astype(bf16)

    return call(
        kernel,
        [links.spot, memory] + blocks.arrays,
        [smem(), pl.BlockSpec((1, tile, width), lambda b, t: (b, t, 0))] + blocks.specs(),
        (struct((seqs, cols, count), bf16), struct((8, width), f32)),
        [pl.BlockSpec((1, cols, tile), lambda b, t: (b, 0, t)), whole((8, width))],
        "project_memory",
        micros=15,
        grid=(seqs, count // tile),
        scratch=[pltpu.VMEM((width, blocks.c), bf16), pltpu.VMEM((cols, width), bf16)],
    )


def causal_forward(links, x, blocks, gain, table, lengths, after):
    seqs, length, width = x.shape
    rows = seqs * length
    cols = 2 * width
    n = blocks.count

    def kernel(spot, len_ref, x_ref, gain_ref, tab_ref, *refs):
        x1_ref, n1_ref, qkv_ref, o1_ref, w_ref, wo_ref = refs[n:]
        blocks.put(spot, refs[:n], w_ref, wo_ref)
        xf = x_ref[...].astype(f32)
        n1 = (xf * norm_scale(xf) * gain_ref[...]).astype(bf16)
        n1_ref[...] = n1
        qkv_ref[...] = dot(n1, w_ref[...]).astype(bf16)
        tab = tab_ref[...]
        for spots in batches(seqs):
            held = [
                (qkv_ref[rows_of(b, length), lanes_of(g)], qkv_ref[rows_of(b, length), lanes_of(g, width)])
                for b, g in spots
            ]
            scores = [dot(heads_low(q), keyval, 1, 1) for q, keyval in held]
            probs = [
                causal_probs(s, tab, g, length, len_ref[b]).astype(bf16)
                for s, (b, g) in zip(scores, spots)
            ]
            for p, (_, keyval), (b, g) in zip(probs, held, spots):
                o1_ref[rows_of(b, length), lanes_of(g)] = merge_high(dot(p, keyval)).astype(bf16)
        x1_ref[...] = xf + dot(o1_ref[...], wo_ref[...])

    return call(
        kernel,
        [links.spot, lengths, x.reshape(rows, width), gain, table] + blocks.arrays,
        [smem(), smem(), whole((rows, width)), whole((1, width)), whole(table.shape)]
        + blocks.specs(cols + width, 0),
        (
            struct((rows, width), f32),
            struct((rows, width), bf16),
            struct((rows, cols), bf16),
            struct((rows, width), bf16),
        ),
        [whole((rows, width)), whole((rows, width)), whole((rows, cols)), whole((rows, width))],
        "causal_forward",
        micros=9,
        after=after,
        scratch=[pltpu.VMEM((width, cols), bf16), pltpu.VMEM((width, width), bf16)],
    )


def cross_forward(links, x1, keyval, blocks, gain_cross, gain_feed, after):
    rows, width = x1.shape
    seqs, _, count = keyval.shape
    length = rows // seqs
    n = blocks.count * 2
    steps = KVH // GROUPS

    def kernel(spot, x1_ref, kv_ref, g2_ref, g3_ref, *refs):
        n2_ref, q2_ref, o2_ref, x2_ref, n3_ref, p_ref, wq_ref, wo_ref = refs[n:]
        b, g = pl.program_id(0), pl.program_id(1)

        @pl.when((b == 0) & (g == 0))
        def _():
            blocks.put(spot, refs[: n // 2], wq_ref)
            blocks.put(spot, refs[n // 2 : n], wo_ref)
            x1v = x1_ref[...]
            n2 = (x1v * norm_scale(x1v) * g2_ref[...]).astype(bf16)
            n2_ref[...] = n2
            q2_ref[...] = dot(n2, wq_ref[...]).astype(bf16)

        part = pl.ds(pl.multiple_of(b * length, length), length)
        lanes = [pl.ds(pl.multiple_of((g * GROUPS + i) * PAIR, PAIR), PAIR) for i in range(GROUPS)]
        scores = [
            dot(heads_low(q2_ref[part, lanes[i]]), kv_ref[0, i * PAIR : (i + 1) * PAIR])
            for i in range(GROUPS)
        ]
        for i, s in enumerate(scores):
            e = jnp.exp(s - jnp.max(s, axis=-1, keepdims=True))
            p_ref[i] = (e * (1.0 / jnp.sum(e, axis=-1, keepdims=True))).astype(bf16)
        for i in range(GROUPS):
            mixed = dot(p_ref[i], kv_ref[0, i * PAIR : (i + 1) * PAIR], 1, 1)
            o2_ref[part, lanes[i]] = merge_high(mixed).astype(bf16)

        @pl.when((b == seqs - 1) & (g == steps - 1))
        def _():
            x2 = x1_ref[...] + dot(o2_ref[...], wo_ref[...])
            x2_ref[...] = x2
            n3_ref[...] = (x2 * norm_scale(x2) * g3_ref[...]).astype(bf16)

    return call(
        kernel,
        [links.spot, x1, keyval, gain_cross, gain_feed] + blocks.arrays * 2,
        [
            smem(),
            whole((rows, width)),
            pl.BlockSpec((1, GROUPS * PAIR, count), lambda b, g: (b, g, 0)),
            whole((1, width)),
            whole((1, width)),
        ]
        + blocks.specs(width, 3)
        + blocks.specs(width, 4),
        (
            struct((rows, width), bf16),
            struct((rows, width), bf16),
            struct((rows, width), bf16),
            struct((rows, width), f32),
            struct((rows, width), bf16),
            struct((seqs * KVH, 2 * length, count), bf16),
        ),
        [whole((rows, width))] * 5
        + [pl.BlockSpec((GROUPS, 2 * length, count), lambda b, g: (b * steps + g, 0, 0))],
        "cross_forward",
        micros=34,
        after=after,
        grid=(seqs, steps),
        scratch=[pltpu.VMEM((width, width), bf16)] * 2,
    )


def stack_rows(refs, out):
    rows = refs[0].shape[0]
    for i, ref in enumerate(refs):
        out[i * rows : (i + 1) * rows] = ref[...]


def feed_prepare(links, cots, blocks, w_down, after):
    rows, width = cots[0].shape
    units = w_down.shape[0]
    n = blocks.count

    def kernel(spot, *refs):
        wd_ref = refs[4]
        wg_ref, wu_ref, dh_ref, cot_all = refs[5 + n :]
        blocks.put(spot, refs[5 : 5 + n], wg_ref, wu_ref)
        stack_rows(refs[:4], cot_all)
        dh_ref[...] = dot(cot_all[...], wd_ref[...], 1, 1)

    return call(
        kernel,
        [links.spot, *cots, w_down] + blocks.arrays,
        [smem()] + [whole((rows, width))] * 4 + [whole(w_down.shape)] + blocks.specs(),
        (
            struct((width, units), bf16),
            struct((width, units), bf16),
            struct((4 * rows, units), f32),
        ),
        [whole((width, units))] * 2 + [whole((4 * rows, units))],
        "feed_prepare",
        micros=6,
        after=after,
        scratch=[pltpu.VMEM((4 * rows, width), bf16)],
    )


def feed_through(n3s, w_gate, w_up, dh, after):
    rows, width = n3s[0].shape
    units = w_gate.shape[1]
    c0 = np.float32(np.sqrt(2.0 / np.pi))
    c1 = np.float32(0.044715)
    cuts = [slice(i, min(i + 256, units)) for i in range(0, units, 256)]

    def kernel(*refs):
        wg_ref, wu_ref, dh_ref = refs[4:7]
        hid_ref, dgate_ref, dup_ref, dn_ref, dn_hi_ref, dn_away_ref, n3_all = refs[7:]
        stack_rows(refs[:4], n3_all)
        for cut in cuts:
            gate = dot(n3_all[...], wg_ref[:, cut])
            up = dot(n3_all[...], wu_ref[:, cut])
            dh = dh_ref[:, cut]
            square = gate * gate
            t = jnp.tanh(c0 * (gate + c1 * (square * gate)))
            cdf = 0.5 * (1.0 + t)
            value = gate * cdf
            slope = cdf + 0.5 * gate * (1.0 - t * t) * (c0 * (1.0 + 3.0 * c1 * square))
            hid_ref[:, cut] = (value * up).astype(bf16)
            dgate_ref[:, cut] = (dh * up * slope).astype(bf16)
            dup_ref[:, cut] = (dh * value).astype(bf16)
        for i in range(0, width, 256):
            at = slice(i, i + 256)
            dn = dot(dgate_ref[...], wg_ref[at, :], 1, 1) + dot(dup_ref[...], wu_ref[at, :], 1, 1)
            dn_ref[:, at] = dn[:rows]
            dn_away_ref[:rows, at] = dn[rows : 2 * rows].astype(bf16)
            dn_hi_ref[:, at] = dn[2 * rows : 3 * rows]
            dn_away_ref[rows:, at] = dn[3 * rows :].astype(bf16)

    return call(
        kernel,
        [*n3s, w_gate, w_up, dh],
        [whole((rows, width))] * 4 + [whole((width, units))] * 2 + [whole((4 * rows, units))],
        (
            struct((4 * rows, units), bf16),
            struct((4 * rows, units), bf16),
            struct((4 * rows, units), bf16),
            struct((rows, width), f32),
            struct((rows, width), f32),
            struct((2 * rows, width), bf16),
        ),
        [whole((4 * rows, units))] * 3 + [whole((rows, width))] * 2 + [whole((2 * rows, width))],
        "feed_through",
        micros=14,
        after=after,
        scratch=[pltpu.VMEM((4 * rows, width), bf16)],
    )


def feed_weight_grads(links, n3s, cots, hidden, dgate, dup, w_down, after):
    rows, width = n3s[0].shape
    units = hidden.shape[1]
    tile = width // links.nf
    r, d = tile // links.nd, units // links.nd

    def kernel(spot, *refs):
        hid_ref, dgate_ref, dup_ref, wd_ref = refs[8:12]
        y_ref, y_hi_ref, y_away_ref = refs[12:15]
        gu_keep, gu_away, gd_keep, gd_away, n3t_ref, cot_all, hid_t, gu_ref, gd_ref = refs[15:]

        @pl.when(pl.program_id(0) == 0)
        def _():
            hid_t[...] = hid_ref[...].T

        for i in range(4):
            n3t_ref[:, i * rows : (i + 1) * rows] = refs[i][...].T
        stack_rows(refs[4:8], cot_all)
        gu_ref[:, :units] = dot(n3t_ref[...], dgate_ref[...])
        gu_ref[:, units:] = dot(n3t_ref[...], dup_ref[...])
        down = dot(hid_t[...], cot_all[...])
        for place in range(links.nd):
            gd_ref[place] = down[place * d : (place + 1) * d]
        for ring in range(links.size):
            for at, gu, gd in ((spot[3], gu_keep, gd_keep), (1 - spot[3], gu_away, gd_away)):
                place = ring * 2 + at
                gu[0, ring] = gu_ref[pl.ds(pl.multiple_of(place * r, 8), r), :].astype(bf16)
                gd[ring] = gd_ref[place].astype(bf16)
        y = dot(hid_ref[...], wd_ref[...])
        y_ref[...] = y[:rows]
        y_away_ref[:rows] = y[rows : 2 * rows].astype(bf16)
        y_hi_ref[...] = y[2 * rows : 3 * rows]
        y_away_ref[rows:] = y[3 * rows :].astype(bf16)

    def columns(count):
        return pl.BlockSpec((count, tile), lambda t: (0, t))

    return call(
        kernel,
        [links.spot, *n3s, *cots, hidden, dgate, dup, w_down],
        [smem()] + [columns(rows)] * 8 + [whole((4 * rows, units))] * 3 + [columns(units)],
        (
            struct((rows, width), f32),
            struct((rows, width), f32),
            struct((2 * rows, width), bf16),
            *[struct((links.nf, links.size, r, 2 * units), bf16)] * 2,
            *[struct((links.size, d, width), bf16)] * 2,
        ),
        [columns(rows)] * 2
        + [columns(2 * rows)]
        + [pl.BlockSpec((1, links.size, r, 2 * units), lambda t: (t, 0, 0, 0))] * 2
        + [pl.BlockSpec((links.size, d, tile), lambda t: (0, 0, t))] * 2,
        "feed_weight_grads",
        micros=12,
        after=after,
        grid=(width // tile,),
        scratch=[
            pltpu.VMEM((tile, 4 * rows), bf16),
            pltpu.VMEM((4 * rows, tile), bf16),
            pltpu.VMEM((units, 4 * rows), bf16),
            pltpu.VMEM((tile, 2 * units), f32),
            pltpu.VMEM((links.nd, d, tile), f32),
        ],
    )


def cross_enter(links, x2, gain_feed, dn3, dn3_core, dn3_hi, cotangent, o2, out_blocks, after):
    rows, width = x2.shape
    n = out_blocks.count
    split = (2, width // 4, width)

    def kernel(spot, x2_ref, g_ref, dn_ref, dn_core_ref, dn_hi_ref, cot_ref, o2_ref, *refs):
        dx_ref, do_ref, keep_ref, away_ref, gg_ref, w_ref, o2t_ref = refs[n:]
        out_blocks.put(spot, refs[:n], w_ref)
        dn = dn_ref[...] + dn_core_ref[...].astype(f32) + dn_hi_ref[...].astype(f32)
        grad_rows, grad_gain = norm_back(dn, x2_ref[...], g_ref[...])
        gg_ref[...] = grad_gain
        dx2 = cot_ref[...].astype(f32) + grad_rows
        dx_ref[...] = dx2
        da = dx2.astype(bf16)
        do_ref[...] = dot(da, w_ref[...], 1, 1).astype(bf16)
        o2t_ref[...] = o2_ref[...].T
        split_rows(o2t_ref, da, spot[1], keep_ref, away_ref)

    return call(
        kernel,
        [links.spot, x2, gain_feed, dn3, dn3_core, dn3_hi, cotangent, o2] + out_blocks.arrays,
        [smem(), whole((rows, width)), whole((1, width))]
        + [whole((rows, width))] * 5
        + out_blocks.specs(width, 4),
        (
            struct((rows, width), f32),
            struct((rows, width), bf16),
            struct(split, bf16),
            struct(split, bf16),
            struct((1, width), f32),
        ),
        [whole((rows, width))] * 2 + [whole(split)] * 2 + [whole((1, width))],
        "cross_enter",
        micros=6,
        after=after,
        scratch=[pltpu.VMEM((width, width), bf16), pltpu.VMEM((width, rows), bf16)],
    )


def cross_backward(q2, do2, o2, keyval, probs, after):
    rows, width = q2.shape
    seqs, cols, count = keyval.shape
    length = rows // seqs
    steps = KVH // GROUPS

    def kernel(q_ref, do_ref, o_ref, kv_ref, p_ref, dq_ref, dkv_ref):
        for i in range(GROUPS):
            lanes = slice(i * PAIR, (i + 1) * PAIR)
            q, do = q_ref[:, lanes], do_ref[:, lanes]
            low, high = heads_low(q), heads_high(do)
            product = do.astype(f32) * o_ref[:, lanes].astype(f32)
            keep = low_lanes(product.shape)
            inner = jnp.concatenate(
                [
                    jnp.sum(jnp.where(keep, product, 0.0), axis=-1, keepdims=True),
                    jnp.sum(jnp.where(keep, 0.0, product), axis=-1, keepdims=True),
                ],
                axis=0,
            )
            kv = kv_ref[0, lanes]
            p = p_ref[i]
            ds = (p.astype(f32) * (dot(high, kv) - inner)).astype(bf16)
            dq_ref[:, lanes] = merge_low(dot(ds, kv, 1, 1)).astype(bf16)
            dkv_ref[0, lanes] = (dot(low.T, ds) + dot(high.T, p)).astype(bf16)

    heads_block = pl.BlockSpec((length, GROUPS * PAIR), lambda b, g: (b, g))
    kv_block = pl.BlockSpec((1, GROUPS * PAIR, count), lambda b, g: (b, g, 0))
    return call(
        kernel,
        [q2, do2, o2, keyval, probs],
        [
            heads_block,
            heads_block,
            heads_block,
            kv_block,
            pl.BlockSpec((GROUPS, 2 * length, count), lambda b, g: (b * steps + g, 0, 0)),
        ],
        (struct((rows, width), bf16), struct((seqs, cols, count), bf16)),
        [heads_block, kv_block],
        "cross_backward",
        micros=25,
        after=after,
        grid=(seqs, steps),
    )


def keyval_weight_grad(links, memory, grad_keyval, small, after):
    seqs, count, width = memory.shape
    cols = grad_keyval.shape[1]
    tile = 1024
    steps = count // tile
    wide = cols + EXTRA
    split = (2, width // 4, wide)

    def kernel(spot, mem_ref, dkv_ref, small_ref, keep_ref, away_ref, acc_ref):
        b, t = pl.program_id(0), pl.program_id(1)

        @pl.when((b == 0) & (t == 0))
        def _():
            acc_ref[...] = jnp.zeros_like(acc_ref)
            acc_ref[cols : cols + 8] = small_ref[...]

        acc_ref[:cols] += dot(dkv_ref[0], mem_ref[0])

        @pl.when((b == seqs - 1) & (t == steps - 1))
        def _():
            half = split[1]
            for hi in range(2):
                for out, at in ((keep_ref, spot[1]), (away_ref, 1 - spot[1])):
                    lanes = pl.ds(pl.multiple_of((hi * 2 + at) * half, half), half)
                    for side in range(2):
                        for g in range(0, KVH, 2):
                            pair = [
                                acc_ref[(g + i) * PAIR + side * HD : (g + i) * PAIR + (side + 1) * HD, lanes]
                                for i in range(2)
                            ]
                            left = side * cols // 2 + g * HD
                            out[hi, :, left : left + PAIR] = jnp.concatenate(pair, axis=0).T.astype(bf16)
                    out[hi, :, cols:] = acc_ref[cols:, lanes].T.astype(bf16)

    return call(
        kernel,
        [links.spot, memory, grad_keyval, small],
        [
            smem(),
            pl.BlockSpec((1, tile, width), lambda b, t: (b, t, 0)),
            pl.BlockSpec((1, cols, tile), lambda b, t: (b, 0, t)),
            whole((8, width)),
        ],
        (struct(split, bf16), struct(split, bf16)),
        [whole(split)] * 2,
        "keyval_weight_grad",
        micros=15,
        after=after,
        grid=(seqs, steps),
        scratch=[pltpu.VMEM((wide, width), f32)],
    )


def memory_gradient(links, grad_keyval, blocks, b, before, after):
    seqs, cols, count = grad_keyval.shape
    width = cols
    tile = 1024
    n = blocks.count
    given = () if before is None else (before,)

    def kernel(spot, dkv_ref, *refs):
        out_ref, w_ref = refs[n + len(given) :]

        @pl.when(pl.program_id(0) == 0)
        def _():
            blocks.put(spot, refs[:n], w_ref)

        out_ref[0] = dot(dkv_ref[0].T, w_ref[...], 1, 1).astype(bf16)

    return call(
        kernel,
        [links.spot, grad_keyval] + blocks.arrays + list(given),
        [smem(), pl.BlockSpec((1, cols, tile), lambda t: (b, 0, t))]
        + blocks.specs(cols, 0)
        + [pl.BlockSpec(memory_space=pl.ANY)] * len(given),
        struct((seqs, count, width), bf16),
        pl.BlockSpec((1, tile, width), lambda t: (b, t, 0)),
        "memory_gradient",
        micros=8,
        after=after,
        grid=(count // tile,),
        scratch=[pltpu.VMEM((width, cols), bf16)],
        aliases={2 + n: 0} if given else {},
    )


def causal_enter(links, dx2, x1, gain_cross, n2, dq2, o1, blocks, after):
    rows, width = x1.shape
    n, m = blocks.count, 2 * blocks.count
    split = (2, width // 4, 2 * width)

    def kernel(spot, dx2_ref, x1_ref, g_ref, n2_ref, dq2_ref, o1_ref, *refs):
        dx_ref, do_ref, keep_ref, away_ref, gg_ref, wo_ref, wq_ref, o1t_ref, n2t_ref = refs[m:]
        blocks.put(spot, refs[:n], wo_ref)
        blocks.put(spot, refs[n:m], wq_ref)
        dq2 = dq2_ref[...]
        grad_rows, grad_gain = norm_back(dot(dq2, wq_ref[...], 1, 1), x1_ref[...], g_ref[...])
        gg_ref[...] = grad_gain
        dx1 = dx2_ref[...] + grad_rows
        dx_ref[...] = dx1
        da = dx1.astype(bf16)
        do_ref[...] = dot(da, wo_ref[...], 1, 1).astype(bf16)
        o1t_ref[...] = o1_ref[...].T
        split_rows(o1t_ref, da, spot[1], keep_ref.at[:, :, :width], away_ref.at[:, :, :width])
        n2t_ref[...] = n2_ref[...].T
        split_rows(n2t_ref, dq2, spot[1], keep_ref.at[:, :, width:], away_ref.at[:, :, width:])

    return call(
        kernel,
        [links.spot, dx2, x1, gain_cross, n2, dq2, o1] + blocks.arrays * 2,
        [smem(), whole((rows, width)), whole((rows, width)), whole((1, width))]
        + [whole((rows, width))] * 3
        + blocks.specs(width, 2)
        + blocks.specs(width, 3),
        (
            struct((rows, width), f32),
            struct((rows, width), bf16),
            struct(split, bf16),
            struct(split, bf16),
            struct((1, width), f32),
        ),
        [whole((rows, width))] * 2 + [whole(split)] * 2 + [whole((1, width))],
        "causal_enter",
        micros=8,
        after=after,
        scratch=[
            pltpu.VMEM((width, width), bf16),
            pltpu.VMEM((width, width), bf16),
            pltpu.VMEM((width, rows), bf16),
            pltpu.VMEM((width, rows), bf16),
        ],
    )


def causal_backward(links, lengths, dx1, do1, qkv1, n1, x, gain_causal, table, blocks, after):
    rows, width = n1.shape
    cols = qkv1.shape[1]
    seqs = lengths.shape[0]
    length = rows // seqs
    n = blocks.count
    split = (2, width // 4, cols)

    def kernel(spot, len_ref, dx1_ref, do_ref, qkv_ref, n1_ref, x_ref, g1_ref, tab_ref, *refs):
        keep_ref, away_ref, gg1_ref, bias_ref, dx_ref, w_ref, dqkv_ref, n1t_ref = refs[n:]
        blocks.put(spot, refs[:n], w_ref)
        tab = tab_ref[...]
        i = lax.broadcasted_iota(jnp.int32, (length, length), 0)
        j = lax.broadcasted_iota(jnp.int32, (length, length), 1)
        flip = jnp.where(i + j == length - 1, 1.0, 0.0).astype(bf16)
        for spots in batches(seqs):
            held = [
                (
                    heads_low(qkv_ref[rows_of(b, length), lanes_of(g)]),
                    heads_high(do_ref[rows_of(b, length), lanes_of(g)]),
                    qkv_ref[rows_of(b, length), lanes_of(g, width)],
                )
                for b, g in spots
            ]
            scores = [dot(low, keyval, 1, 1) for low, _, keyval in held]
            dps = [dot(high, keyval, 1, 1) for _, high, keyval in held]
            probs = [causal_probs(s, tab, g, length, len_ref[b]) for s, (b, g) in zip(scores, spots)]
            dss = [
                (p * (dp - jnp.sum(p * dp, axis=-1, keepdims=True))).astype(bf16)
                for p, dp in zip(probs, dps)
            ]
            for ds, p, (low, high, keyval), (b, g) in zip(dss, probs, held, spots):
                part = rows_of(b, length)
                dqkv_ref[part, lanes_of(g)] = merge_low(dot(ds, keyval)).astype(bf16)
                dqkv_ref[part, lanes_of(g, width)] = (
                    dot(ds.T, low) + dot(p.astype(bf16).T, high)
                ).astype(bf16)
            for i in range(0, len(spots), seqs):
                g = spots[i][1]
                for side in range(2):
                    total = None
                    for ds in dss[i : i + seqs]:
                        term = dot(flip, ds[side * length : (side + 1) * length])
                        total = term if total is None else total + term
                    bias_ref[2 * g + side : 2 * g + side + 1] = diagonal_sums(total)
        dqkv = dqkv_ref[...]
        n1t_ref[...] = n1_ref[...].T
        grad_rows, grad_gain = norm_back(
            dot(dqkv, w_ref[...], 1, 1), x_ref[...].astype(f32), g1_ref[...]
        )
        split_rows(n1t_ref, dqkv[:, :width], spot[1], keep_ref.at[:, :, :width], away_ref.at[:, :, :width])
        keep_low = low_lanes((rows, PAIR))
        apart = [[], []]
        for g in range(0, KVH, 2):
            one, two = (dqkv[:, width + i * PAIR : width + (i + 1) * PAIR] for i in (g, g + 1))
            apart[0].append(jnp.where(keep_low, one, swap_halves(two)))
            apart[1].append(jnp.where(keep_low, swap_halves(one), two))
        dkv = jnp.concatenate(apart[0] + apart[1], axis=1)
        split_rows(n1t_ref, dkv, spot[1], keep_ref.at[:, :, width:], away_ref.at[:, :, width:])
        gg1_ref[...] = grad_gain
        dx_ref[...] = (dx1_ref[...] + grad_rows).astype(bf16)

    return call(
        kernel,
        [links.spot, lengths, dx1, do1, qkv1, n1, x, gain_causal, table] + blocks.arrays,
        [smem(), smem(), whole((rows, width)), whole((rows, width)), whole((rows, cols))]
        + [whole((rows, width))] * 2
        + [whole((1, width)), whole(table.shape)]
        + blocks.specs(cols, 0),
        (
            struct(split, bf16),
            struct(split, bf16),
            struct((1, width), f32),
            struct((HEADS, bucket_reach), f32),
            struct((rows, width), bf16),
        ),
        [whole(split)] * 2 + [whole((1, width)), whole((HEADS, bucket_reach)), whole((rows, width))],
        "causal_backward",
        micros=15,
        after=after,
        scratch=[
            pltpu.VMEM((width, cols), bf16),
            pltpu.VMEM((rows, cols), bf16),
            pltpu.VMEM((width, rows), bf16),
        ],
    )


def interleave(w_key, w_value):
    r = w_key.shape[0]
    return jnp.concatenate(
        [w_key.reshape(r, KVH, HD), w_value.reshape(r, KVH, HD)], axis=2
    ).reshape(r, KVH * PAIR)


EXTRA = 128


def local(
    links,
    inputs,
    memory,
    lengths,
    cotangent,
    causal_query,
    causal_key,
    causal_value,
    causal_out,
    cross_query,
    cross_key,
    cross_value,
    cross_out,
    feed_gate,
    feed_up,
    feed_down,
    gain_causal,
    gain_cross,
    gain_feed,
    bias_table,
):
    links.locate()
    seqs, length, width = inputs.shape
    rows = seqs * length
    r = causal_query.shape[0]
    devices = links.nf * links.nd
    table_part = bias_table.shape[0]
    x = inputs.reshape(rows, width)
    cot = cotangent.reshape(rows, width)

    small = jnp.concatenate(
        [
            gain_causal[:, None],
            gain_cross[:, None],
            gain_feed[:, None],
            jnp.pad(bias_table[:, None], ((0, r - table_part), (0, 0))),
            jnp.zeros((r, EXTRA - 4), bf16),
        ],
        axis=1,
    )
    first_shard = jnp.concatenate([interleave(cross_key, cross_value), small], axis=1)
    causal_shard = jnp.concatenate(
        [causal_query, interleave(causal_key, causal_value), causal_out], axis=1
    )
    second_shard = jnp.concatenate([causal_shard, cross_query, cross_out], axis=1)
    units = feed_gate.shape[1] // links.nf
    feed_wide = jnp.stack(
        [
            jnp.concatenate([w[:, f * units : (f + 1) * units] for w in (feed_gate, feed_up)], axis=1)
            for f in range(links.nf)
        ]
    )

    bits = links.bits
    near = [frozenset()]
    lo_hi, hi_lo = ("lo", "hi"), ("hi", "lo")

    first_ring = links.grow((first_shard[None], near), bits)
    first_lo = links.grow(first_ring, ("lo",))
    second_one = links.grow((second_shard[None], near), bits[:1], first_ring[0])
    first_near = links.grow(first_lo, ("hi",))
    cot_core = links.send(cot, "core", first_lo[0])
    cot_hi = links.send(cot, "hi", first_lo[0])
    first_far = links.send(first_near[0], "core"), [f | {"core"} for f in first_near[1]]
    first_blocks = Blocks(links, first_near, first_far)
    second_ring = links.grow(second_one, bits[1:], first_near[0])
    feed_near = links.quarters(feed_wide, first_near[0], cot_core, cot_hi)

    stack, fars = second_ring
    half = stack.shape[2] // 2
    left_one = links.grow((stack[..., :half], fars), ("lo",))
    right_one = links.grow((stack[..., half:], fars), ("hi",))
    keyval, small_all = project_memory(
        links, tie(memory, stack, first_far[0], feed_near), first_blocks
    )
    feed_one = links.grow((feed_near[None], near), bits[:1], stack, then=(keyval,))
    left_two = links.send(left_one[0], "hi", keyval, feed_one[0])
    right_two = links.send(right_one[0], "lo", keyval, feed_one[0])
    feed_ring = links.grow(feed_one, bits[1:], keyval, then=(left_two, right_two))
    down_one = links.grow((feed_down[None], near), bits[:1], feed_one[0], left_one[0])
    n = len(fars)
    second_near = jnp.concatenate(
        [
            jnp.concatenate([left_one[0], left_two], axis=0),
            jnp.concatenate(
                [right_one[0][:n], right_two[:n], right_one[0][n:], right_two[n:]], axis=0
            ),
        ],
        axis=2,
    )
    down_ring = links.grow(down_one, bits[1:], then=(left_two, right_two))
    second_near = tie(second_near, feed_ring[0], down_ring[0])
    cot_both = links.send(cot_hi, "core", second_near)
    second_fars = left_one[1] + [f | {"hi"} for f in left_one[1]]
    second_far = links.send(second_near, "core"), [f | {"core"} for f in second_fars]
    second_blocks = Blocks(links, (second_near, second_fars), second_far)
    feed_far = links.send(feed_ring[0], "lo", right_two), [f | {"lo"} for f in feed_ring[1]]
    feed_blocks = Blocks(links, feed_ring, feed_far, quads=True)
    down_far = links.send(down_ring[0], "lo", right_two), [f | {"lo"} for f in down_ring[1]]
    cots = (cot, cot_core, cot_hi, cot_both)

    gain_one, gain_two, gain_three = (small_all[i : i + 1] for i in range(3))
    bias_all = small_all[3].reshape(devices, r)[:, :table_part].reshape(HEADS, BUCKETS)
    onehot = jnp.asarray(reversed_buckets())
    table = jnp.dot(bias_all.astype(bf16), onehot.astype(bf16), preferred_element_type=f32)

    x1, n1, qkv1, o1 = causal_forward(
        links, inputs, second_blocks, gain_one, table, lengths, (keyval,)
    )
    n2, q2, o2, x2, n3, probs = cross_forward(
        links, x1, keyval, second_blocks, gain_two, gain_three, ()
    )
    n3_hi = links.send(n3, "hi")
    n3_core = links.send(n3, "core")
    w_down = assemble(links, (down_ring, down_far), (n3,))
    w_gate, w_up, dh = feed_prepare(links, cots, feed_blocks, w_down, (n3,))
    n3_both = links.send(n3_hi, "core", dh)
    n3s = (n3, n3_core, n3_hi, n3_both)
    hidden, dgate, dup, dn3, dn3_hi, dn3_away = feed_through(n3s, w_gate, w_up, dh, ())

    dn3_got = links.send(dn3_away, "core")
    dn3_passed = (dn3_hi + dn3_got[rows:].astype(f32)).astype(bf16)
    dn3_terms = (dn3, dn3_got[:rows], links.send(dn3_passed, "hi"))
    y, y_hi, y_away, gu_keep, gu_away, down_keep, down_away = feed_weight_grads(
        links, n3s, cots, hidden, dgate, dup, w_down, (dn3_passed,)
    )

    def split(a, axes):
        return a.reshape((2,) * len(axes) + (-1, a.shape[-1]))

    dp_axes = bits + ("lo",)
    apart = ("hi",) + dp_axes
    back = tuple(reversed(bits))

    def halves(keep, away, ways, *windows):
        got = split(links.send(away, "core"), apart)
        keep = split(keep, apart)
        return [
            Sum([Leaf(keep, apart, left, width), Leaf(got, apart, left, width)], ways + back)
            for left, width in windows
        ]

    feed_sums = []
    for keep, away, axes in (
        (gu_keep, gu_away, ("hi", "core") + bits),
        (down_keep, down_away, bits),
    ):
        got = links.send(away, "lo").reshape((2,) * len(axes) + away.shape[-2:])
        keep = keep.reshape(got.shape)
        feed_sums.append(Sum([Leaf(keep, axes), Leaf(got, axes)], back))
    done = (y,)
    dx2, do2, keep, away, grad_gain_three = cross_enter(
        links, x2, gain_three, *dn3_terms, cot, o2, second_blocks, done
    )
    early_sums = halves(keep, away, hi_lo, (0, width))
    y_got = links.send(y_away, "core", dx2)
    dq2, grad_keyval = cross_backward(q2, do2, o2, keyval, probs, (dx2,))
    dx1, do1, keep, away, grad_gain_two = causal_enter(
        links, dx2, x1, gain_two, n2, dq2, o1, second_blocks, ()
    )
    done = advance(links, early_sums, (dx1,))
    o1q2_sums = halves(keep, away, hi_lo, (0, 2 * width))
    y_passed = (tie(y_hi, dx1) + y_got[rows:].astype(f32)).astype(bf16)
    y_terms = (y, y_got[:rows], links.send(y_passed, "hi"))
    keep, away, grad_gain_one, grad_bias, input_grad = causal_backward(
        links, lengths, dx1, do1, qkv1, n1, x, gain_one, table, second_blocks, done
    )
    middle_sums = halves(keep, away, hi_lo, (0, 2 * width))
    done = advance(links, feed_sums, (input_grad,))
    done = advance(links, o1q2_sums + early_sums, (*done, y_terms[2]))

    grad_table = lax.dot_general(
        grad_bias, onehot, (((1,), (1,)), ((), ())), precision=lax.Precision.HIGHEST
    )
    table_rows = jnp.pad(
        grad_table.reshape(devices, table_part), ((0, 0), (0, r - table_part))
    ).reshape(1, width)
    small_rows = jnp.concatenate(
        [grad_gain_one, grad_gain_two, grad_gain_three, table_rows, jnp.zeros((4, width), f32)],
        axis=0,
    )
    keep, away = keyval_weight_grad(links, memory, grad_keyval, small_rows, done)
    late_sums = halves(keep, away, lo_hi, (0, KVH * PAIR + EXTRA))
    memory_grad = memory_gradient(links, grad_keyval, first_blocks, 0, None, (keep,))
    done = advance(links, feed_sums + o1q2_sums + middle_sums + late_sums, (memory_grad,))
    early_sums += o1q2_sums
    for b in range(1, seqs):
        memory_grad = memory_gradient(links, grad_keyval, first_blocks, b, memory_grad, done)
    done = (memory_grad,)
    done = advance(links, early_sums + middle_sums + late_sums, done)
    half = width // 2
    while feed_sums[0].ways:
        done = advance(links, feed_sums, done)
    sum_gu, sum_down = finish(links, feed_sums, [(2 * units,), (width,)], done)
    done = (sum_down,)
    while late_sums[0].ways:
        done = advance(links, [one for one in early_sums + middle_sums + late_sums if one.ways], done)
    wide = links.unquarter(sum_gu, done)
    sum_o2, sum_o1, sum_q2, sum_q1, sum_k1, sum_v1, sum_k2, sum_v2, sum_small = finish(
        links,
        early_sums + middle_sums + late_sums,
        [(width,), (width, width), (width, half, half), (half, half, EXTRA)],
        done,
    )

    layer_out = (x2 + sum(tie(t, memory_grad).astype(f32) for t in y_terms)).astype(bf16)
    sum_gate, sum_up = (
        jnp.concatenate([part[:, i * units : (i + 1) * units] for part in wide], axis=1)
        for i in range(2)
    )
    return (
        layer_out.reshape(seqs, length, width),
        input_grad.reshape(seqs, length, width),
        memory_grad,
        sum_q1,
        sum_k1,
        sum_v1,
        sum_o1,
        sum_q2,
        sum_k2,
        sum_v2,
        sum_o2,
        sum_gate,
        sum_up,
        sum_down,
        sum_small[:, 0],
        sum_small[:, 1],
        sum_small[:, 2],
        sum_small[:table_part, 3],
    )


def solution(mesh):
    three = P(AXES, None, None)
    two = P(AXES, None)
    one = P(AXES)
    in_specs = (three, three, one, three) + (two,) * 11 + (one,) * 4
    out_specs = (three,) * 3 + (two,) * 11 + (one,) * 4
    body = functools.partial(local, Links(mesh))
    return jax.shard_map(body, mesh=mesh, in_specs=in_specs, out_specs=out_specs, check_vma=False)
```

```python
import functools

import jax
import jax.numpy as jnp
import numpy as np
from jax import lax
from jax.experimental import pallas as pl
from jax.experimental.pallas import tpu as pltpu
from jax.sharding import PartitionSpec as P

HEADS = 16
HD = 64
BUCKETS = 32
KVH = 8
PAIR = 2 * HD
AXES = ("fsdp", "dp")
norm_eps = 1e-06
masked_score = -1000000000.0
bucket_reach = 128
f32 = jnp.float32
bf16 = jnp.bfloat16
VMEM_LIMIT = 56 * 1024 * 1024
PLAN = 2e9
GROUPS = 4


def reversed_buckets():
    distance = (-np.arange(bucket_reach)) % bucket_reach
    exact_count = BUCKETS // 2
    spread = (
        np.log(np.maximum(distance, 1) / exact_count)
        / np.log(bucket_reach / exact_count)
        * (BUCKETS - exact_count)
    )
    far_bucket = np.minimum(exact_count + np.floor(spread).astype(np.int64), BUCKETS - 1)
    bucket_id = np.where(distance < exact_count, distance, far_bucket)
    return (bucket_id[None] == np.arange(BUCKETS)[:, None]).astype(np.float32)


def dot(a, b, ca=1, cb=0):
    return lax.dot_general(a, b, (((ca,), (cb,)), ((), ())), preferred_element_type=f32)


def call(kernel, ins, in_specs, out_shape, out_specs, name, after=(), grid=(1,), scratch=(), prefetch=None, micros=1, aliases=None):
    lead = 0 if prefetch is None else 1
    n = lead + len(ins)

    def body(*refs):
        kernel(*refs[:n], *refs[n + len(after) :])

    spec = pltpu.PrefetchScalarGridSpec(
        num_scalar_prefetch=lead,
        grid=grid,
        in_specs=list(in_specs) + [pl.BlockSpec(memory_space=pl.ANY)] * len(after),
        out_specs=out_specs,
        scratch_shapes=list(scratch),
    )
    front = () if prefetch is None else (prefetch,)
    return pl.pallas_call(
        body,
        grid_spec=spec,
        out_shape=out_shape,
        input_output_aliases=aliases or {},
        compiler_params=pltpu.CompilerParams(vmem_limit_bytes=VMEM_LIMIT),
        cost_estimate=pl.CostEstimate(
            flops=int(micros * PLAN), bytes_accessed=1000, transcendentals=0
        ),
        name=name,
    )(*front, *ins, *after)


def whole(shape):
    return pl.BlockSpec(shape, lambda *_: (0,) * len(shape))


def struct(shape, dtype):
    return jax.ShapeDtypeStruct(shape, dtype)


def smem():
    return pl.BlockSpec(memory_space=pltpu.SMEM)


class Links:
    def __init__(self, mesh):
        nf, nd = mesh.shape["fsdp"], mesh.shape["dp"]
        self.nf, self.nd, self.size = nf, nd, nd // 2
        self.bits = tuple(f"z{b}" for b in reversed(range(self.size.bit_length() - 1)))
        self.names = ("hi", "core", "ring", "lo") + self.bits
        spots = [(f, d) for f in range(nf) for d in range(nd)]

        def pairs(flip_f, flip_d):
            return [(f * nd + d, (f ^ flip_f) * nd + (d ^ flip_d)) for f, d in spots]

        self.pairs = {"core": pairs(1, 0), "hi": pairs(2, 0), "both": pairs(3, 0), "lo": pairs(0, 1)}
        self.masks = {}
        for name in self.bits:
            self.masks[name] = 1 << int(name[1:])
            self.pairs[name] = pairs(0, 2 << int(name[1:]))

    def locate(self):
        f, d = lax.axis_index("fsdp"), lax.axis_index("dp")
        self.hi, self.core, self.ring, self.lo = f // 2, f % 2, d // 2, d % 2
        zs = [(self.ring // self.masks[name]) % 2 for name in self.bits]
        self.spot = jnp.stack([self.hi, self.core, self.ring, self.lo, *zs]).astype(jnp.int32)

    def send(self, a, way, *after):
        return lax.ppermute(tie(a, *after), AXES, self.pairs[way])

    def grow(self, held, ways, *after, then=()):
        array, fars = held
        for way in ways:
            got = self.send(array, way, *after)
            after = ()
            array = jnp.concatenate([tie(array, *then), got], axis=0)
            fars = fars + [f | {way} for f in fars]
        return array, fars

    def quarters(self, wide, *after):
        mine = self.hi * 2 + self.core
        out = [lax.dynamic_index_in_dim(wide, mine, 0, keepdims=False)]
        for flip, way in ((1, "core"), (2, "hi"), (3, "both")):
            theirs = lax.dynamic_index_in_dim(wide, mine ^ flip, 0, keepdims=False)
            out.append(self.send(theirs, way, *after))
        return jnp.concatenate(out, axis=0)

    def unquarter(self, wide, after):
        _, _, r, c = wide.shape
        wide = wide.reshape(self.nf, r, c)
        mine = self.hi * 2 + self.core
        near = [tie(lax.dynamic_index_in_dim(wide, mine, 0, keepdims=False), *after)]
        for flip, way in ((1, "core"), (2, "hi"), (3, "both")):
            theirs = lax.dynamic_index_in_dim(wide, mine ^ flip, 0, keepdims=False).astype(bf16)
            near.append(tie(self.send(theirs, way), *after).astype(f32))
        near = jnp.stack(near)
        return [lax.dynamic_index_in_dim(near, mine ^ f, 0, keepdims=False) for f in range(self.nf)]


class Blocks:
    def __init__(self, links, *helds, quads=False):
        self.links = links
        self.arrays = [a for a, _ in helds]
        self.fars = [f for _, f in helds]
        self.quads = quads
        _, self.r, self.c = self.arrays[0].shape
        self.count = len(helds)

    def specs(self, width=None, index=0):
        return [
            pl.BlockSpec((*a.shape[:2], width or self.c), lambda *_: (0, 0, index))
            for a in self.arrays
        ]

    def put(self, spot, refs, *outs):
        quads = [(0, 0), (0, 1), (1, 0), (1, 1)] if self.quads else [None]
        r = self.r // len(quads)
        for ref, fars in zip(refs, self.fars):
            for i, far in enumerate(fars):
                for q, quad in enumerate(quads):
                    far_hi, far_core = quad or ("hi" in far, "core" in far)
                    at_hi = 1 - spot[0] if far_hi else spot[0]
                    at_core = 1 - spot[1] if far_core else spot[1]
                    row = ((at_hi * 2 + at_core) * self.links.nd + place_of(self.links, spot, far)) * r
                    rows = pl.ds(pl.multiple_of(row, r), r)
                    left = 0
                    for out in outs:
                        width = out.shape[-1]
                        out[rows, :] = ref[i, q * r : (q + 1) * r, left : left + width]
                        left += width


def place_of(links, spot, far):
    mask = sum(links.masks[name] for name in links.bits if name in far)
    at_ring = jnp.bitwise_xor(spot[2], mask) if mask else spot[2]
    at_lo = 1 - spot[3] if "lo" in far else spot[3]
    return at_ring * 2 + at_lo


def tie(x, *after):
    return lax.optimization_barrier((x, *after))[0] if after else x


def assemble(links, helds, after=()):
    _, r, c = helds[0][0].shape
    n = len(helds)
    most = max(len(f) for _, f in helds)

    def kernel(spot, *refs):
        out, held, sems_in, sems_out = refs[n:]
        copies = []
        for k, (ref, (_, fars)) in enumerate(zip(refs, helds)):
            for i, far in enumerate(fars):
                copies.append(
                    (
                        pltpu.make_async_copy(ref.at[i], held.at[k, i], sems_in.at[k, i]),
                        pltpu.make_async_copy(
                            held.at[k, i], out.at[place_of(links, spot, far)], sems_out.at[k, i]
                        ),
                    )
                )
        for one, _ in copies:
            one.start()
        for one, two in copies:
            one.wait()
            two.start()
        for _, two in copies:
            two.wait()

    out = call(
        kernel,
        [links.spot] + [a for a, _ in helds],
        [smem()] + [pl.BlockSpec(memory_space=pl.ANY)] * n,
        struct((links.nd, r, c), bf16),
        pl.BlockSpec(memory_space=pl.ANY),
        "assemble",
        micros=3,
        after=after,
        scratch=[
            pltpu.VMEM((n, most, r, c), bf16),
            pltpu.SemaphoreType.DMA((n, most)),
            pltpu.SemaphoreType.DMA((n, most)),
        ],
    )
    return out.reshape(-1, c)


class Leaf:
    def __init__(self, array, axes, left=0, width=None, held=()):
        self.array, self.axes, self.left, self.held = array, axes, left, dict(held)
        self.width = width or array.shape[-1]

    def hold(self, way, far):
        held = dict(self.held)
        if way in self.axes:
            held[way] = far
        return Leaf(self.array, self.axes, self.left, self.width, held)

    def free(self):
        return tuple(a for a in self.axes if a not in self.held)

    def spec(self, links):
        shape = tuple(None if a in self.held else 2 for a in self.axes) + self.array.shape[-2:]
        picks = [(self.held.get(a), links.names.index(a)) for a in self.axes]

        def index(_, spot):
            return (
                *(0 if far is None else 1 - spot[i] if far else spot[i] for far, i in picks),
                0,
                0,
            )

        return pl.BlockSpec(shape, index)


class Sum:
    def __init__(self, leaves, ways):
        self.leaves, self.ways = leaves, list(ways)


def gather_terms(links, leaves_of):
    ins = [leaf.array for leaves in leaves_of for leaf in leaves]
    specs = [leaf.spec(links) for leaves in leaves_of for leaf in leaves]

    def totals(refs):
        n = 0
        for leaves in leaves_of:
            total = None
            for leaf in leaves:
                term = refs[n][..., leaf.left : leaf.left + leaf.width].astype(f32)
                total = term if total is None else total + term
                n += 1
            yield total

    return ins, specs, totals


def advance(links, sums, after=()):
    moves = []
    for one in sums:
        way = one.ways.pop(0)
        moves.append((way, [leaf.hold(way, True) for leaf in one.leaves]))
        one.leaves = [leaf.hold(way, False) for leaf in one.leaves]
    groups, where = {}, []
    for way, leaves in moves:
        free = leaves[0].free()
        key = (way, free, leaves[0].array.shape[-2])
        left = groups.get(key, 0)
        groups[key] = left + leaves[0].width
        where.append((key, left, leaves[0].width))
    keys = list(groups)
    outs = [struct((2,) * len(free) + (r, groups[way, free, r]), bf16) for way, free, r in keys]
    ins, specs, totals = gather_terms(links, [leaves for _, leaves in moves])

    def kernel(spot, *refs):
        for total, (key, left, width) in zip(totals(refs), where):
            refs[len(ins) + keys.index(key)][..., left : left + width] = total.astype(bf16)

    sent = call(
        kernel, ins, specs, outs, [whole(o.shape) for o in outs], "combine", micros=3, after=after, prefetch=links.spot
    )
    got = {key: links.send(a, key[0]) for key, a in zip(keys, sent)}
    for one, (key, left, width) in zip(sums, where):
        one.leaves.append(Leaf(got[key], key[1], left, width))
    return (sent[0],)


def finish(links, sums, cuts, after=()):
    ins, specs, totals = gather_terms(links, [one.leaves for one in sums])
    outs = [
        struct((2,) * len(one.leaves[0].free()) + (one.leaves[0].array.shape[-2], width), f32)
        for one, widths in zip(sums, cuts)
        for width in widths
    ]

    def kernel(spot, *refs):
        n = len(ins)
        for total, widths in zip(totals(refs), cuts):
            left = 0
            for width in widths:
                refs[n][...] = total[..., left : left + width]
                left += width
                n += 1

    return call(
        kernel, ins, specs, outs, [whole(o.shape) for o in outs], "finish", micros=3, after=after, prefetch=links.spot
    )


def norm_scale(rows):
    return lax.rsqrt(jnp.mean(rows * rows, axis=-1, keepdims=True) + norm_eps)


def norm_back(grad_normed, rows, gain):
    scale = norm_scale(rows)
    scaled = grad_normed * gain
    inner_mean = jnp.mean(scaled * rows, axis=-1, keepdims=True)
    grad_rows = scale * scaled - rows * (scale * scale * scale) * inner_mean
    return grad_rows, jnp.sum(grad_normed * rows * scale, axis=0, keepdims=True)


def swap_halves(block):
    return pltpu.roll(block.astype(f32), HD, 1).astype(bf16)


def low_lanes(shape):
    return lax.broadcasted_iota(jnp.int32, shape, 1) < HD


def heads_low(block):
    keep = low_lanes(block.shape)
    zero = jnp.zeros_like(block)
    return jnp.concatenate(
        [jnp.where(keep, block, zero), jnp.where(keep, swap_halves(block), zero)], axis=0
    )


def heads_high(block):
    keep = low_lanes(block.shape)
    zero = jnp.zeros_like(block)
    return jnp.concatenate(
        [jnp.where(keep, zero, swap_halves(block)), jnp.where(keep, zero, block)], axis=0
    )


def merge_low(both):
    half = both.shape[0] // 2
    even, odd = both[:half], both[half:]
    return jnp.where(low_lanes(even.shape), even, pltpu.roll(odd, HD, 1))


def merge_high(both):
    half = both.shape[0] // 2
    even, odd = both[:half], both[half:]
    return jnp.where(low_lanes(even.shape), pltpu.roll(even, HD, 1), odd)


def toeplitz(row, length):
    return pltpu.roll(jnp.broadcast_to(row, (length, length)), 0, 1, stride=1, stride_axis=0)


def diagonal_sums(flipped):
    turned = pltpu.roll(flipped, 1, 1, stride=1, stride_axis=0)
    return jnp.sum(turned, axis=0, keepdims=True)


def batches(seqs):
    return [[(b, g) for g in range(k, k + 4) for b in range(seqs)] for k in range(0, KVH, 4)]


def rows_of(b, length):
    return slice(b * length, (b + 1) * length)


def lanes_of(g, left=0):
    return slice(left + g * PAIR, left + (g + 1) * PAIR)


def causal_probs(s, table, g, length, valid_len):
    bias = jnp.concatenate(
        [toeplitz(table[2 * g : 2 * g + 1], length), toeplitz(table[2 * g + 1 : 2 * g + 2], length)],
        axis=0,
    )
    i = lax.broadcasted_iota(jnp.int32, (length, length), 0)
    j = lax.broadcasted_iota(jnp.int32, (length, length), 1)
    valid = (j <= i) & (j < valid_len)
    valid = jnp.concatenate([valid, valid], axis=0)
    s = jnp.where(valid, s + bias, masked_score)
    e = jnp.exp(s - jnp.max(s, axis=-1, keepdims=True))
    return e / jnp.sum(e, axis=-1, keepdims=True)


def split_rows(lhs_t, rhs, core, keep, away):
    half = keep.shape[1]
    for hi in range(keep.shape[0]):
        for out, at in ((keep, core), (away, 1 - core)):
            row = pl.multiple_of((hi * 2 + at) * half, half)
            out[hi] = dot(lhs_t[pl.ds(row, half), :], rhs).astype(bf16)


def project_memory(links, memory, blocks):
    seqs, count, width = memory.shape
    cols = KVH * PAIR
    tile = 1024
    n = blocks.count

    def kernel(spot, mem_ref, *refs):
        held = refs[:n]
        out_ref, small_ref, w_ref, wt_ref = refs[n:]

        @pl.when((pl.program_id(0) == 0) & (pl.program_id(1) == 0))
        def _():
            blocks.put(spot, held, w_ref)
            wt_ref[...] = w_ref[:, :cols].T
            small_ref[...] = w_ref[:, cols:].astype(f32).T[:8]

        out_ref[0] = dot(wt_ref[...], mem_ref[0], 1, 1).astype(bf16)

    return call(
        kernel,
        [links.spot, memory] + blocks.arrays,
        [smem(), pl.BlockSpec((1, tile, width), lambda b, t: (b, t, 0))] + blocks.specs(),
        (struct((seqs, cols, count), bf16), struct((8, width), f32)),
        [pl.BlockSpec((1, cols, tile), lambda b, t: (b, 0, t)), whole((8, width))],
        "project_memory",
        micros=15,
        grid=(seqs, count // tile),
        scratch=[pltpu.VMEM((width, blocks.c), bf16), pltpu.VMEM((cols, width), bf16)],
    )


def causal_forward(links, x, blocks, gain, table, lengths, after):
    seqs, length, width = x.shape
    rows = seqs * length
    cols = 2 * width
    n = blocks.count

    def kernel(spot, len_ref, x_ref, gain_ref, tab_ref, *refs):
        x1_ref, n1_ref, qkv_ref, o1_ref, w_ref, wo_ref = refs[n:]
        blocks.put(spot, refs[:n], w_ref, wo_ref)
        xf = x_ref[...].astype(f32)
        n1 = (xf * norm_scale(xf) * gain_ref[...]).astype(bf16)
        n1_ref[...] = n1
        qkv_ref[...] = dot(n1, w_ref[...]).astype(bf16)
        tab = tab_ref[...]
        for spots in batches(seqs):
            held = [
                (qkv_ref[rows_of(b, length), lanes_of(g)], qkv_ref[rows_of(b, length), lanes_of(g, width)])
                for b, g in spots
            ]
            scores = [dot(heads_low(q), keyval, 1, 1) for q, keyval in held]
            probs = [
                causal_probs(s, tab, g, length, len_ref[b]).astype(bf16)
                for s, (b, g) in zip(scores, spots)
            ]
            for p, (_, keyval), (b, g) in zip(probs, held, spots):
                o1_ref[rows_of(b, length), lanes_of(g)] = merge_high(dot(p, keyval)).astype(bf16)
        x1_ref[...] = xf + dot(o1_ref[...], wo_ref[...])

    return call(
        kernel,
        [links.spot, lengths, x.reshape(rows, width), gain, table] + blocks.arrays,
        [smem(), smem(), whole((rows, width)), whole((1, width)), whole(table.shape)]
        + blocks.specs(cols + width, 0),
        (
            struct((rows, width), f32),
            struct((rows, width), bf16),
            struct((rows, cols), bf16),
            struct((rows, width), bf16),
        ),
        [whole((rows, width)), whole((rows, width)), whole((rows, cols)), whole((rows, width))],
        "causal_forward",
        micros=9,
        after=after,
        scratch=[pltpu.VMEM((width, cols), bf16), pltpu.VMEM((width, width), bf16)],
    )


def cross_forward(links, x1, keyval, blocks, gain_cross, gain_feed, after):
    rows, width = x1.shape
    seqs, _, count = keyval.shape
    length = rows // seqs
    n = blocks.count * 2
    steps = KVH // GROUPS

    def kernel(spot, x1_ref, kv_ref, g2_ref, g3_ref, *refs):
        n2_ref, q2_ref, o2_ref, x2_ref, n3_ref, p_ref, wq_ref, wo_ref = refs[n:]
        b, g = pl.program_id(0), pl.program_id(1)

        @pl.when((b == 0) & (g == 0))
        def _():
            blocks.put(spot, refs[: n // 2], wq_ref)
            blocks.put(spot, refs[n // 2 : n], wo_ref)
            x1v = x1_ref[...]
            n2 = (x1v * norm_scale(x1v) * g2_ref[...]).astype(bf16)
            n2_ref[...] = n2
            q2_ref[...] = dot(n2, wq_ref[...]).astype(bf16)

        part = pl.ds(pl.multiple_of(b * length, length), length)
        lanes = [pl.ds(pl.multiple_of((g * GROUPS + i) * PAIR, PAIR), PAIR) for i in range(GROUPS)]
        scores = [
            dot(heads_low(q2_ref[part, lanes[i]]), kv_ref[0, i * PAIR : (i + 1) * PAIR])
            for i in range(GROUPS)
        ]
        for i, s in enumerate(scores):
            e = jnp.exp(s - jnp.max(s, axis=-1, keepdims=True))
            p_ref[i] = (e * (1.0 / jnp.sum(e, axis=-1, keepdims=True))).astype(bf16)
        for i in range(GROUPS):
            mixed = dot(p_ref[i], kv_ref[0, i * PAIR : (i + 1) * PAIR], 1, 1)
            o2_ref[part, lanes[i]] = merge_high(mixed).astype(bf16)

        @pl.when((b == seqs - 1) & (g == steps - 1))
        def _():
            x2 = x1_ref[...] + dot(o2_ref[...], wo_ref[...])
            x2_ref[...] = x2
            n3_ref[...] = (x2 * norm_scale(x2) * g3_ref[...]).astype(bf16)

    return call(
        kernel,
        [links.spot, x1, keyval, gain_cross, gain_feed] + blocks.arrays * 2,
        [
            smem(),
            whole((rows, width)),
            pl.BlockSpec((1, GROUPS * PAIR, count), lambda b, g: (b, g, 0)),
            whole((1, width)),
            whole((1, width)),
        ]
        + blocks.specs(width, 3)
        + blocks.specs(width, 4),
        (
            struct((rows, width), bf16),
            struct((rows, width), bf16),
            struct((rows, width), bf16),
            struct((rows, width), f32),
            struct((rows, width), bf16),
            struct((seqs * KVH, 2 * length, count), bf16),
        ),
        [whole((rows, width))] * 5
        + [pl.BlockSpec((GROUPS, 2 * length, count), lambda b, g: (b * steps + g, 0, 0))],
        "cross_forward",
        micros=34,
        after=after,
        grid=(seqs, steps),
        scratch=[pltpu.VMEM((width, width), bf16)] * 2,
    )


def stack_rows(refs, out):
    rows = refs[0].shape[0]
    for i, ref in enumerate(refs):
        out[i * rows : (i + 1) * rows] = ref[...]


def feed_prepare(links, cots, blocks, w_down, after):
    rows, width = cots[0].shape
    units = w_down.shape[0]
    n = blocks.count

    def kernel(spot, *refs):
        wd_ref = refs[4]
        wg_ref, wu_ref, dh_ref, cot_all = refs[5 + n :]
        blocks.put(spot, refs[5 : 5 + n], wg_ref, wu_ref)
        stack_rows(refs[:4], cot_all)
        dh_ref[...] = dot(cot_all[...], wd_ref[...], 1, 1)

    return call(
        kernel,
        [links.spot, *cots, w_down] + blocks.arrays,
        [smem()] + [whole((rows, width))] * 4 + [whole(w_down.shape)] + blocks.specs(),
        (
            struct((width, units), bf16),
            struct((width, units), bf16),
            struct((4 * rows, units), f32),
        ),
        [whole((width, units))] * 2 + [whole((4 * rows, units))],
        "feed_prepare",
        micros=6,
        after=after,
        scratch=[pltpu.VMEM((4 * rows, width), bf16)],
    )


def feed_through(n3s, w_gate, w_up, dh, after):
    rows, width = n3s[0].shape
    units = w_gate.shape[1]
    c0 = np.float32(np.sqrt(2.0 / np.pi))
    c1 = np.float32(0.044715)
    cuts = [slice(i, min(i + 256, units)) for i in range(0, units, 256)]

    def kernel(*refs):
        wg_ref, wu_ref, dh_ref = refs[4:7]
        hid_ref, dgate_ref, dup_ref, dn_ref, dn_hi_ref, dn_away_ref, n3_all = refs[7:]
        stack_rows(refs[:4], n3_all)
        for cut in cuts:
            gate = dot(n3_all[...], wg_ref[:, cut])
            up = dot(n3_all[...], wu_ref[:, cut])
            dh = dh_ref[:, cut]
            square = gate * gate
            t = jnp.tanh(c0 * (gate + c1 * (square * gate)))
            cdf = 0.5 * (1.0 + t)
            value = gate * cdf
            slope = cdf + 0.5 * gate * (1.0 - t * t) * (c0 * (1.0 + 3.0 * c1 * square))
            hid_ref[:, cut] = (value * up).astype(bf16)
            dgate_ref[:, cut] = (dh * up * slope).astype(bf16)
            dup_ref[:, cut] = (dh * value).astype(bf16)
        for i in range(0, width, 256):
            at = slice(i, i + 256)
            dn = dot(dgate_ref[...], wg_ref[at, :], 1, 1) + dot(dup_ref[...], wu_ref[at, :], 1, 1)
            dn_ref[:, at] = dn[:rows]
            dn_away_ref[:rows, at] = dn[rows : 2 * rows].astype(bf16)
            dn_hi_ref[:, at] = dn[2 * rows : 3 * rows]
            dn_away_ref[rows:, at] = dn[3 * rows :].astype(bf16)

    return call(
        kernel,
        [*n3s, w_gate, w_up, dh],
        [whole((rows, width))] * 4 + [whole((width, units))] * 2 + [whole((4 * rows, units))],
        (
            struct((4 * rows, units), bf16),
            struct((4 * rows, units), bf16),
            struct((4 * rows, units), bf16),
            struct((rows, width), f32),
            struct((rows, width), f32),
            struct((2 * rows, width), bf16),
        ),
        [whole((4 * rows, units))] * 3 + [whole((rows, width))] * 2 + [whole((2 * rows, width))],
        "feed_through",
        micros=14,
        after=after,
        scratch=[pltpu.VMEM((4 * rows, width), bf16)],
    )


def feed_weight_grads(links, n3s, cots, hidden, dgate, dup, w_down, after):
    rows, width = n3s[0].shape
    units = hidden.shape[1]
    tile = width // links.nf
    r, d = tile // links.nd, units // links.nd

    def kernel(spot, *refs):
        hid_ref, dgate_ref, dup_ref, wd_ref = refs[8:12]
        y_ref, y_hi_ref, y_away_ref = refs[12:15]
        gu_keep, gu_away, gd_keep, gd_away, n3t_ref, cot_all, hid_t, gu_ref, gd_ref = refs[15:]

        @pl.when(pl.program_id(0) == 0)
        def _():
            hid_t[...] = hid_ref[...].T

        for i in range(4):
            n3t_ref[:, i * rows : (i + 1) * rows] = refs[i][...].T
        stack_rows(refs[4:8], cot_all)
        gu_ref[:, :units] = dot(n3t_ref[...], dgate_ref[...])
        gu_ref[:, units:] = dot(n3t_ref[...], dup_ref[...])
        down = dot(hid_t[...], cot_all[...])
        for place in range(links.nd):
            gd_ref[place] = down[place * d : (place + 1) * d]
        for ring in range(links.size):
            for at, gu, gd in ((spot[3], gu_keep, gd_keep), (1 - spot[3], gu_away, gd_away)):
                place = ring * 2 + at
                gu[0, ring] = gu_ref[pl.ds(pl.multiple_of(place * r, 8), r), :].astype(bf16)
                gd[ring] = gd_ref[place].astype(bf16)
        y = dot(hid_ref[...], wd_ref[...])
        y_ref[...] = y[:rows]
        y_away_ref[:rows] = y[rows : 2 * rows].astype(bf16)
        y_hi_ref[...] = y[2 * rows : 3 * rows]
        y_away_ref[rows:] = y[3 * rows :].astype(bf16)

    def columns(count):
        return pl.BlockSpec((count, tile), lambda t: (0, t))

    return call(
        kernel,
        [links.spot, *n3s, *cots, hidden, dgate, dup, w_down],
        [smem()] + [columns(rows)] * 8 + [whole((4 * rows, units))] * 3 + [columns(units)],
        (
            struct((rows, width), f32),
            struct((rows, width), f32),
            struct((2 * rows, width), bf16),
            *[struct((links.nf, links.size, r, 2 * units), bf16)] * 2,
            *[struct((links.size, d, width), bf16)] * 2,
        ),
        [columns(rows)] * 2
        + [columns(2 * rows)]
        + [pl.BlockSpec((1, links.size, r, 2 * units), lambda t: (t, 0, 0, 0))] * 2
        + [pl.BlockSpec((links.size, d, tile), lambda t: (0, 0, t))] * 2,
        "feed_weight_grads",
        micros=12,
        after=after,
        grid=(width // tile,),
        scratch=[
            pltpu.VMEM((tile, 4 * rows), bf16),
            pltpu.VMEM((4 * rows, tile), bf16),
            pltpu.VMEM((units, 4 * rows), bf16),
            pltpu.VMEM((tile, 2 * units), f32),
            pltpu.VMEM((links.nd, d, tile), f32),
        ],
    )


def cross_enter(links, x2, gain_feed, dn3, dn3_core, dn3_hi, cotangent, o2, out_blocks, after):
    rows, width = x2.shape
    n = out_blocks.count
    split = (2, width // 4, width)

    def kernel(spot, x2_ref, g_ref, dn_ref, dn_core_ref, dn_hi_ref, cot_ref, o2_ref, *refs):
        dx_ref, do_ref, keep_ref, away_ref, gg_ref, w_ref, o2t_ref = refs[n:]
        out_blocks.put(spot, refs[:n], w_ref)
        dn = dn_ref[...] + dn_core_ref[...].astype(f32) + dn_hi_ref[...].astype(f32)
        grad_rows, grad_gain = norm_back(dn, x2_ref[...], g_ref[...])
        gg_ref[...] = grad_gain
        dx2 = cot_ref[...].astype(f32) + grad_rows
        dx_ref[...] = dx2
        da = dx2.astype(bf16)
        do_ref[...] = dot(da, w_ref[...], 1, 1).astype(bf16)
        o2t_ref[...] = o2_ref[...].T
        split_rows(o2t_ref, da, spot[1], keep_ref, away_ref)

    return call(
        kernel,
        [links.spot, x2, gain_feed, dn3, dn3_core, dn3_hi, cotangent, o2] + out_blocks.arrays,
        [smem(), whole((rows, width)), whole((1, width))]
        + [whole((rows, width))] * 5
        + out_blocks.specs(width, 4),
        (
            struct((rows, width), f32),
            struct((rows, width), bf16),
            struct(split, bf16),
            struct(split, bf16),
            struct((1, width), f32),
        ),
        [whole((rows, width))] * 2 + [whole(split)] * 2 + [whole((1, width))],
        "cross_enter",
        micros=6,
        after=after,
        scratch=[pltpu.VMEM((width, width), bf16), pltpu.VMEM((width, rows), bf16)],
    )


def cross_backward(q2, do2, o2, keyval, probs, after):
    rows, width = q2.shape
    seqs, cols, count = keyval.shape
    length = rows // seqs
    steps = KVH // GROUPS

    def kernel(q_ref, do_ref, o_ref, kv_ref, p_ref, dq_ref, dkv_ref):
        for i in range(GROUPS):
            lanes = slice(i * PAIR, (i + 1) * PAIR)
            q, do = q_ref[:, lanes], do_ref[:, lanes]
            low, high = heads_low(q), heads_high(do)
            product = do.astype(f32) * o_ref[:, lanes].astype(f32)
            keep = low_lanes(product.shape)
            inner = jnp.concatenate(
                [
                    jnp.sum(jnp.where(keep, product, 0.0), axis=-1, keepdims=True),
                    jnp.sum(jnp.where(keep, 0.0, product), axis=-1, keepdims=True),
                ],
                axis=0,
            )
            kv = kv_ref[0, lanes]
            p = p_ref[i]
            ds = (p.astype(f32) * (dot(high, kv) - inner)).astype(bf16)
            dq_ref[:, lanes] = merge_low(dot(ds, kv, 1, 1)).astype(bf16)
            dkv_ref[0, lanes] = (dot(low.T, ds) + dot(high.T, p)).astype(bf16)

    heads_block = pl.BlockSpec((length, GROUPS * PAIR), lambda b, g: (b, g))
    kv_block = pl.BlockSpec((1, GROUPS * PAIR, count), lambda b, g: (b, g, 0))
    return call(
        kernel,
        [q2, do2, o2, keyval, probs],
        [
            heads_block,
            heads_block,
            heads_block,
            kv_block,
            pl.BlockSpec((GROUPS, 2 * length, count), lambda b, g: (b * steps + g, 0, 0)),
        ],
        (struct((rows, width), bf16), struct((seqs, cols, count), bf16)),
        [heads_block, kv_block],
        "cross_backward",
        micros=25,
        after=after,
        grid=(seqs, steps),
    )


def keyval_weight_grad(links, memory, grad_keyval, small, after):
    seqs, count, width = memory.shape
    cols = grad_keyval.shape[1]
    tile = 1024
    steps = count // tile
    wide = cols + EXTRA
    split = (2, width // 4, wide)

    def kernel(spot, mem_ref, dkv_ref, small_ref, keep_ref, away_ref, acc_ref):
        b, t = pl.program_id(0), pl.program_id(1)

        @pl.when((b == 0) & (t == 0))
        def _():
            acc_ref[...] = jnp.zeros_like(acc_ref)
            acc_ref[cols : cols + 8] = small_ref[...]

        acc_ref[:cols] += dot(dkv_ref[0], mem_ref[0])

        @pl.when((b == seqs - 1) & (t == steps - 1))
        def _():
            half = split[1]
            for hi in range(2):
                for out, at in ((keep_ref, spot[1]), (away_ref, 1 - spot[1])):
                    lanes = pl.ds(pl.multiple_of((hi * 2 + at) * half, half), half)
                    for side in range(2):
                        for g in range(0, KVH, 2):
                            pair = [
                                acc_ref[(g + i) * PAIR + side * HD : (g + i) * PAIR + (side + 1) * HD, lanes]
                                for i in range(2)
                            ]
                            left = side * cols // 2 + g * HD
                            out[hi, :, left : left + PAIR] = jnp.concatenate(pair, axis=0).T.astype(bf16)
                    out[hi, :, cols:] = acc_ref[cols:, lanes].T.astype(bf16)

    return call(
        kernel,
        [links.spot, memory, grad_keyval, small],
        [
            smem(),
            pl.BlockSpec((1, tile, width), lambda b, t: (b, t, 0)),
            pl.BlockSpec((1, cols, tile), lambda b, t: (b, 0, t)),
            whole((8, width)),
        ],
        (struct(split, bf16), struct(split, bf16)),
        [whole(split)] * 2,
        "keyval_weight_grad",
        micros=15,
        after=after,
        grid=(seqs, steps),
        scratch=[pltpu.VMEM((wide, width), f32)],
    )


def memory_gradient(links, grad_keyval, blocks, b, before, after):
    seqs, cols, count = grad_keyval.shape
    width = cols
    tile = 1024
    n = blocks.count
    given = () if before is None else (before,)

    def kernel(spot, dkv_ref, *refs):
        out_ref, w_ref = refs[n + len(given) :]

        @pl.when(pl.program_id(0) == 0)
        def _():
            blocks.put(spot, refs[:n], w_ref)

        out_ref[0] = dot(dkv_ref[0].T, w_ref[...], 1, 1).astype(bf16)

    return call(
        kernel,
        [links.spot, grad_keyval] + blocks.arrays + list(given),
        [smem(), pl.BlockSpec((1, cols, tile), lambda t: (b, 0, t))]
        + blocks.specs(cols, 0)
        + [pl.BlockSpec(memory_space=pl.ANY)] * len(given),
        struct((seqs, count, width), bf16),
        pl.BlockSpec((1, tile, width), lambda t: (b, t, 0)),
        "memory_gradient",
        micros=8,
        after=after,
        grid=(count // tile,),
        scratch=[pltpu.VMEM((width, cols), bf16)],
        aliases={2 + n: 0} if given else {},
    )


def causal_enter(links, dx2, x1, gain_cross, n2, dq2, o1, blocks, after):
    rows, width = x1.shape
    n, m = blocks.count, 2 * blocks.count
    split = (2, width // 4, 2 * width)

    def kernel(spot, dx2_ref, x1_ref, g_ref, n2_ref, dq2_ref, o1_ref, *refs):
        dx_ref, do_ref, keep_ref, away_ref, gg_ref, wo_ref, wq_ref, o1t_ref, n2t_ref = refs[m:]
        blocks.put(spot, refs[:n], wo_ref)
        blocks.put(spot, refs[n:m], wq_ref)
        dq2 = dq2_ref[...]
        grad_rows, grad_gain = norm_back(dot(dq2, wq_ref[...], 1, 1), x1_ref[...], g_ref[...])
        gg_ref[...] = grad_gain
        dx1 = dx2_ref[...] + grad_rows
        dx_ref[...] = dx1
        da = dx1.astype(bf16)
        do_ref[...] = dot(da, wo_ref[...], 1, 1).astype(bf16)
        o1t_ref[...] = o1_ref[...].T
        split_rows(o1t_ref, da, spot[1], keep_ref.at[:, :, :width], away_ref.at[:, :, :width])
        n2t_ref[...] = n2_ref[...].T
        split_rows(n2t_ref, dq2, spot[1], keep_ref.at[:, :, width:], away_ref.at[:, :, width:])

    return call(
        kernel,
        [links.spot, dx2, x1, gain_cross, n2, dq2, o1] + blocks.arrays * 2,
        [smem(), whole((rows, width)), whole((rows, width)), whole((1, width))]
        + [whole((rows, width))] * 3
        + blocks.specs(width, 2)
        + blocks.specs(width, 3),
        (
            struct((rows, width), f32),
            struct((rows, width), bf16),
            struct(split, bf16),
            struct(split, bf16),
            struct((1, width), f32),
        ),
        [whole((rows, width))] * 2 + [whole(split)] * 2 + [whole((1, width))],
        "causal_enter",
        micros=8,
        after=after,
        scratch=[
            pltpu.VMEM((width, width), bf16),
            pltpu.VMEM((width, width), bf16),
            pltpu.VMEM((width, rows), bf16),
            pltpu.VMEM((width, rows), bf16),
        ],
    )


def causal_backward(links, lengths, dx1, do1, qkv1, n1, x, gain_causal, table, blocks, after):
    rows, width = n1.shape
    cols = qkv1.shape[1]
    seqs = lengths.shape[0]
    length = rows // seqs
    n = blocks.count
    split = (2, width // 4, cols)

    def kernel(spot, len_ref, dx1_ref, do_ref, qkv_ref, n1_ref, x_ref, g1_ref, tab_ref, *refs):
        keep_ref, away_ref, gg1_ref, bias_ref, dx_ref, w_ref, dqkv_ref, n1t_ref = refs[n:]
        blocks.put(spot, refs[:n], w_ref)
        tab = tab_ref[...]
        i = lax.broadcasted_iota(jnp.int32, (length, length), 0)
        j = lax.broadcasted_iota(jnp.int32, (length, length), 1)
        flip = jnp.where(i + j == length - 1, 1.0, 0.0).astype(bf16)
        for spots in batches(seqs):
            held = [
                (
                    heads_low(qkv_ref[rows_of(b, length), lanes_of(g)]),
                    heads_high(do_ref[rows_of(b, length), lanes_of(g)]),
                    qkv_ref[rows_of(b, length), lanes_of(g, width)],
                )
                for b, g in spots
            ]
            scores = [dot(low, keyval, 1, 1) for low, _, keyval in held]
            dps = [dot(high, keyval, 1, 1) for _, high, keyval in held]
            probs = [causal_probs(s, tab, g, length, len_ref[b]) for s, (b, g) in zip(scores, spots)]
            dss = [
                (p * (dp - jnp.sum(p * dp, axis=-1, keepdims=True))).astype(bf16)
                for p, dp in zip(probs, dps)
            ]
            for ds, p, (low, high, keyval), (b, g) in zip(dss, probs, held, spots):
                part = rows_of(b, length)
                dqkv_ref[part, lanes_of(g)] = merge_low(dot(ds, keyval)).astype(bf16)
                dqkv_ref[part, lanes_of(g, width)] = (
                    dot(ds.T, low) + dot(p.astype(bf16).T, high)
                ).astype(bf16)
            for i in range(0, len(spots), seqs):
                g = spots[i][1]
                for side in range(2):
                    total = None
                    for ds in dss[i : i + seqs]:
                        term = dot(flip, ds[side * length : (side + 1) * length])
                        total = term if total is None else total + term
                    bias_ref[2 * g + side : 2 * g + side + 1] = diagonal_sums(total)
        dqkv = dqkv_ref[...]
        n1t_ref[...] = n1_ref[...].T
        grad_rows, grad_gain = norm_back(
            dot(dqkv, w_ref[...], 1, 1), x_ref[...].astype(f32), g1_ref[...]
        )
        split_rows(n1t_ref, dqkv[:, :width], spot[1], keep_ref.at[:, :, :width], away_ref.at[:, :, :width])
        keep_low = low_lanes((rows, PAIR))
        apart = [[], []]
        for g in range(0, KVH, 2):
            one, two = (dqkv[:, width + i * PAIR : width + (i + 1) * PAIR] for i in (g, g + 1))
            apart[0].append(jnp.where(keep_low, one, swap_halves(two)))
            apart[1].append(jnp.where(keep_low, swap_halves(one), two))
        dkv = jnp.concatenate(apart[0] + apart[1], axis=1)
        split_rows(n1t_ref, dkv, spot[1], keep_ref.at[:, :, width:], away_ref.at[:, :, width:])
        gg1_ref[...] = grad_gain
        dx_ref[...] = (dx1_ref[...] + grad_rows).astype(bf16)

    return call(
        kernel,
        [links.spot, lengths, dx1, do1, qkv1, n1, x, gain_causal, table] + blocks.arrays,
        [smem(), smem(), whole((rows, width)), whole((rows, width)), whole((rows, cols))]
        + [whole((rows, width))] * 2
        + [whole((1, width)), whole(table.shape)]
        + blocks.specs(cols, 0),
        (
            struct(split, bf16),
            struct(split, bf16),
            struct((1, width), f32),
            struct((HEADS, bucket_reach), f32),
            struct((rows, width), bf16),
        ),
        [whole(split)] * 2 + [whole((1, width)), whole((HEADS, bucket_reach)), whole((rows, width))],
        "causal_backward",
        micros=15,
        after=after,
        scratch=[
            pltpu.VMEM((width, cols), bf16),
            pltpu.VMEM((rows, cols), bf16),
            pltpu.VMEM((width, rows), bf16),
        ],
    )


def interleave(w_key, w_value):
    r = w_key.shape[0]
    return jnp.concatenate(
        [w_key.reshape(r, KVH, HD), w_value.reshape(r, KVH, HD)], axis=2
    ).reshape(r, KVH * PAIR)


EXTRA = 128


def local(
    links,
    inputs,
    memory,
    lengths,
    cotangent,
    causal_query,
    causal_key,
    causal_value,
    causal_out,
    cross_query,
    cross_key,
    cross_value,
    cross_out,
    feed_gate,
    feed_up,
    feed_down,
    gain_causal,
    gain_cross,
    gain_feed,
    bias_table,
):
    links.locate()
    seqs, length, width = inputs.shape
    rows = seqs * length
    r = causal_query.shape[0]
    devices = links.nf * links.nd
    table_part = bias_table.shape[0]
    x = inputs.reshape(rows, width)
    cot = cotangent.reshape(rows, width)

    small = jnp.concatenate(
        [
            gain_causal[:, None],
            gain_cross[:, None],
            gain_feed[:, None],
            jnp.pad(bias_table[:, None], ((0, r - table_part), (0, 0))),
            jnp.zeros((r, EXTRA - 4), bf16),
        ],
        axis=1,
    )
    first_shard = jnp.concatenate([interleave(cross_key, cross_value), small], axis=1)
    causal_shard = jnp.concatenate(
        [causal_query, interleave(causal_key, causal_value), causal_out], axis=1
    )
    second_shard = jnp.concatenate([causal_shard, cross_query, cross_out], axis=1)
    units = feed_gate.shape[1] // links.nf
    feed_wide = jnp.stack(
        [
            jnp.concatenate([w[:, f * units : (f + 1) * units] for w in (feed_gate, feed_up)], axis=1)
            for f in range(links.nf)
        ]
    )

    bits = links.bits
    near = [frozenset()]
    lo_hi, hi_lo = ("lo", "hi"), ("hi", "lo")

    first_ring = links.grow((first_shard[None], near), bits)
    first_lo = links.grow(first_ring, ("lo",))
    second_one = links.grow((second_shard[None], near), bits[:1], first_ring[0])
    first_near = links.grow(first_lo, ("hi",))
    cot_core = links.send(cot, "core", first_lo[0])
    cot_hi = links.send(cot, "hi", first_lo[0])
    first_far = links.send(first_near[0], "core"), [f | {"core"} for f in first_near[1]]
    first_blocks = Blocks(links, first_near, first_far)
    second_ring = links.grow(second_one, bits[1:], first_near[0])
    feed_near = links.quarters(feed_wide, first_near[0], cot_core, cot_hi)

    stack, fars = second_ring
    half = stack.shape[2] // 2
    left_one = links.grow((stack[..., :half], fars), ("lo",))
    right_one = links.grow((stack[..., half:], fars), ("hi",))
    keyval, small_all = project_memory(
        links, tie(memory, stack, first_far[0], feed_near), first_blocks
    )
    feed_one = links.grow((feed_near[None], near), bits[:1], stack, then=(keyval,))
    left_two = links.send(left_one[0], "hi", keyval, feed_one[0])
    right_two = links.send(right_one[0], "lo", keyval, feed_one[0])
    feed_ring = links.grow(feed_one, bits[1:], keyval, then=(left_two, right_two))
    down_one = links.grow((feed_down[None], near), bits[:1], feed_one[0], left_one[0])
    n = len(fars)
    second_near = jnp.concatenate(
        [
            jnp.concatenate([left_one[0], left_two], axis=0),
            jnp.concatenate(
                [right_one[0][:n], right_two[:n], right_one[0][n:], right_two[n:]], axis=0
            ),
        ],
        axis=2,
    )
    down_ring = links.grow(down_one, bits[1:], then=(left_two, right_two))
    second_near = tie(second_near, feed_ring[0], down_ring[0])
    cot_both = links.send(cot_hi, "core", second_near)
    second_fars = left_one[1] + [f | {"hi"} for f in left_one[1]]
    second_far = links.send(second_near, "core"), [f | {"core"} for f in second_fars]
    second_blocks = Blocks(links, (second_near, second_fars), second_far)
    feed_far = links.send(feed_ring[0], "lo", right_two), [f | {"lo"} for f in feed_ring[1]]
    feed_blocks = Blocks(links, feed_ring, feed_far, quads=True)
    down_far = links.send(down_ring[0], "lo", right_two), [f | {"lo"} for f in down_ring[1]]
    cots = (cot, cot_core, cot_hi, cot_both)

    gain_one, gain_two, gain_three = (small_all[i : i + 1] for i in range(3))
    bias_all = small_all[3].reshape(devices, r)[:, :table_part].reshape(HEADS, BUCKETS)
    onehot = jnp.asarray(reversed_buckets())
    table = jnp.dot(bias_all.astype(bf16), onehot.astype(bf16), preferred_element_type=f32)

    x1, n1, qkv1, o1 = causal_forward(
        links, inputs, second_blocks, gain_one, table, lengths, (keyval,)
    )
    n2, q2, o2, x2, n3, probs = cross_forward(
        links, x1, keyval, second_blocks, gain_two, gain_three, ()
    )
    n3_hi = links.send(n3, "hi")
    n3_core = links.send(n3, "core")
    w_down = assemble(links, (down_ring, down_far), (n3,))
    w_gate, w_up, dh = feed_prepare(links, cots, feed_blocks, w_down, (n3,))
    n3_both = links.send(n3_hi, "core", dh)
    n3s = (n3, n3_core, n3_hi, n3_both)
    hidden, dgate, dup, dn3, dn3_hi, dn3_away = feed_through(n3s, w_gate, w_up, dh, ())

    dn3_got = links.send(dn3_away, "core")
    dn3_passed = (dn3_hi + dn3_got[rows:].astype(f32)).astype(bf16)
    dn3_terms = (dn3, dn3_got[:rows], links.send(dn3_passed, "hi"))
    y, y_hi, y_away, gu_keep, gu_away, down_keep, down_away = feed_weight_grads(
        links, n3s, cots, hidden, dgate, dup, w_down, (dn3_passed,)
    )

    def split(a, axes):
        return a.reshape((2,) * len(axes) + (-1, a.shape[-1]))

    dp_axes = bits + ("lo",)
    apart = ("hi",) + dp_axes
    back = tuple(reversed(bits))

    def halves(keep, away, ways, *windows):
        got = split(links.send(away, "core"), apart)
        keep = split(keep, apart)
        return [
            Sum([Leaf(keep, apart, left, width), Leaf(got, apart, left, width)], ways + back)
            for left, width in windows
        ]

    feed_sums = []
    for keep, away, axes in (
        (gu_keep, gu_away, ("hi", "core") + bits),
        (down_keep, down_away, bits),
    ):
        got = links.send(away, "lo").reshape((2,) * len(axes) + away.shape[-2:])
        keep = keep.reshape(got.shape)
        feed_sums.append(Sum([Leaf(keep, axes), Leaf(got, axes)], back))
    done = (y,)
    dx2, do2, keep, away, grad_gain_three = cross_enter(
        links, x2, gain_three, *dn3_terms, cot, o2, second_blocks, done
    )
    early_sums = halves(keep, away, hi_lo, (0, width))
    y_got = links.send(y_away, "core", dx2)
    dq2, grad_keyval = cross_backward(q2, do2, o2, keyval, probs, (dx2,))
    dx1, do1, keep, away, grad_gain_two = causal_enter(
        links, dx2, x1, gain_two, n2, dq2, o1, second_blocks, ()
    )
    done = advance(links, early_sums, (dx1,))
    o1q2_sums = halves(keep, away, hi_lo, (0, 2 * width))
    y_passed = (tie(y_hi, dx1) + y_got[rows:].astype(f32)).astype(bf16)
    y_terms = (y, y_got[:rows], links.send(y_passed, "hi"))
    keep, away, grad_gain_one, grad_bias, input_grad = causal_backward(
        links, lengths, dx1, do1, qkv1, n1, x, gain_one, table, second_blocks, done
    )
    middle_sums = halves(keep, away, hi_lo, (0, 2 * width))
    done = advance(links, feed_sums, (input_grad,))
    done = advance(links, o1q2_sums + early_sums, (*done, y_terms[2]))

    grad_table = lax.dot_general(
        grad_bias, onehot, (((1,), (1,)), ((), ())), precision=lax.Precision.HIGHEST
    )
    table_rows = jnp.pad(
        grad_table.reshape(devices, table_part), ((0, 0), (0, r - table_part))
    ).reshape(1, width)
    small_rows = jnp.concatenate(
        [grad_gain_one, grad_gain_two, grad_gain_three, table_rows, jnp.zeros((4, width), f32)],
        axis=0,
    )
    keep, away = keyval_weight_grad(links, memory, grad_keyval, small_rows, done)
    late_sums = halves(keep, away, lo_hi, (0, KVH * PAIR + EXTRA))
    memory_grad = memory_gradient(links, grad_keyval, first_blocks, 0, None, (keep,))
    o2_got = early_sums[0].leaves[-1].array
    done = advance(links, feed_sums + o1q2_sums + middle_sums + late_sums, (memory_grad, o2_got))
    early_sums += o1q2_sums
    for b in range(1, seqs):
        memory_grad = memory_gradient(links, grad_keyval, first_blocks, b, memory_grad, done)
    done = (memory_grad,)
    done = advance(links, early_sums + middle_sums + late_sums, done)
    half = width // 2
    while feed_sums[0].ways:
        done = advance(links, feed_sums, done)
    sum_gu, sum_down = finish(links, feed_sums, [(2 * units,), (width,)], done)
    done = (sum_down,)
    while late_sums[0].ways:
        done = advance(links, [one for one in early_sums + middle_sums + late_sums if one.ways], done)
    wide = links.unquarter(sum_gu, done)
    sum_o2, sum_o1, sum_q2, sum_q1, sum_k1, sum_v1, sum_k2, sum_v2, sum_small = finish(
        links,
        early_sums + middle_sums + late_sums,
        [(width,), (width, width), (width, half, half), (half, half, EXTRA)],
        done,
    )

    layer_out = (x2 + sum(tie(t, memory_grad).astype(f32) for t in y_terms)).astype(bf16)
    sum_gate, sum_up = (
        jnp.concatenate([part[:, i * units : (i + 1) * units] for part in wide], axis=1)
        for i in range(2)
    )
    return (
        layer_out.reshape(seqs, length, width),
        input_grad.reshape(seqs, length, width),
        memory_grad,
        sum_q1,
        sum_k1,
        sum_v1,
        sum_o1,
        sum_q2,
        sum_k2,
        sum_v2,
        sum_o2,
        sum_gate,
        sum_up,
        sum_down,
        sum_small[:, 0],
        sum_small[:, 1],
        sum_small[:, 2],
        sum_small[:table_part, 3],
    )


def solution(mesh):
    three = P(AXES, None, None)
    two = P(AXES, None)
    one = P(AXES)
    in_specs = (three, three, one, three) + (two,) * 11 + (one,) * 4
    out_specs = (three,) * 3 + (two,) * 11 + (one,) * 4
    body = functools.partial(local, Links(mesh))
    return jax.shard_map(body, mesh=mesh, in_specs=in_specs, out_specs=out_specs, check_vma=False)
```
